128 devices in a mesh: dp: 64 (over z_hi, x, y, core), expert: 2 (over z_lo).
Axes of the slice: x: 4, y: 4, z: 4 (z_hi: 2, z_lo: 2; z = z_hi * 2 + z_lo), core: 2. Of those that a mesh axis runs over, the one named last changes fastest.
Arguments:
- hidden_in: bfloat16 [32768, 1536], P(('dp', 'expert')), may hold values from -6 to 6
- out_grad: bfloat16 [32768, 1536], P(('dp', 'expert')), may hold values from -6 to 6
- doc_lengths: int32 [128, 4], P(('dp', 'expert')), may hold values from 1 to 192, 256 in all within a row
- expert_ids: int32 [32768, 6], P(('dp', 'expert')), may hold values from 0 to 63, all different within a row; in each aligned block of 256 rows (0 to 255, 256 to 511, ...) at most 32 rows name the same one
- gain_attn: bfloat16 [1536], P(('dp', 'expert')), may hold values from 0.5 to 1.5
- w_query: bfloat16 [1536, 1536], P(('dp', 'expert')), may hold values from -0.15625 to 0.15625
- key_weight_shard: bfloat16 [1536, 512], P(('dp', 'expert')), may hold values from -0.15625 to 0.15625
- value_weight_shard: bfloat16 [1536, 512], P(('dp', 'expert')), may hold values from -0.15625 to 0.15625
- w_out: bfloat16 [1536, 1536], P(('dp', 'expert')), may hold values from -0.875 to 0.875
- gain_ffn: bfloat16 [1536], P(('dp', 'expert')), may hold values from 0.5 to 1.5
- w_router: bfloat16 [1536, 64], P(('dp', 'expert')), may hold values from -0.078125 to 0.078125
- w_shared_gate: bfloat16 [1536, 1024], P(('dp', 'expert')), may hold values from -0.15625 to 0.15625
- w_shared_up: bfloat16 [1536, 1024], P(('dp', 'expert')), may hold values from -0.15625 to 0.15625
- w_shared_down: bfloat16 [1024, 1536], P(('dp', 'expert')), may hold values from -0.1875 to 0.1875
- expert_gate: bfloat16 [64, 1536, 512], P('dp', None, 'expert'), may hold values from -0.15625 to 0.15625
- expert_up: bfloat16 [64, 1536, 512], P('dp', None, 'expert'), may hold values from -0.15625 to 0.15625
- expert_down: bfloat16 [64, 512, 1536], P('dp', 'expert'), may hold values from -0.75 to 0.75
Outputs:
- block_out: bfloat16 [32768, 1536], P(('dp', 'expert'))
- grad_in: float32 [32768, 1536], P(('dp', 'expert'))
- grad_gain_attn: float32 [1536], P(('dp', 'expert'))
- grad_w_query: float32 [1536, 1536], P(('dp', 'expert'))
- grad_w_key: float32 [1536, 512], P(('dp', 'expert'))
- grad_w_value: float32 [1536, 512], P(('dp', 'expert'))
- grad_w_out: float32 [1536, 1536], P(('dp', 'expert'))
- grad_gain_ffn: float32 [1536], P(('dp', 'expert'))
- grad_w_router: float32 [1536, 64], P(('dp', 'expert'))
- grad_w_shared_gate: float32 [1536, 1024], P(('dp', 'expert'))
- grad_w_shared_up: float32 [1536, 1024], P(('dp', 'expert'))
- grad_w_shared_down: float32 [1024, 1536], P(('dp', 'expert'))
- grad_expert_gate: float32 [64, 1536, 512], P('dp', None, 'expert')
- grad_expert_up: float32 [64, 1536, 512], P('dp', None, 'expert')
- grad_expert_down: float32 [64, 512, 1536], P('dp', 'expert')
The draws below stay inside these ranges and needn't reach their ends.
Inputs may be any that keep to these rules, and one draw needn't show every extreme that they name: `doc_lengths`: each row holds the lengths of the 4 documents of one device's 256 tokens; they sum to 256 and the longest is 192. `expert_ids`: each row names 6 different experts. Among the rows of one device no expert is named more than 32 times, and on some device one expert is named exactly 32 times.
All inputs are finite; a program needn't handle non-finite values.
Results may differ from the reference program's by a relative error of at most 0.02.
Values may be sent and summed in bfloat16 or wider, within the bound.
No kernel may reach another device: no remote copies, remote signals or barrier semaphores. Data moves between devices by JAX's collectives and lax.ppermute only.
A program may use at most 320 MiB of HBM per device.

```python
import math
import jax
import jax.numpy as jnp
import numpy as np
from jax import lax

MODEL_WIDTH = 1536
QUERY_HEADS = 12
KEY_VALUE_HEADS = 4
HEAD_WIDTH = 128
SH = 1024
EH = 512
TOPK = 6
DEVICE_TOKENS = 256
DOCS = 4
EXPERTS = 64
C = 32
LONGEST = 192
TOKENS = 32768
N_DP = 64
N_EXPERT = 2


def steps_of(own_key, shape, cuts, least, largest):
    level, own = 1.0, jax.random.fold_in(own_key, 6)
    for dim, blocks in cuts:
        steps = jnp.exp(jax.random.uniform(jax.random.fold_in(own, dim), (blocks,), jnp.float32, least / len(cuts), largest / len(cuts)))
        level = level * jnp.repeat(steps, shape[dim] // blocks).reshape([-1 if axis == dim else 1 for axis in range(len(shape))])
    return level


def length_profile(amount, total, most, slope):
    weights = [(1 << 20) // math.isqrt(grade ** slope) + 1 for grade in range(2, amount + 1)]
    spare, counts = total - most - (amount - 1), [1] * (amount - 1)
    while spare > 0:
        free = [i for i in range(amount - 1) if counts[i] < most]
        pool, left = sum([weights[i] for i in free]), spare
        for i in free:
            extra = min(most - counts[i], max(1, left * weights[i] // pool), spare)
            counts[i] = counts[i] + extra
            spare = spare - extra
    return np.array([most] + counts)


def uneven_parts(own_key, amount, total, most, skew):
    if amount == 2:
        one = jax.random.randint(own_key, (), max(1, total - most), min(most, total - 1) + 1)
        return jnp.stack([one, total - one])
    lengths = jnp.asarray(length_profile(amount, total, most, skew), jnp.int32)
    couples = (amount - 1) // 2
    donor, taker = lengths[1:1 + 2 * couples:2], lengths[2:2 + 2 * couples:2]
    margin = jnp.minimum(donor - 1, most - taker)
    shifted = jax.random.randint(jax.random.fold_in(own_key, 1), (couples,), 0, 1 << 20) % (margin + 1)
    lengths = lengths.at[1:1 + 2 * couples:2].set(donor - shifted).at[2:2 + 2 * couples:2].set(taker + shifted)
    return lengths[jax.random.permutation(jax.random.fold_in(own_key, 2), amount)]


def deal_out(rng, own, number, rows, amount, top, most, slope):
    ranking = jax.random.permutation(rng, amount)
    heavy_load, ordinary = shares(amount, rows * top, most, slope, True), shares(amount, rows * top, most, slope, False)
    places = jnp.arange(amount)

    def named(sizes, offset_by):
        used = int((sizes > 0).sum())
        fixed = max(1, used // 4)
        shifted = fixed + (places - fixed + offset_by * (used - fixed)) % max(1, amount - fixed)
        return jnp.zeros((amount,), jnp.int32).at[ranking[jnp.where(places < fixed, places, shifted)]].set(jnp.asarray(sizes, jnp.int32))

    sizes = jnp.where(number % 4 == 0, named(heavy_load, number // 4), named(ordinary, number - number // 4 - 1))
    mixed = jax.random.permutation(jax.random.fold_in(own, 3), amount)
    source_of, taker = mixed[0:amount // 2 * 2:2], mixed[1:amount // 2 * 2:2]
    slack = jnp.minimum(sizes[source_of] - 1, most - sizes[taker]) // 2
    slack = jnp.where((source_of == ranking[0]) | (taker == ranking[0]) | (sizes[taker] == 0), 0, jnp.maximum(slack, 0))
    shifted = jax.random.randint(jax.random.fold_in(own, 4), (amount // 2,), 0, 1 << 20) % (slack + 1)
    sizes = sizes.at[source_of].add(-shifted).at[taker].add(shifted)
    labels = jnp.searchsorted(jnp.cumsum(sizes), jnp.arange(rows * top), side="right").astype(jnp.int32)
    listing = labels.reshape(top, rows).T
    listing = listing[jax.random.permutation(jax.random.fold_in(own, 1), rows)]
    offset_by = jax.random.randint(jax.random.fold_in(own, 2), (rows, 1), 0, top)
    return jnp.take_along_axis(listing, (jnp.arange(top)[None, :] + offset_by) % top, axis=1)


def shares(number_of, total, limit, skew, full):
    portions = [(1 << 20) // math.isqrt(grade ** skew) + 1 for grade in range(1, number_of + 1)]
    largest = limit if full else min(limit, max(-(-total // number_of), total * portions[0] // sum(portions)))
    least = 1 if total - largest >= number_of - 1 else 0
    given, surplus = [largest] + [least] * (number_of - 1), total - largest - least * (number_of - 1)
    while surplus > 0:
        movable = [i for i in range(1, number_of) if given[i] < largest] or [i for i in range(1, number_of) if given[i] < limit]
        whole, remaining = sum([portions[i] for i in movable]), surplus
        for i in movable:
            addition = min(limit - given[i], max(1, remaining * portions[i] // whole), surplus)
            given[i] = given[i] + addition
            surplus = surplus - addition
    return np.array(given)


def centred(rng, dims, deviation, limit, shards=(), held_as=jnp.bfloat16):
    gain = steps_of(rng, dims, shards, -0.22, 0.18) if shards else 1.0
    values = jax.random.normal(rng, dims, jnp.float32) * deviation * gain
    return jnp.minimum(jnp.maximum(values, -limit), limit).astype(held_as)


def setup_inputs(seed: int = 0) -> dict:
    seeds = jax.random.split(jax.random.key(seed), 18)
    hidden_in = centred(seeds[0], (TOKENS, MODEL_WIDTH), 1.0, 6.0, ((0, 128),))
    out_grad = centred(seeds[1], (TOKENS, MODEL_WIDTH), 1.0, 6.0, ((0, 128),))
    doc_lengths = jax.vmap(lambda own: uneven_parts(own, DOCS, DEVICE_TOKENS, LONGEST, 2))(jax.random.split(seeds[2], (N_DP * N_EXPERT))).reshape((N_DP * N_EXPERT, DOCS)).astype(jnp.int32)
    expert_ids_keys = jax.random.split(jax.random.fold_in(seeds[3], 1), TOKENS // DEVICE_TOKENS)
    expert_ids_turns = jax.random.permutation(jax.random.fold_in(seeds[3], 3), TOKENS // DEVICE_TOKENS)
    expert_ids = jax.vmap(lambda own, number: deal_out(jax.random.fold_in(seeds[3], 2), own, number, DEVICE_TOKENS, EXPERTS, TOPK, C, 2))(expert_ids_keys, expert_ids_turns).reshape((TOKENS, TOPK))
    gain_attn = jnp.clip(1.0 + 0.1 * jax.random.normal(seeds[4], (MODEL_WIDTH,), jnp.float32), 0.5, 1.5).astype(jnp.bfloat16)
    w_query = centred(seeds[5], (MODEL_WIDTH, QUERY_HEADS * HEAD_WIDTH), MODEL_WIDTH ** -0.5, 0.15625, ((0, 128),))
    key_weight_shard = centred(seeds[6], (MODEL_WIDTH, KEY_VALUE_HEADS * HEAD_WIDTH), MODEL_WIDTH ** -0.5, 0.15625, ((0, 128),))
    value_weight_shard = centred(seeds[7], (MODEL_WIDTH, KEY_VALUE_HEADS * HEAD_WIDTH), MODEL_WIDTH ** -0.5, 0.15625, ((0, 128),))
    w_out = centred(seeds[8], (QUERY_HEADS * HEAD_WIDTH, MODEL_WIDTH), (QUERY_HEADS * HEAD_WIDTH // 32) ** -0.5, 0.875, ((0, 128),))
    gain_ffn = jnp.clip(1.0 + 0.1 * jax.random.normal(seeds[9], (MODEL_WIDTH,), jnp.float32), 0.5, 1.5).astype(jnp.bfloat16)
    w_router = centred(seeds[10], (MODEL_WIDTH, EXPERTS), (4 * MODEL_WIDTH) ** -0.5, 0.078125, ((0, 128),))
    w_shared_gate = centred(seeds[11], (MODEL_WIDTH, SH), MODEL_WIDTH ** -0.5, 0.15625, ((0, 128),))
    w_shared_up = centred(seeds[12], (MODEL_WIDTH, SH), MODEL_WIDTH ** -0.5, 0.15625, ((0, 128),))
    w_shared_down = centred(seeds[13], (SH, MODEL_WIDTH), SH ** -0.5, 0.1875, ((0, 128),))
    expert_gate = centred(seeds[14], (EXPERTS, MODEL_WIDTH, EH), MODEL_WIDTH ** -0.5, 0.15625, ((0, 64), (2, 2)))
    expert_up = centred(seeds[15], (EXPERTS, MODEL_WIDTH, EH), MODEL_WIDTH ** -0.5, 0.15625, ((0, 64), (2, 2)))
    expert_down = centred(seeds[16], (EXPERTS, EH, MODEL_WIDTH), (EH // 8) ** -0.5, 0.75, ((0, 64), (1, 2)))
    return {"hidden_in": hidden_in, "out_grad": out_grad, "doc_lengths": doc_lengths, "expert_ids": expert_ids, "gain_attn": gain_attn, "w_query": w_query, "key_weight_shard": key_weight_shard, "value_weight_shard": value_weight_shard, "w_out": w_out, "gain_ffn": gain_ffn, "w_router": w_router, "w_shared_gate": w_shared_gate, "w_shared_up": w_shared_up, "w_shared_down": w_shared_down, "expert_gate": expert_gate, "expert_up": expert_up, "expert_down": expert_down}


@jax.custom_vjp
def low(v):
    return lax.optimization_barrier(v.astype(jnp.bfloat16)).astype(jnp.float32)

@jax.custom_vjp
def low_back(v):
    return v

def low_keep(v):
    return (low(v), None)

def low_pass(kept, grad):
    return (grad,)

def back_keep(v):
    return (v, None)

def back_low(kept, grad):
    return (low(grad),)
low.defvjp(low_keep, low_pass)
low_back.defvjp(back_keep, back_low)
EPSILON = 1e-06
NEGATIVE = -1e+30

def product(first, second):
    return jnp.dot(first, second, precision=lax.Precision.HIGHEST)

def root_norm(values, gain_vector):
    root_scale = lax.rsqrt(lax.optimization_barrier(jnp.mean(values * values, axis=-1, keepdims=True)) + EPSILON)
    return values * root_scale * gain_vector

def attention_block_step(projected_queries, projected_keys, projected_values, document_segment):
    token_row_count = projected_queries.shape[0]
    projected_queries = projected_queries.reshape(token_row_count, KEY_VALUE_HEADS, QUERY_HEADS // KEY_VALUE_HEADS, HEAD_WIDTH)
    projected_keys = projected_keys.reshape(token_row_count, KEY_VALUE_HEADS, HEAD_WIDTH)
    projected_values = projected_values.reshape(token_row_count, KEY_VALUE_HEADS, HEAD_WIDTH)
    scores = jnp.einsum('qhgd,khd->hgqk', projected_queries, projected_keys, precision=lax.Precision.HIGHEST) * HEAD_WIDTH ** (-0.5)
    scores = low_back(scores)
    position = jnp.arange(token_row_count, dtype=jnp.int32)
    visible = (document_segment[:, None] == document_segment[None, :]) & (position[:, None] >= position[None, :])
    scores = jnp.where(visible, scores, NEGATIVE)
    probabilities = low(jax.nn.softmax(scores, axis=-1))
    attention_result = jnp.einsum('hgqk,khd->qhgd', probabilities, projected_values, precision=lax.Precision.HIGHEST)
    return attention_result.reshape(token_row_count, QUERY_HEADS * HEAD_WIDTH)

def reference(hidden_in, out_grad, doc_lengths, expert_ids, gain_attn, w_query, key_weight_shard, value_weight_shard, w_out, gain_ffn, w_router, w_shared_gate, w_shared_up, w_shared_down, expert_gate, expert_up, expert_down):
    device_list = N_DP * N_EXPERT
    doc_ends = jnp.cumsum(doc_lengths, axis=1).astype(jnp.int32)
    position = jnp.arange(DEVICE_TOKENS, dtype=jnp.int32)
    document_segment = lax.optimization_barrier(jnp.sum((position[None, :, None] >= doc_ends[:, None, :]).astype(jnp.int32), axis=2))
    expert_range = jnp.arange(EXPERTS, dtype=jnp.int32)
    flat_ids = expert_ids.reshape(device_list, DEVICE_TOKENS * TOPK)
    route_match = (flat_ids[:, :, None] == expert_range).astype(jnp.int32)
    route_rank = lax.optimization_barrier(jnp.sum(route_match * (jnp.cumsum(route_match, axis=1) - 1), axis=2)).astype(jnp.int32)
    device_of = jnp.arange(device_list, dtype=jnp.int32)[:, None]
    route_slot = (flat_ids * (device_list * C) + device_of * C + route_rank).reshape(-1).astype(jnp.int32)
    route_token = (device_of * DEVICE_TOKENS + jnp.arange(DEVICE_TOKENS * TOPK, dtype=jnp.int32)[None, :] // TOPK).reshape(-1).astype(jnp.int32)
    slot_token = jnp.full((EXPERTS * device_list * C,), TOKENS, jnp.int32).at[route_slot].set(route_token)
    slot_alive = (slot_token < TOKENS).reshape(EXPERTS, device_list * C)
    slot_token = jnp.minimum(slot_token, TOKENS - 1).reshape(EXPERTS, device_list * C).astype(jnp.int32)
    route_hits = expert_ids[:, :, None] == expert_range

    def forward(tokens, gain_one, query_weight_full, key_weight_full, value_weight_full, out_w, gain_two, router_w, shared_gate_w, shared_up_w, shared_down_w, gate_bank, upper_bank, down_bank):
        normed_attn = low(root_norm(tokens, gain_one))
        projected_queries = low(low_back(product(normed_attn, query_weight_full)))
        projected_keys = low(low_back(product(normed_attn, key_weight_full)))
        projected_values = low(low_back(product(normed_attn, value_weight_full)))
        attention_result = lax.map(jax.checkpoint(lambda entry_element: attention_block_step(*entry_element)), (projected_queries.reshape(device_list, DEVICE_TOKENS, QUERY_HEADS * HEAD_WIDTH), projected_keys.reshape(device_list, DEVICE_TOKENS, KEY_VALUE_HEADS * HEAD_WIDTH), projected_values.reshape(device_list, DEVICE_TOKENS, KEY_VALUE_HEADS * HEAD_WIDTH), document_segment))
        attention_result = low(low_back(attention_result.reshape(TOKENS, QUERY_HEADS * HEAD_WIDTH)))
        middle = tokens + low_back(product(attention_result, out_w))
        normed_ffn = low(root_norm(middle, gain_two))
        logits = low_back(product(normed_ffn, router_w))
        chosen = lax.optimization_barrier(jnp.sum(jnp.where(route_hits, logits[:, None, :], 0.0), axis=2))
        gates = jax.nn.softmax(chosen, axis=-1)
        shared_gate = low_back(product(normed_ffn, shared_gate_w))
        shared_upper = low_back(product(normed_ffn, shared_up_w))
        shared_act = low(jax.nn.silu(shared_gate) * shared_upper)
        shared_out = product(shared_act, shared_down_w)

        def one_expert(entry_element):
            tokens_of, alive, gate_w, upper_w, down_w = entry_element
            slot_rows = low_back(jnp.where(alive[:, None], normed_ffn[tokens_of], 0.0))
            gate_value = low_back(product(slot_rows, gate_w))
            upper_value = low_back(product(slot_rows, upper_w))
            activation = low(jax.nn.silu(gate_value) * upper_value)
            return low(low_back(product(activation, down_w)))
        results = lax.map(jax.checkpoint(one_expert), (slot_token, slot_alive, gate_bank, upper_bank, down_bank))
        picked = results.reshape(EXPERTS * device_list * C, MODEL_WIDTH)[route_slot].reshape(TOKENS, TOPK, MODEL_WIDTH)
        return middle + shared_out + lax.optimization_barrier(jnp.sum(gates[:, :, None] * picked, axis=1))
    primals = (hidden_in.astype(jnp.float32), gain_attn.astype(jnp.float32), w_query.astype(jnp.float32), key_weight_shard.astype(jnp.float32), value_weight_shard.astype(jnp.float32), w_out.astype(jnp.float32), gain_ffn.astype(jnp.float32), w_router.astype(jnp.float32), w_shared_gate.astype(jnp.float32), w_shared_up.astype(jnp.float32), w_shared_down.astype(jnp.float32), expert_gate.astype(jnp.float32), expert_up.astype(jnp.float32), expert_down.astype(jnp.float32))
    block_sum, pullback = jax.vjp(forward, *primals)
    grads = pullback(out_grad.astype(jnp.float32))
    return (block_sum.astype(jnp.bfloat16), grads[0], grads[1], grads[2], grads[3], grads[4], grads[5], grads[6], grads[7], grads[8], grads[9], grads[10], grads[11], grads[12], grads[13])
```

```python
import jax
import jax.numpy as jnp
from jax import lax
from jax.sharding import Mesh, PartitionSpec as P

QUERY_HEADS = 12
KEY_VALUE_HEADS = 4
GROUP = 3
HEAD = 128
EXPERTS = 64
SLOTS = 32
TOKENS = 256
WIDTH = 1536
EXTRA = 128

EPSILON = 1e-06
NEGATIVE = -1e30
BF = jnp.bfloat16
F32 = jnp.float32

AXES = ("zh", "x", "y", "c", "zl")
DP = ("zh", "x", "y", "c")
PLANE = ("x", "y", "c")


def mm(a, b):
    return jnp.dot(a, b, preferred_element_type=F32)


def mm_l(a, b):
    return lax.dot_general(a, b, (((0,), (0,)), ((), ())), preferred_element_type=F32)


def mm_r(a, b):
    return lax.dot_general(a, b, (((1,), (1,)), ((), ())), preferred_element_type=F32)


def swap(x, axis):
    return lax.ppermute(x, axis, [(0, 1), (1, 0)])


def gather_rows(shard):
    rows, width = shard.shape
    four = lax.all_gather(shard, ("zh", "zl"), axis=0, tiled=False)
    pairs = four.reshape(2, 2 * rows, width)
    whole = lax.all_gather(pairs, PLANE, axis=1, tiled=True)
    return whole.reshape(128 * rows, width)


def scatter_rows(grads):
    rows, width = grads.shape
    r = rows // 128
    plane = lax.psum_scatter(
        grads.reshape(2, rows // 2, width), PLANE, scatter_dimension=1, tiled=True
    )
    zh = lax.axis_index("zh")
    zl = lax.axis_index("zl")
    keep = jnp.where(zh == 0, plane[0], plane[1])
    give = jnp.where(zh == 0, plane[1], plane[0])
    pair = keep.astype(F32) + swap(give, "zh").astype(F32)
    keep = jnp.where(zl == 0, pair[:r], pair[r:])
    give = jnp.where(zl == 0, pair[r:], pair[:r]).astype(BF)
    return keep + swap(give, "zl").astype(F32)


def to_experts(rows):
    return lax.all_to_all(
        rows.reshape(EXPERTS, SLOTS, -1), DP, split_axis=0, concat_axis=0, tiled=True
    ).reshape(EXPERTS * SLOTS, -1)


def norm(values, gain):
    scale = lax.rsqrt(jnp.mean(values * values, axis=-1, keepdims=True) + EPSILON)
    return values * scale * gain, scale


def norm_back(values, scale, gain, cot):
    grad_gain = jnp.sum(cot * values * scale, axis=0)
    weighted = cot * gain
    centre = jnp.mean(weighted * values, axis=-1, keepdims=True)
    return scale * weighted - values * (scale * scale * scale) * centre, grad_gain


def body(
    hidden_in,
    out_grad,
    doc_lengths,
    expert_ids,
    gain_attn,
    w_query,
    w_key,
    w_value,
    w_out,
    gain_ffn,
    w_router,
    w_shared_gate,
    w_shared_up,
    w_shared_down,
    expert_gate,
    expert_up,
    expert_down,
):
    small = jnp.concatenate(
        [w_router, gain_attn[:, None], gain_ffn[:, None], jnp.zeros((12, 62), BF)], axis=1
    )
    first = gather_rows(jnp.concatenate([w_query, w_key, w_value, w_out, small], axis=1))
    second = gather_rows(jnp.concatenate([w_shared_gate, w_shared_up], axis=1))
    down_full = gather_rows(w_shared_down)
    w_qkv = first[:, :2560]
    w_out_full = first[:, 2560:4096]
    router_full = first[:, 4096:4160]
    gain_one = first[:, 4160].astype(F32)
    gain_two = first[:, 4161].astype(F32)

    own_gate, own_up, own_down = expert_gate[0], expert_up[0], expert_down[0]
    wg = jnp.concatenate([own_gate, swap(own_gate, "zl")], axis=1)
    wu = jnp.concatenate([own_up, swap(own_up, "zl")], axis=1)
    wd = jnp.concatenate([own_down, swap(own_down, "zl")], axis=0)

    expert_range = jnp.arange(EXPERTS, dtype=jnp.int32)
    hits = jnp.any(expert_ids[:, :, None] == expert_range, axis=1)
    hits_low = hits.astype(BF)
    place = jnp.arange(TOKENS, dtype=jnp.int32)
    earlier = (place[:, None] > place[None, :]).astype(BF)
    rank = jnp.where(hits, mm(earlier, hits_low), -1.0)
    slot_range = jnp.arange(SLOTS, dtype=F32)
    deal = (rank.T[:, None, :] == slot_range[None, :, None]).astype(BF)
    deal = deal.reshape(EXPERTS * SLOTS, TOKENS)

    marked = jnp.concatenate([out_grad, hits_low, jnp.zeros((TOKENS, 64), BF)], axis=1)
    cot_rows = to_experts(mm(deal, marked).astype(BF))

    tokens = hidden_in.astype(F32)
    normed_attn, scale_one = norm(tokens, gain_one)
    attn_in = normed_attn.astype(BF)
    qkv = mm(attn_in, w_qkv).astype(BF)
    queries = qkv[:, :1536].reshape(TOKENS, KEY_VALUE_HEADS, GROUP, HEAD)
    keys = qkv[:, 1536:2048].reshape(TOKENS, KEY_VALUE_HEADS, HEAD)
    values = qkv[:, 2048:].reshape(TOKENS, KEY_VALUE_HEADS, HEAD)
    doc_ends = jnp.cumsum(doc_lengths[0])
    segment = jnp.sum((place[:, None] >= doc_ends[None, :]).astype(jnp.int32), axis=1)
    visible = (segment[:, None] == segment[None, :]) & (place[:, None] >= place[None, :])
    scaling = HEAD ** (-0.5)
    scores = (
        jnp.einsum("qhgd,khd->hgqk", queries, keys, preferred_element_type=F32) * scaling
    )
    scores = jnp.where(visible, scores, NEGATIVE)
    exponent = jnp.exp(scores - jnp.max(scores, axis=-1, keepdims=True))
    probs = exponent / jnp.sum(exponent, axis=-1, keepdims=True)
    probs_low = probs.astype(BF)
    attended = jnp.einsum("hgqk,khd->qhgd", probs_low, values, preferred_element_type=F32)
    attended = attended.reshape(TOKENS, WIDTH).astype(BF)
    middle = tokens + mm(attended, w_out_full)
    normed_ffn, scale_two = norm(middle, gain_two)
    ffn_in = normed_ffn.astype(BF)

    rows = to_experts(mm(deal, ffn_in).astype(BF))

    logits = mm(ffn_in, router_full)
    top = jnp.max(jnp.where(hits, logits, NEGATIVE), axis=-1, keepdims=True)
    weight = jnp.where(hits, jnp.exp(jnp.where(hits, logits - top, 0.0)), 0.0)
    gates = weight / jnp.sum(weight, axis=-1, keepdims=True)

    shared_pair = mm(ffn_in, second)
    shared_gate, shared_upper = shared_pair[:, :1024], shared_pair[:, 1024:]
    sig = jax.nn.sigmoid(shared_gate)
    silu = shared_gate * sig
    shared_low = (silu * shared_upper).astype(BF)
    shared_out = mm(shared_low, down_full)
    shared_cot = mm_r(out_grad, down_full)
    slope = sig * (1.0 + shared_gate * (1.0 - sig))
    pair_low = jnp.concatenate(
        [(shared_cot * shared_upper * slope).astype(BF), (shared_cot * silu).astype(BF)], axis=1
    )
    pair_grad = scatter_rows(mm_l(ffn_in, pair_low).astype(BF))
    down_grad = scatter_rows(mm_l(shared_low, out_grad).astype(BF))
    ffn_cot = mm_r(pair_low, second)

    cot, marks = cot_rows[:, :WIDTH], cot_rows[:, WIDTH : WIDTH + EXPERTS] > 0
    act_cot = mm_r(cot, wd)
    gate_value = mm(rows, wg)
    upper_value = mm(rows, wu)
    row_logits = mm(rows, router_full)
    row_top = jnp.max(jnp.where(marks, row_logits, NEGATIVE), axis=-1, keepdims=True)
    row_weight = jnp.where(marks, jnp.exp(jnp.where(marks, row_logits - row_top, 0.0)), 0.0)
    own = expert_range == lax.axis_index(DP)
    row_sum = jnp.sum(row_weight, axis=-1, keepdims=True)
    row_own = jnp.sum(jnp.where(own, row_weight, 0.0), axis=-1, keepdims=True)
    row_gate = row_own / jnp.where(row_sum > 0, row_sum, 1.0)
    sig = jax.nn.sigmoid(gate_value)
    silu = gate_value * sig
    act = row_gate * silu * upper_value
    act_low = act.astype(BF)
    scaled_cot = row_gate * act_cot
    gate_low = (scaled_cot * upper_value * (sig * (1.0 + gate_value * (1.0 - sig)))).astype(BF)
    upper_low = (scaled_cot * silu).astype(BF)
    share = jnp.sum(act_cot * act, axis=-1, keepdims=True)
    share_high = share.astype(BF)
    share_low = (share - share_high.astype(F32)).astype(BF)
    zero = jnp.zeros((), BF)
    row_cot = (mm_r(gate_low, wg) + mm_r(upper_low, wu)).astype(BF)
    back = to_experts(
        jnp.concatenate(
            [row_cot, jnp.where(own, share_high, zero), jnp.where(own, share_low, zero)], axis=1
        )
    )
    result = to_experts(mm(act_low, wd).astype(BF))
    gate_w_grad = mm_l(rows, gate_low)
    upper_w_grad = mm_l(rows, upper_low)
    down_w_grad = mm_l(act_low, cot)
    gate_w_grad = gate_w_grad[:, :256] + swap(gate_w_grad[:, 256:].astype(BF), "zl").astype(F32)
    upper_w_grad = upper_w_grad[:, :256] + swap(upper_w_grad[:, 256:].astype(BF), "zl").astype(F32)
    down_w_grad = down_w_grad[:256] + swap(down_w_grad[256:].astype(BF), "zl").astype(F32)

    returned = mm_l(deal, back)
    shares = returned[:, WIDTH : WIDTH + 64] + returned[:, WIDTH + 64 :]
    logit_low = (shares - gates * jnp.sum(shares, axis=-1, keepdims=True)).astype(BF)
    ffn_cot = ffn_cot + returned[:, :WIDTH] + mm_r(logit_low, router_full)
    upstream = out_grad.astype(F32)
    norm_cot, gain_two_grad = norm_back(middle, scale_two, gain_two, ffn_cot)
    middle_cot = upstream + norm_cot
    middle_low = middle_cot.astype(BF)
    out_w_grad = mm_l(attended, middle_low).astype(BF)
    attended_cot = (
        mm_r(middle_low, w_out_full)
        .astype(BF)
        .reshape(TOKENS, KEY_VALUE_HEADS, GROUP, HEAD)
    )
    prob_cot = jnp.einsum(
        "qhgd,khd->hgqk", attended_cot, values, preferred_element_type=F32
    )
    value_cot = jnp.einsum(
        "hgqk,qhgd->khd", probs_low, attended_cot, preferred_element_type=F32
    )
    centre = jnp.sum(probs * prob_cot, axis=-1, keepdims=True)
    score_cot = (probs * (prob_cot - centre)).astype(BF)
    query_cot = (
        jnp.einsum("hgqk,khd->qhgd", score_cot, keys, preferred_element_type=F32) * scaling
    )
    key_cot = (
        jnp.einsum("hgqk,qhgd->khd", score_cot, queries, preferred_element_type=F32)
        * scaling
    )
    qkv_low = jnp.concatenate(
        [
            query_cot.astype(BF).reshape(TOKENS, -1),
            key_cot.astype(BF).reshape(TOKENS, -1),
            value_cot.astype(BF).reshape(TOKENS, -1),
        ],
        axis=1,
    )
    attn_cot = mm_r(qkv_low, w_qkv)
    token_cot, gain_one_grad = norm_back(tokens, scale_one, gain_one, attn_cot)
    grad_in = middle_cot + token_cot
    router_grad = mm_l(ffn_in, logit_low).astype(BF)
    misc = jnp.concatenate(
        [
            router_grad,
            gain_one_grad[:, None].astype(BF),
            gain_two_grad[:, None].astype(BF),
            jnp.zeros((WIDTH, 62), BF),
        ],
        axis=1,
    )
    dense = scatter_rows(
        jnp.concatenate([mm_l(attn_in, qkv_low).astype(BF), out_w_grad, misc], axis=1)
    )
    block_out = (middle + shared_out + mm_l(deal, result)).astype(BF)
    return (
        block_out,
        grad_in,
        dense[:, 4160],
        dense[:, :1536],
        dense[:, 1536:2048],
        dense[:, 2048:2560],
        dense[:, 2560:4096],
        dense[:, 4161],
        dense[:, 4096:4160],
        pair_grad[:, :1024],
        pair_grad[:, 1024:],
        down_grad,
        gate_w_grad[None],
        upper_w_grad[None],
        down_w_grad[None],
    )


def solution(mesh):
    fine = Mesh(mesh.devices.reshape(2, 4, 4, 2, 2), AXES)
    rows, vector = P(AXES, None), P(AXES)
    banks = (P(DP, None, "zl"), P(DP, None, "zl"), P(DP, "zl", None))
    return jax.shard_map(
        body,
        mesh=fine,
        in_specs=(rows, rows, rows, rows, vector, rows, rows, rows, rows, vector)
        + (rows, rows, rows, rows)
        + banks,
        out_specs=(rows, rows, vector, rows, rows, rows, rows, vector)
        + (rows, rows, rows, rows)
        + banks,
        check_vma=False,
    )
```

```python
import functools

import jax
import jax.numpy as jnp
from jax import lax
from jax.experimental import pallas as pl
from jax.experimental.pallas import tpu as pltpu
from jax.sharding import Mesh, PartitionSpec as P

GROUP = 3
HEAD = 128
EXPERTS = 64
SLOTS = 32
TOKENS = 256
WIDTH = 1536
SHARED = 1024
HALF = 256
ROWS = EXPERTS * SLOTS
WIDE = WIDTH + 128
PACK = 2 * WIDTH + 1024 + 128

EPSILON = 1e-06
NEGATIVE = -1e30
SCALING = HEAD ** (-0.5)
BF = jnp.bfloat16
F32 = jnp.float32

AXES = ("zh", "x", "y", "c", "zl")
DP = ("zh", "x", "y", "c")
PLANE = ("x", "y", "c")
ANY = pl.BlockSpec(memory_space=pl.ANY)


def mm(a, b):
    return jnp.dot(a, b, preferred_element_type=F32)


def mm_l(a, b):
    return lax.dot_general(a, b, (((0,), (0,)), ((), ())), preferred_element_type=F32)


def mm_r(a, b):
    return lax.dot_general(a, b, (((1,), (1,)), ((), ())), preferred_element_type=F32)


def swap(x, axis):
    return lax.ppermute(x, axis, [(0, 1), (1, 0)])


def out(shape, dtype):
    return jax.ShapeDtypeStruct(shape, dtype)


def full(shape):
    return pl.BlockSpec(shape, lambda *i: (0,) * len(shape))


def call(kernel, grid, in_specs, out_specs, out_shape, scratch=(), flops=0):
    return pl.pallas_call(
        kernel,
        grid=grid,
        in_specs=in_specs,
        out_specs=out_specs,
        out_shape=out_shape,
        scratch_shapes=list(scratch),
        compiler_params=pltpu.CompilerParams(vmem_limit_bytes=56 * 1024 * 1024),
        cost_estimate=pl.CostEstimate(flops=flops, bytes_accessed=0, transcendentals=0),
    )


def gather_plane(four):
    _, rows, width = four.shape
    whole = lax.all_gather(four.reshape(2, 2 * rows, width), PLANE, axis=1, tiled=True)
    return whole.reshape(128 * rows, width)


def scatter_plane(grads):
    return lax.psum_scatter(grads, PLANE, scatter_dimension=0, tiled=True)


def scatter_line(plane):
    r, width = plane.shape[0] // 2, plane.shape[1] // 2
    zh = lax.axis_index("zh")
    zl = lax.axis_index("zl")
    low, high = plane[:, :width], plane[:, width:]
    keep = jnp.where(zh == 0, low, high)
    give = jnp.where(zh == 0, high, low)
    pair = keep.astype(F32) + swap(give, "zh").astype(F32)
    keep = jnp.where(zl == 0, pair[:r], pair[r:])
    give = jnp.where(zl == 0, pair[r:], pair[:r]).astype(BF)
    return keep + swap(give, "zl").astype(F32)


def one_hot(rank_ref):
    rank = rank_ref[...]
    slot = lax.broadcasted_iota(jnp.int32, (8, SLOTS, TOKENS), 1).astype(F32)
    hit = jnp.where(rank[:, None, :] == slot, 1.0, 0.0)
    return hit.reshape(8 * SLOTS, TOKENS).astype(BF)


def dispatch_kernel(n, rank_ref, rows_ref, *refs):
    refs[n][...] = mm(one_hot(rank_ref), rows_ref[...]).astype(BF)


def dispatch(rank, rows, *after):
    width = rows.shape[1]
    return call(
        functools.partial(dispatch_kernel, len(after)),
        (8,),
        [pl.BlockSpec((8, TOKENS), lambda i: (i, 0)), full((TOKENS, width))]
        + [ANY] * len(after),
        pl.BlockSpec((8 * SLOTS, width), lambda i: (i, 0)),
        out((ROWS, width), BF),
    )(rank, rows, *after)


def to_experts(rows):
    return lax.all_to_all(
        rows.reshape(EXPERTS, SLOTS, -1), DP, split_axis=0, concat_axis=0, tiled=True
    ).reshape(ROWS, -1)


def result_kernel(rank_ref, rows_ref, base_ref, out_ref, acc):
    step = pl.program_id(0)

    @pl.when(step == 0)
    def _():
        acc[...] = base_ref[...]

    acc[...] += mm_l(one_hot(rank_ref), rows_ref[...])

    @pl.when(step == 7)
    def _():
        out_ref[...] = acc[...].astype(BF)


def add_results(rank, rows, base):
    return call(
        result_kernel,
        (8,),
        [
            pl.BlockSpec((8, TOKENS), lambda i: (i, 0)),
            pl.BlockSpec((8 * SLOTS, WIDTH), lambda i: (i, 0)),
            full((TOKENS, WIDTH)),
        ],
        full((TOKENS, WIDTH)),
        out((TOKENS, WIDTH), BF),
        [pltpu.VMEM((TOKENS, WIDTH), F32)],
    )(rank, rows, base)


def root_scale(values):
    return lax.rsqrt(jnp.mean(values * values, axis=-1, keepdims=True) + EPSILON)


def forward_kernel(
    hidden_ref,
    docs_ref,
    hits_ref,
    wq_ref,
    wo_ref,
    wkv_ref,
    small_ref,
    attn_in_ref,
    q_ref,
    kv_ref,
    probs_ref,
    attended_ref,
    middle_ref,
    ffn_in_ref,
    gates_ref,
    gains_ref,
):
    gains = jnp.transpose(small_ref[...].astype(F32))
    gains_ref[...] = gains[64:72]
    gain_one, gain_two = gains[64:65], gains[65:66]
    tokens = hidden_ref[...].astype(F32)
    attn_in_ref[...] = (tokens * root_scale(tokens) * gain_one).astype(BF)
    for j in range(0, WIDTH, 512):
        q_ref[:, j : j + 512] = mm(attn_in_ref[...], wq_ref[:, j : j + 512]).astype(BF)
    for j in range(0, 1024, 512):
        kv_ref[:, j : j + 512] = mm(attn_in_ref[...], wkv_ref[:, j : j + 512]).astype(BF)
    first = docs_ref[0, 0]
    second = first + docs_ref[0, 1]
    third = second + docs_ref[0, 2]
    row = lax.broadcasted_iota(jnp.int32, (TOKENS, TOKENS), 0)
    col = lax.broadcasted_iota(jnp.int32, (TOKENS, TOKENS), 1)

    def segment(place):
        return (
            (place >= first).astype(jnp.int32)
            + (place >= second).astype(jnp.int32)
            + (place >= third).astype(jnp.int32)
        )

    visible = (segment(row) == segment(col)) & (row >= col)
    for kv_head in range(4):
        key = kv_ref[:, kv_head * HEAD : (kv_head + 1) * HEAD]
        value = kv_ref[:, 512 + kv_head * HEAD : 512 + (kv_head + 1) * HEAD]
        for head in range(kv_head * GROUP, (kv_head + 1) * GROUP):
            at = slice(head * HEAD, (head + 1) * HEAD)
            scores = jnp.where(visible, mm_r(q_ref[:, at], key) * SCALING, NEGATIVE)
            exponent = jnp.exp(scores - jnp.max(scores, axis=-1, keepdims=True))
            probs = exponent / jnp.sum(exponent, axis=-1, keepdims=True)
            probs_ref[head] = probs
            attended_ref[:, at] = mm(probs.astype(BF), value).astype(BF)
    for j in range(0, WIDTH, 512):
        at = slice(j, j + 512)
        middle_ref[:, at] = hidden_ref[:, at].astype(F32) + mm(
            attended_ref[...], wo_ref[:, at]
        )
    middle = middle_ref[...]
    ffn_in_ref[...] = (middle * root_scale(middle) * gain_two).astype(BF)
    logits = mm(ffn_in_ref[...], small_ref[...])
    hits = hits_ref[...] > 0
    top = jnp.max(jnp.where(hits, logits, NEGATIVE), axis=-1, keepdims=True)
    weight = jnp.where(hits, jnp.exp(jnp.where(hits, logits - top, 0.0)), 0.0)
    gates_ref[...] = weight / jnp.sum(weight, axis=-1, keepdims=True)


def pack_specs():
    return [
        pl.BlockSpec((WIDTH, WIDTH), lambda *i: (0, 0)),
        pl.BlockSpec((WIDTH, WIDTH), lambda *i: (0, 1)),
        pl.BlockSpec((WIDTH, 1024), lambda *i: (0, 3)),
        pl.BlockSpec((WIDTH, 128), lambda *i: (0, 32)),
    ]


def forward(hidden, docs, hits, pack):
    wide = (TOKENS, WIDTH)
    shapes = [
        (wide, BF),
        (wide, BF),
        ((TOKENS, 1024), BF),
        ((12, TOKENS, TOKENS), F32),
        (wide, BF),
        (wide, F32),
        (wide, BF),
        ((TOKENS, 128), F32),
        ((8, WIDTH), F32),
    ]
    return call(
        forward_kernel,
        (1,),
        [full(wide), pl.BlockSpec(memory_space=pltpu.SMEM), full((TOKENS, 128))] + pack_specs(),
        [full(s) for s, _ in shapes],
        [out(s, d) for s, d in shapes],
    )(hidden, docs, hits, pack, pack, pack, pack)


def act_cot_kernel(cot_ref, down_ref, other_ref, out_ref):
    out_ref[:, :HALF] = mm_r(cot_ref[...], down_ref[...])
    out_ref[:, HALF:] = mm_r(cot_ref[...], other_ref[...])


def act_cots(cot_rows, down, other):
    return call(
        act_cot_kernel,
        (8,),
        [pl.BlockSpec((256, WIDTH), lambda i: (i, 0)), full((HALF, WIDTH)), full((HALF, WIDTH))],
        pl.BlockSpec((256, 2 * HALF), lambda i: (i, 0)),
        out((ROWS, 2 * HALF), F32),
    )(cot_rows, down, other)


def expert_kernel(
    rows_ref,
    marks_ref,
    act_cot_ref,
    own_ref,
    small_ref,
    gate_ref,
    gate_other_ref,
    up_ref,
    up_other_ref,
    _after_ref,
    back_ref,
    act_ref,
    gate_cot_ref,
    up_cot_ref,
):
    rows = rows_ref[...]
    marks = marks_ref[...] > 0
    logits = mm(rows, small_ref[...])
    top = jnp.max(jnp.where(marks, logits, NEGATIVE), axis=-1, keepdims=True)
    weight = jnp.where(marks, jnp.exp(jnp.where(marks, logits - top, 0.0)), 0.0)
    own = own_ref[...]
    total = jnp.sum(weight, axis=-1, keepdims=True)
    mine = jnp.sum(weight * own, axis=-1, keepdims=True)
    route_gate = mine / jnp.where(total > 0, total, 1.0)
    share = jnp.zeros((256, 1), F32)
    for half, gate_w, up_w in ((0, gate_ref, up_ref), (1, gate_other_ref, up_other_ref)):
        at = slice(half * HALF, (half + 1) * HALF)
        gate = mm(rows, gate_w[...])
        upper = mm(rows, up_w[...])
        sig = 1.0 / (1.0 + jnp.exp(-gate))
        silu = gate * sig
        act_cot = act_cot_ref[:, at]
        act = route_gate * silu * upper
        act_ref[:, at] = act.astype(BF)
        share += jnp.sum(act_cot * act, axis=-1, keepdims=True)
        scaled = route_gate * act_cot
        gate_cot_ref[:, at] = (scaled * upper * (sig * (1.0 + gate * (1.0 - sig)))).astype(BF)
        up_cot_ref[:, at] = (scaled * silu).astype(BF)
    for j in range(0, WIDTH, 512):
        at = slice(j, j + 512)
        total = mm_r(gate_cot_ref[:, :HALF], gate_ref[at, :])
        total += mm_r(gate_cot_ref[:, HALF:], gate_other_ref[at, :])
        total += mm_r(up_cot_ref[:, :HALF], up_ref[at, :])
        total += mm_r(up_cot_ref[:, HALF:], up_other_ref[at, :])
        back_ref[:, at] = total.astype(BF)
    high = share.astype(BF).astype(F32)
    lane = lax.broadcasted_iota(jnp.int32, (1, 128), 1)
    placed = jnp.where(lane < 64, high, share - high) * (own + pltpu.roll(own, 64, 1))
    back_ref[:, WIDTH:] = placed.astype(BF)


def expert_phase(rows, cot_rows, act_cot, own, pack, gate, gate_other, up, up_other, after):
    tile = lambda w, j=0: pl.BlockSpec((256, w), lambda i: (i, j))
    weight = full((WIDTH, HALF))
    return call(
        expert_kernel,
        (8,),
        [tile(WIDTH), tile(128, 12), tile(512), full((1, 128)), pack_specs()[3]]
        + [weight] * 4
        + [ANY],
        [tile(WIDE), tile(512), tile(512), tile(512)],
        [out((ROWS, WIDE), BF)] + [out((ROWS, 512), BF)] * 3,
    )(rows, cot_rows, act_cot, own, pack, gate, gate_other, up, up_other, after)


def expert_out_kernel(act_ref, down_ref, other_ref, _after_ref, out_ref):
    total = mm(act_ref[:, :HALF], down_ref[...]) + mm(act_ref[:, HALF:], other_ref[...])
    out_ref[...] = total.astype(BF)


def expert_outs(act, down, other, after):
    return call(
        expert_out_kernel,
        (8,),
        [
            pl.BlockSpec((256, 512), lambda i: (i, 0)),
            full((HALF, WIDTH)),
            full((HALF, WIDTH)),
            ANY,
        ],
        pl.BlockSpec((256, WIDTH), lambda i: (i, 0)),
        out((ROWS, WIDTH), BF),
    )(act, down, other, after)


def expert_grad_kernel(
    rows_ref, cot_ref, act_ref, gate_cot_ref, up_cot_ref, _after_ref, gate_ref, up_ref, down_ref, gate, up, down
):
    step = pl.program_id(0)

    @pl.when(step == 0)
    def _():
        gate[...] = jnp.zeros_like(gate)
        up[...] = jnp.zeros_like(up)
        down[...] = jnp.zeros_like(down)

    gate[...] += mm_l(rows_ref[...], gate_cot_ref[...])
    up[...] += mm_l(rows_ref[...], up_cot_ref[...])
    down[...] += mm_l(act_ref[...], cot_ref[...])

    @pl.when(step == 7)
    def _():
        gate_ref[...] = gate[...].astype(gate_ref.dtype)
        up_ref[...] = up[...].astype(up_ref.dtype)
        down_ref[...] = down[...].astype(down_ref.dtype)


def expert_grads(half, dtype, rows, cot_rows, act, gate_cot, up_cot, after):
    tile = lambda w, j=0: pl.BlockSpec((256, w), lambda i: (i, j))
    shapes = [(WIDTH, HALF), (WIDTH, HALF), (HALF, WIDTH)]
    return call(
        expert_grad_kernel,
        (8,),
        [tile(WIDTH), tile(WIDTH), tile(HALF, half), tile(HALF, half), tile(HALF, half), ANY],
        [full(s) for s in shapes],
        [out(s, dtype) for s in shapes],
        [pltpu.VMEM(s, F32) for s in shapes],
    )(rows, cot_rows, act, gate_cot, up_cot, after)


def shared_grad_kernel(ffn_in_ref, pair_ref, act_ref, cot_ref, _after_ref, pair_out_ref, down_out_ref):
    for j in range(0, 2 * SHARED, 512):
        at = slice(j, j + 512)
        pair_out_ref[:, at] = mm_l(ffn_in_ref[...], pair_ref[:, at]).astype(BF)
    for j in range(0, WIDTH, 512):
        at = slice(j, j + 512)
        down_out_ref[:, at] = mm_l(act_ref[...], cot_ref[:, at]).astype(BF)


def shared_grads(ffn_in, pair_low, shared_low, out_grad, after):
    return call(
        shared_grad_kernel,
        (2,),
        [
            pl.BlockSpec((TOKENS, 768), lambda h: (0, h)),
            full((TOKENS, 2 * SHARED)),
            pl.BlockSpec((TOKENS, 512), lambda h: (0, h)),
            full((TOKENS, WIDTH)),
            ANY,
        ],
        [
            pl.BlockSpec((768, 2 * SHARED), lambda h: (0, h)),
            pl.BlockSpec((512, WIDTH), lambda h: (0, h)),
        ],
        [out((768, 4 * SHARED), BF), out((512, 2 * WIDTH), BF)],
    )(ffn_in, pair_low, shared_low, out_grad, after)


def norm_back(values, scale, gain, cot):
    weighted = cot * gain
    centre = jnp.mean(weighted * values, axis=-1, keepdims=True)
    return scale * weighted - values * (scale * scale * scale * centre)


def middle_kernel(
    rank_ref,
    back_ref,
    shared_cot_ref,
    gates_ref,
    middle_ref,
    gains_ref,
    out_grad_ref,
    small_ref,
    wo_ref,
    middle_cot_ref,
    middle_low_ref,
    attended_cot_ref,
    logit_ref,
    gain_rows_ref,
    acc,
):
    step = pl.program_id(0)

    @pl.when(step == 0)
    def _():
        acc[...] = jnp.zeros_like(acc)

    acc[...] += mm_l(one_hot(rank_ref), back_ref[...])

    @pl.when(step == 7)
    def _():
        extra = acc[:, WIDTH:]
        lane = lax.broadcasted_iota(jnp.int32, (1, 128), 1)
        shares = jnp.where(lane < 64, extra + pltpu.roll(extra, 64, 1), 0.0)
        logit = shares - gates_ref[...] * jnp.sum(shares, axis=-1, keepdims=True)
        logit_ref[...] = logit.astype(BF)
        cot = acc[:, :WIDTH] + shared_cot_ref[...] + mm_r(logit_ref[...], small_ref[...])
        middle = middle_ref[...]
        scale = root_scale(middle)
        gain_rows_ref[...] = (cot * middle * scale).astype(BF)
        total = out_grad_ref[...].astype(F32) + norm_back(middle, scale, gains_ref[1:2], cot)
        middle_cot_ref[...] = total
        middle_low_ref[...] = total.astype(BF)
        for j in range(0, WIDTH, 512):
            at = slice(j, j + 512)
            attended_cot_ref[:, at] = mm_r(middle_low_ref[...], wo_ref[at, :]).astype(BF)


def middle_back(rank, back, shared_cot, gates, middle, gains, out_grad, pack):
    wide = (TOKENS, WIDTH)
    shapes = [(wide, F32), (wide, BF), (wide, BF), ((TOKENS, 128), BF), (wide, BF)]
    specs = pack_specs()
    return call(
        middle_kernel,
        (8,),
        [
            pl.BlockSpec((8, TOKENS), lambda i: (i, 0)),
            pl.BlockSpec((8 * SLOTS, WIDE), lambda i: (i, 0)),
            full(wide),
            full((TOKENS, 128)),
            full(wide),
            full((8, WIDTH)),
            full(wide),
            specs[3],
            specs[1],
        ],
        [full(s) for s, _ in shapes],
        [out(s, d) for s, d in shapes],
        [pltpu.VMEM((TOKENS, WIDE), F32)],
    )(rank, back, shared_cot, gates, middle, gains, out_grad, pack, pack)


def attention_back_kernel(
    q_ref,
    k_ref,
    v_ref,
    probs_ref,
    cot_ref,
    wq_ref,
    wk_ref,
    wv_ref,
    hidden_ref,
    gains_ref,
    middle_cot_ref,
    dq_ref,
    dk_ref,
    dv_ref,
    grad_in_ref,
    gain_rows_ref,
    acc,
):
    step = pl.program_id(0)
    key, value = k_ref[...], v_ref[...]
    dk = jnp.zeros((TOKENS, HEAD), F32)
    dv = jnp.zeros((TOKENS, HEAD), F32)
    for g in range(GROUP):
        at = slice(g * HEAD, (g + 1) * HEAD)
        probs = probs_ref[g]
        cot = cot_ref[:, at]
        dprobs = mm_r(cot, value)
        dv += mm_l(probs.astype(BF), cot)
        centre = jnp.sum(probs * dprobs, axis=-1, keepdims=True)
        dscores = (probs * (dprobs - centre)).astype(BF)
        dq_ref[:, at] = (mm(dscores, key) * SCALING).astype(BF)
        dk += mm_l(dscores, q_ref[:, at])
    dk_ref[...] = (dk * SCALING).astype(BF)
    dv_ref[...] = dv.astype(BF)

    @pl.when(step == 0)
    def _():
        acc[...] = jnp.zeros_like(acc)

    for j in range(0, WIDTH, 512):
        at = slice(j, j + 512)
        acc[:, at] += (
            mm_r(dq_ref[...], wq_ref[at, :])
            + mm_r(dk_ref[...], wk_ref[at, :])
            + mm_r(dv_ref[...], wv_ref[at, :])
        )

    @pl.when(step == 3)
    def _():
        tokens = hidden_ref[...].astype(F32)
        scale = root_scale(tokens)
        cot = acc[...]
        gain_rows_ref[...] = (cot * tokens * scale).astype(BF)
        grad_in_ref[...] = middle_cot_ref[...] + norm_back(tokens, scale, gains_ref[0:1], cot)


def attention_back(q, kv, probs, attended_cot, pack, hidden, gains, middle_cot):
    wide = (TOKENS, WIDTH)
    col = lambda w, j: pl.BlockSpec((TOKENS, w), lambda h: (0, j + h))
    weight = lambda w, j: pl.BlockSpec((WIDTH, w), lambda h: (0, j + h))
    return call(
        attention_back_kernel,
        (4,),
        [
            col(GROUP * HEAD, 0),
            col(HEAD, 0),
            col(HEAD, 4),
            pl.BlockSpec((GROUP, TOKENS, TOKENS), lambda h: (h, 0, 0)),
            col(GROUP * HEAD, 0),
            weight(GROUP * HEAD, 0),
            weight(HEAD, 24),
            weight(HEAD, 28),
            full(wide),
            full((8, WIDTH)),
            full(wide),
        ],
        [col(GROUP * HEAD, 0), col(HEAD, 0), col(HEAD, 0), full(wide), full(wide)],
        [
            out(wide, BF),
            out((TOKENS, 512), BF),
            out((TOKENS, 512), BF),
            out(wide, F32),
            out(wide, BF),
        ],
        [pltpu.VMEM(wide, F32)],
    )(q, kv, kv, probs, attended_cot, pack, pack, pack, hidden, gains, middle_cot)


def dense_grad_kernel(
    attn_in_ref,
    attended_ref,
    ffn_in_ref,
    gain_one_ref,
    gain_two_ref,
    dq_ref,
    middle_ref,
    dk_ref,
    dv_ref,
    logit_ref,
    out_ref,
):
    for j in range(0, WIDTH, 512):
        at = slice(j, j + 512)
        out_ref[:, at] = mm_l(attn_in_ref[...], dq_ref[:, at]).astype(BF)
        out_ref[:, WIDTH + j : WIDTH + j + 512] = mm_l(
            attended_ref[...], middle_ref[:, at]
        ).astype(BF)
    out_ref[:, 2 * WIDTH : 2 * WIDTH + 512] = mm_l(attn_in_ref[...], dk_ref[...]).astype(BF)
    out_ref[:, 2 * WIDTH + 512 : 2 * WIDTH + 1024] = mm_l(attn_in_ref[...], dv_ref[...]).astype(BF)
    lane = lax.broadcasted_iota(jnp.int32, (TOKENS, 128), 1)
    small = mm_l(ffn_in_ref[...], logit_ref[...])
    small += mm_l(gain_one_ref[...], jnp.where(lane == 64, 1.0, 0.0).astype(BF))
    small += mm_l(gain_two_ref[...], jnp.where(lane == 65, 1.0, 0.0).astype(BF))
    out_ref[:, 2 * WIDTH + 1024 :] = small.astype(BF)


def dense_grads(attn_in, attended, ffn_in, gain_one, gain_two, dq, middle_low, dk, dv, logit):
    left = pl.BlockSpec((TOKENS, 768), lambda h: (0, h))
    wide = full((TOKENS, WIDTH))
    thin = full((TOKENS, 512))
    return call(
        dense_grad_kernel,
        (2,),
        [left] * 5 + [wide, wide, thin, thin, full((TOKENS, 128))],
        pl.BlockSpec((768, PACK), lambda h: (0, h)),
        out((768, 2 * PACK), BF),
    )(attn_in, attended, ffn_in, gain_one, gain_two, dq, middle_low, dk, dv, logit)


def body(
    hidden_in,
    out_grad,
    doc_lengths,
    expert_ids,
    gain_attn,
    w_query,
    w_key,
    w_value,
    w_out,
    gain_ffn,
    w_router,
    w_shared_gate,
    w_shared_up,
    w_shared_down,
    expert_gate,
    expert_up,
    expert_down,
):
    parts = [w_query, w_out, w_key, w_value, w_router, gain_attn[:, None], gain_ffn[:, None]]
    parts += [jnp.zeros((12, 62), BF), w_shared_gate, w_shared_up, w_shared_down.reshape(12, 1024)]
    line = lax.all_gather(jnp.concatenate(parts, axis=1), ("zh", "zl"), axis=0, tiled=False)
    pack = gather_plane(line[:, :, :PACK])
    pair_w = gather_plane(line[:, :, PACK : PACK + 2 * SHARED])
    down_w = gather_plane(line[:, :, PACK + 2 * SHARED :].reshape(4, 8, WIDTH))
    gate, up, down = expert_gate[0], expert_up[0], expert_down[0]
    gate_other, up_other, down_other = swap(gate, "zl"), swap(up, "zl"), swap(down, "zl")

    lanes = jnp.arange(128, dtype=jnp.int32)
    hits = jnp.any(expert_ids[:, :, None] == lanes, axis=1)
    hits_low = hits.astype(BF)
    place = jnp.arange(TOKENS, dtype=jnp.int32)
    earlier = (place[:, None] > place[None, :]).astype(BF)
    rank = jnp.where(hits, mm(earlier, hits_low), -1.0).T[:EXPERTS]
    own = (lanes == lax.axis_index(DP)).astype(F32)[None]

    marked = jnp.concatenate([out_grad, hits_low], axis=1)
    cot_rows = to_experts(dispatch(rank, marked, pack, gate_other, up_other, down_other))

    attn_in, q, kv, probs, attended, middle, ffn_in, gates, gains = forward(
        hidden_in, doc_lengths, hits_low, pack
    )
    rows = to_experts(dispatch(rank, ffn_in))

    pair = mm(ffn_in, pair_w)
    shared_gate, shared_upper = pair[:, :SHARED], pair[:, SHARED:]
    sig = jax.nn.sigmoid(shared_gate)
    silu = shared_gate * sig
    shared_low = (silu * shared_upper).astype(BF)
    shared_sum = middle + mm(shared_low, down_w)
    shared_cot = mm_r(out_grad, down_w)
    slope = sig * (1.0 + shared_gate * (1.0 - sig))
    pair_low = jnp.concatenate(
        [(shared_cot * shared_upper * slope).astype(BF), (shared_cot * silu).astype(BF)], axis=1
    )
    shared_cot = mm_r(pair_low, pair_w)

    act_cot = act_cots(cot_rows, down, down_other)
    back, act, gate_cot, up_cot = expert_phase(
        rows, cot_rows, act_cot, own, pack, gate, gate_other, up, up_other, shared_cot
    )
    pair_grad, down_grad = shared_grads(ffn_in, pair_low, shared_low, out_grad, act)
    pair_grad, down_grad = scatter_plane(pair_grad), scatter_plane(down_grad)
    back = to_experts(back)
    result = to_experts(expert_outs(act, down, down_other, gate_cot))

    middle_cot, middle_low, attended_cot, logit, gain_two_rows = middle_back(
        rank, back, shared_cot, gates, middle, gains, out_grad, pack
    )
    dq, dk, dv, grad_in, gain_one_rows = attention_back(
        q, kv, probs, attended_cot, pack, hidden_in, gains, middle_cot
    )
    dense_grad = dense_grads(
        attn_in, attended, ffn_in, gain_one_rows, gain_two_rows, dq, middle_low, dk, dv, logit
    )
    dense = scatter_line(scatter_plane(dense_grad))
    pair_grad = scatter_line(pair_grad)
    down_grad = scatter_line(down_grad)
    block_out = add_results(rank, result, shared_sum)
    sent = expert_grads(1, BF, rows, cot_rows, act, gate_cot, up_cot, dense_grad)
    kept = expert_grads(0, F32, rows, cot_rows, act, gate_cot, up_cot, back)
    expert = [(k + swap(s, "zl").astype(F32))[None] for k, s in zip(kept, sent)]
    at = 2 * WIDTH
    return (
        block_out,
        grad_in,
        dense[:, at + 1088],
        dense[:, :WIDTH],
        dense[:, at : at + 512],
        dense[:, at + 512 : at + 1024],
        dense[:, WIDTH:at],
        dense[:, at + 1089],
        dense[:, at + 1024 : at + 1088],
        pair_grad[:, :SHARED],
        pair_grad[:, SHARED:],
        down_grad,
        expert[0],
        expert[1],
        expert[2],
    )


def solution(mesh):
    fine = Mesh(mesh.devices.reshape(2, 4, 4, 2, 2), AXES)
    rows, vector = P(AXES, None), P(AXES)
    banks = (P(DP, None, "zl"), P(DP, None, "zl"), P(DP, "zl", None))
    return jax.shard_map(
        body,
        mesh=fine,
        in_specs=(rows, rows, rows, rows, vector, rows, rows, rows, rows, vector)
        + (rows, rows, rows, rows)
        + banks,
        out_specs=(rows, rows, vector, rows, rows, rows, rows, vector)
        + (rows, rows, rows, rows)
        + banks,
        check_vma=False,
    )
```

```python
import jax
import jax.numpy as jnp
from jax import lax
from jax.experimental import pallas as pl
from jax.experimental.pallas import tpu as pltpu
from jax.sharding import Mesh, PartitionSpec as P

GROUP = 3
HEAD = 128
EXPERTS = 64
SLOTS = 32
TOKENS = 256
WIDTH = 1536
SHARED = 1024
HALF = 256
ROWS = EXPERTS * SLOTS
WIDE = WIDTH + 128
PACK = 2 * WIDTH + 1024 + 128

EPSILON = 1e-06
NEGATIVE = -1e30
SCALING = HEAD ** (-0.5)
BF = jnp.bfloat16
F32 = jnp.float32

AXES = ("zh", "x", "y", "c", "zl")
DP = ("zh", "x", "y", "c")
PLANE = ("x", "y", "c")
ANY = pl.BlockSpec(memory_space=pl.ANY)


def mm(a, b):
    return jnp.dot(a, b, preferred_element_type=F32)


def mm_l(a, b):
    return lax.dot_general(a, b, (((0,), (0,)), ((), ())), preferred_element_type=F32)


def mm_r(a, b):
    return lax.dot_general(a, b, (((1,), (1,)), ((), ())), preferred_element_type=F32)


def swap(x, axis):
    return lax.ppermute(x, axis, [(0, 1), (1, 0)])


def out(shape, dtype):
    return jax.ShapeDtypeStruct(shape, dtype)


def full(shape):
    return pl.BlockSpec(shape, lambda *i: (0,) * len(shape))


def call(kernel, grid, in_specs, out_specs, out_shape, scratch=(), flops=0):
    return pl.pallas_call(
        kernel,
        grid=grid,
        in_specs=in_specs,
        out_specs=out_specs,
        out_shape=out_shape,
        scratch_shapes=list(scratch),
        compiler_params=pltpu.CompilerParams(vmem_limit_bytes=56 * 1024 * 1024),
        cost_estimate=pl.CostEstimate(flops=flops, bytes_accessed=0, transcendentals=0),
    )


def tie_kernel(*refs):
    pass


def tie(x, *after):
    return pl.pallas_call(
        tie_kernel,
        in_specs=[ANY] * (1 + len(after)),
        out_specs=ANY,
        out_shape=out(x.shape, x.dtype),
        input_output_aliases={0: 0},
    )(x, *after)


def gather_plane(pairs):
    _, rows, width = pairs.shape
    return lax.all_gather(pairs, PLANE, axis=1, tiled=True).reshape(64 * rows, width)


def scatter_plane(grads):
    return lax.psum_scatter(grads, PLANE, scatter_dimension=0, tiled=True)


def sum_zh(plane):
    width = plane.shape[1] // 2
    zh = lax.axis_index("zh")
    low, high = plane[:, :width], plane[:, width:]
    keep = jnp.where(zh == 0, low, high)
    give = jnp.where(zh == 0, high, low)
    return keep.astype(F32) + swap(give, "zh").astype(F32)


def sum_zl(mine, other):
    zl = lax.axis_index("zl")
    keep = jnp.where(zl == 0, mine, other)
    give = jnp.where(zl == 0, other, mine).astype(BF)
    return keep + swap(give, "zl").astype(F32)


def fold_down(rows):
    tail = [rows[:, :8, 1024:], rows[:, 8:, 1024:]]
    return jnp.concatenate([rows[:, :, :1024], jnp.concatenate(tail, axis=2)], axis=1)


def unfold_down(rows):
    tail = jnp.concatenate([rows[:, 16:, :512], rows[:, 16:, 512:]], axis=1)
    return jnp.concatenate([rows[:, :16], tail], axis=2)


def one_hot(rank_ref):
    rank = rank_ref[...]
    slot = lax.broadcasted_iota(jnp.int32, (8, SLOTS, TOKENS), 1).astype(F32)
    hit = jnp.where(rank[:, None, :] == slot, 1.0, 0.0)
    return hit.reshape(8 * SLOTS, TOKENS).astype(BF)


def dispatch_kernel(rank_ref, rows_ref, out_ref):
    out_ref[...] = mm(one_hot(rank_ref), rows_ref[...]).astype(BF)


def dispatch(rank, rows):
    width = rows.shape[1]
    return call(
        dispatch_kernel,
        (8,),
        [pl.BlockSpec((8, TOKENS), lambda i: (i, 0)), full((TOKENS, width))],
        pl.BlockSpec((8 * SLOTS, width), lambda i: (i, 0)),
        out((ROWS, width), BF),
    )(rank, rows)


def to_experts(rows):
    return lax.all_to_all(
        rows.reshape(EXPERTS, SLOTS, -1), DP, split_axis=0, concat_axis=0, tiled=True
    ).reshape(ROWS, -1)


def result_kernel(rank_ref, rows_ref, base_ref, out_ref, acc):
    step = pl.program_id(0)

    @pl.when(step == 0)
    def _():
        acc[...] = base_ref[...]

    acc[...] += mm_l(one_hot(rank_ref), rows_ref[...])

    @pl.when(step == 7)
    def _():
        out_ref[...] = acc[...].astype(BF)


def add_results(rank, rows, base):
    return call(
        result_kernel,
        (8,),
        [
            pl.BlockSpec((8, TOKENS), lambda i: (i, 0)),
            pl.BlockSpec((8 * SLOTS, WIDTH), lambda i: (i, 0)),
            full((TOKENS, WIDTH)),
        ],
        full((TOKENS, WIDTH)),
        out((TOKENS, WIDTH), BF),
        [pltpu.VMEM((TOKENS, WIDTH), F32)],
        flops=10**12,
    )(rank, rows, base)


def root_scale(values):
    return lax.rsqrt(jnp.mean(values * values, axis=-1, keepdims=True) + EPSILON)


def forward_kernel(
    hidden_ref,
    docs_ref,
    hits_ref,
    wq_ref,
    wo_ref,
    wkv_ref,
    small_ref,
    attn_in_ref,
    q_ref,
    kv_ref,
    probs_ref,
    attended_ref,
    middle_ref,
    ffn_in_ref,
    gates_ref,
    gains_ref,
):
    gains = jnp.transpose(small_ref[...].astype(F32))
    gains_ref[...] = gains[64:72]
    gain_one, gain_two = gains[64:65], gains[65:66]
    tokens = hidden_ref[...].astype(F32)
    attn_in_ref[...] = (tokens * root_scale(tokens) * gain_one).astype(BF)
    for j in range(0, WIDTH, 512):
        q_ref[:, j : j + 512] = mm(attn_in_ref[...], wq_ref[:, j : j + 512]).astype(BF)
    for j in range(0, 1024, 512):
        kv_ref[:, j : j + 512] = mm(attn_in_ref[...], wkv_ref[:, j : j + 512]).astype(BF)
    first = docs_ref[0, 0]
    second = first + docs_ref[0, 1]
    third = second + docs_ref[0, 2]
    row = lax.broadcasted_iota(jnp.int32, (TOKENS, TOKENS), 0)
    col = lax.broadcasted_iota(jnp.int32, (TOKENS, TOKENS), 1)

    def segment(place):
        return (
            (place >= first).astype(jnp.int32)
            + (place >= second).astype(jnp.int32)
            + (place >= third).astype(jnp.int32)
        )

    visible = (segment(row) == segment(col)) & (row >= col)
    for kv_head in range(4):
        key = kv_ref[:, kv_head * HEAD : (kv_head + 1) * HEAD]
        value = kv_ref[:, 512 + kv_head * HEAD : 512 + (kv_head + 1) * HEAD]
        for head in range(kv_head * GROUP, (kv_head + 1) * GROUP):
            at = slice(head * HEAD, (head + 1) * HEAD)
            scores = jnp.where(visible, mm_r(q_ref[:, at], key) * SCALING, NEGATIVE)
            exponent = jnp.exp(scores - jnp.max(scores, axis=-1, keepdims=True))
            probs = exponent / jnp.sum(exponent, axis=-1, keepdims=True)
            probs_ref[head] = probs
            attended_ref[:, at] = mm(probs.astype(BF), value).astype(BF)
    for j in range(0, WIDTH, 512):
        at = slice(j, j + 512)
        middle_ref[:, at] = hidden_ref[:, at].astype(F32) + mm(
            attended_ref[...], wo_ref[:, at]
        )
    middle = middle_ref[...]
    ffn_in_ref[...] = (middle * root_scale(middle) * gain_two).astype(BF)
    logits = mm(ffn_in_ref[...], small_ref[...])
    hits = hits_ref[...] > 0
    top = jnp.max(jnp.where(hits, logits, NEGATIVE), axis=-1, keepdims=True)
    weight = jnp.where(hits, jnp.exp(jnp.where(hits, logits - top, 0.0)), 0.0)
    gates_ref[...] = weight / jnp.sum(weight, axis=-1, keepdims=True)


def pack_specs():
    return [
        pl.BlockSpec((WIDTH, WIDTH), lambda *i: (0, 0)),
        pl.BlockSpec((WIDTH, WIDTH), lambda *i: (0, 1)),
        pl.BlockSpec((WIDTH, 1024), lambda *i: (0, 3)),
        pl.BlockSpec((WIDTH, 128), lambda *i: (0, 32)),
    ]


def forward(hidden, docs, hits, pack):
    wide = (TOKENS, WIDTH)
    shapes = [
        (wide, BF),
        (wide, BF),
        ((TOKENS, 1024), BF),
        ((12, TOKENS, TOKENS), F32),
        (wide, BF),
        (wide, F32),
        (wide, BF),
        ((TOKENS, 128), F32),
        ((8, WIDTH), F32),
    ]
    return call(
        forward_kernel,
        (1,),
        [full(wide), pl.BlockSpec(memory_space=pltpu.SMEM), full((TOKENS, 128))] + pack_specs(),
        [full(s) for s, _ in shapes],
        [out(s, d) for s, d in shapes],
    )(hidden, docs, hits, pack, pack, pack, pack)


def act_cot_kernel(cot_ref, down_ref, other_ref, out_ref):
    out_ref[:, :HALF] = mm_r(cot_ref[...], down_ref[...])
    out_ref[:, HALF:] = mm_r(cot_ref[...], other_ref[...])


def act_cots(cot_rows, down, other):
    return call(
        act_cot_kernel,
        (8,),
        [pl.BlockSpec((256, WIDTH), lambda i: (i, 0)), full((HALF, WIDTH)), full((HALF, WIDTH))],
        pl.BlockSpec((256, 2 * HALF), lambda i: (i, 0)),
        out((ROWS, 2 * HALF), F32),
    )(cot_rows, down, other)


def expert_kernel(
    rows_ref,
    marks_ref,
    act_cot_ref,
    own_ref,
    small_ref,
    gate_ref,
    gate_other_ref,
    up_ref,
    up_other_ref,
    _after_ref,
    back_ref,
    act_ref,
    gate_cot_ref,
    up_cot_ref,
):
    rows = rows_ref[...]
    marks = marks_ref[...] > 0
    logits = mm(rows, small_ref[...])
    top = jnp.max(jnp.where(marks, logits, NEGATIVE), axis=-1, keepdims=True)
    weight = jnp.where(marks, jnp.exp(jnp.where(marks, logits - top, 0.0)), 0.0)
    own = own_ref[...]
    total = jnp.sum(weight, axis=-1, keepdims=True)
    mine = jnp.sum(weight * own, axis=-1, keepdims=True)
    route_gate = mine / jnp.where(total > 0, total, 1.0)
    share = jnp.zeros((256, 1), F32)
    for half, gate_w, up_w in ((0, gate_ref, up_ref), (1, gate_other_ref, up_other_ref)):
        at = slice(half * HALF, (half + 1) * HALF)
        gate = mm(rows, gate_w[...])
        upper = mm(rows, up_w[...])
        sig = 1.0 / (1.0 + jnp.exp(-gate))
        silu = gate * sig
        act_cot = act_cot_ref[:, at]
        act = route_gate * silu * upper
        act_ref[:, at] = act.astype(BF)
        share += jnp.sum(act_cot * act, axis=-1, keepdims=True)
        scaled = route_gate * act_cot
        gate_cot_ref[:, at] = (scaled * upper * (sig * (1.0 + gate * (1.0 - sig)))).astype(BF)
        up_cot_ref[:, at] = (scaled * silu).astype(BF)
    for j in range(0, WIDTH, 512):
        at = slice(j, j + 512)
        total = mm_r(gate_cot_ref[:, :HALF], gate_ref[at, :])
        total += mm_r(gate_cot_ref[:, HALF:], gate_other_ref[at, :])
        total += mm_r(up_cot_ref[:, :HALF], up_ref[at, :])
        total += mm_r(up_cot_ref[:, HALF:], up_other_ref[at, :])
        back_ref[:, at] = total.astype(BF)
    high = share.astype(BF).astype(F32)
    lane = lax.broadcasted_iota(jnp.int32, (1, 128), 1)
    placed = jnp.where(lane < 64, high, share - high) * (own + pltpu.roll(own, 64, 1))
    back_ref[:, WIDTH:] = placed.astype(BF)


def expert_phase(rows, cot_rows, act_cot, own, pack, gate, gate_other, up, up_other, after):
    tile = lambda w, j=0: pl.BlockSpec((256, w), lambda i: (i, j))
    weight = full((WIDTH, HALF))
    return call(
        expert_kernel,
        (8,),
        [tile(WIDTH), tile(128, 12), tile(512), full((1, 128)), pack_specs()[3]]
        + [weight] * 4
        + [ANY],
        [tile(WIDE), tile(512), tile(512), tile(512)],
        [out((ROWS, WIDE), BF)] + [out((ROWS, 512), BF)] * 3,
    )(rows, cot_rows, act_cot, own, pack, gate, gate_other, up, up_other, after)


def expert_out_kernel(act_ref, down_ref, other_ref, _after_ref, out_ref):
    total = mm(act_ref[:, :HALF], down_ref[...]) + mm(act_ref[:, HALF:], other_ref[...])
    out_ref[...] = total.astype(BF)


def expert_outs(act, down, other, after):
    return call(
        expert_out_kernel,
        (8,),
        [
            pl.BlockSpec((256, 512), lambda i: (i, 0)),
            full((HALF, WIDTH)),
            full((HALF, WIDTH)),
            ANY,
        ],
        pl.BlockSpec((256, WIDTH), lambda i: (i, 0)),
        out((ROWS, WIDTH), BF),
        flops=10**11,
    )(act, down, other, after)


def expert_grad_kernel(
    rows_ref, cot_ref, act_ref, gate_cot_ref, up_cot_ref, _after_ref, gate_ref, up_ref, down_ref, gate, up, down
):
    step = pl.program_id(0)

    @pl.when(step == 0)
    def _():
        gate[...] = jnp.zeros_like(gate)
        up[...] = jnp.zeros_like(up)
        down[...] = jnp.zeros_like(down)

    gate[...] += mm_l(rows_ref[...], gate_cot_ref[...])
    up[...] += mm_l(rows_ref[...], up_cot_ref[...])
    down[...] += mm_l(act_ref[...], cot_ref[...])

    @pl.when(step == 7)
    def _():
        gate_ref[...] = gate[...].astype(gate_ref.dtype)
        up_ref[...] = up[...].astype(up_ref.dtype)
        down_ref[...] = down[...].astype(down_ref.dtype)


def expert_grads(half, dtype, rows, cot_rows, act, gate_cot, up_cot, after):
    tile = lambda w, j=0: pl.BlockSpec((256, w), lambda i: (i, j))
    shapes = [(WIDTH, HALF), (WIDTH, HALF), (HALF, WIDTH)]
    return call(
        expert_grad_kernel,
        (8,),
        [tile(WIDTH), tile(WIDTH), tile(HALF, half), tile(HALF, half), tile(HALF, half), ANY],
        [full(s) for s in shapes],
        [out(s, dtype) for s in shapes],
        [pltpu.VMEM(s, F32) for s in shapes],
        flops=10**11,
    )(rows, cot_rows, act, gate_cot, up_cot, after)


def shared_grad_kernel(ffn_in_ref, pair_ref, act_ref, cot_ref, _after_ref, out_ref):
    for j in range(0, 2 * SHARED, 512):
        at = slice(j, j + 512)
        out_ref[:, at] = mm_l(ffn_in_ref[...], pair_ref[:, at]).astype(BF)
    for j in range(0, 1024, 512):
        body = mm_l(act_ref[...], cot_ref[:, j : j + 512]).reshape(32, 16, 512)
        tail = mm_l(act_ref[...], cot_ref[:, 1024:]).reshape(32, 16, 512)
        tail = tail[:, :8] if j == 0 else tail[:, 8:]
        both = jnp.concatenate([body, tail], axis=1).reshape(768, 512)
        out_ref[:, 2 * SHARED + j : 2 * SHARED + j + 512] = both.astype(BF)


def shared_grads(ffn_in, pair_low, shared_low, out_grad, after):
    return call(
        shared_grad_kernel,
        (2,),
        [
            pl.BlockSpec((TOKENS, 768), lambda h: (0, h)),
            full((TOKENS, 2 * SHARED)),
            pl.BlockSpec((TOKENS, 512), lambda h: (0, h)),
            full((TOKENS, WIDTH)),
            ANY,
        ],
        pl.BlockSpec((768, 2 * SHARED + 1024), lambda h: (0, h)),
        out((768, 4 * SHARED + 2048), BF),
        flops=10**11,
    )(ffn_in, pair_low, shared_low, out_grad, after)


def norm_back(values, scale, gain, cot):
    weighted = cot * gain
    centre = jnp.mean(weighted * values, axis=-1, keepdims=True)
    return scale * weighted - values * (scale * scale * scale * centre)


def middle_kernel(
    rank_ref,
    back_ref,
    shared_cot_ref,
    gates_ref,
    middle_ref,
    gains_ref,
    out_grad_ref,
    small_ref,
    wo_ref,
    _after_ref,
    middle_cot_ref,
    middle_low_ref,
    attended_cot_ref,
    logit_ref,
    gain_rows_ref,
    acc,
):
    step = pl.program_id(0)

    @pl.when(step == 0)
    def _():
        acc[...] = jnp.zeros_like(acc)

    acc[...] += mm_l(one_hot(rank_ref), back_ref[...])

    @pl.when(step == 7)
    def _():
        extra = acc[:, WIDTH:]
        lane = lax.broadcasted_iota(jnp.int32, (1, 128), 1)
        shares = jnp.where(lane < 64, extra + pltpu.roll(extra, 64, 1), 0.0)
        logit = shares - gates_ref[...] * jnp.sum(shares, axis=-1, keepdims=True)
        logit_ref[...] = logit.astype(BF)
        cot = acc[:, :WIDTH] + shared_cot_ref[...] + mm_r(logit_ref[...], small_ref[...])
        middle = middle_ref[...]
        scale = root_scale(middle)
        gain_rows_ref[...] = (cot * middle * scale).astype(BF)
        total = out_grad_ref[...].astype(F32) + norm_back(middle, scale, gains_ref[1:2], cot)
        middle_cot_ref[...] = total
        middle_low_ref[...] = total.astype(BF)
        for j in range(0, WIDTH, 512):
            at = slice(j, j + 512)
            attended_cot_ref[:, at] = mm_r(middle_low_ref[...], wo_ref[at, :]).astype(BF)


def middle_back(rank, back, shared_cot, gates, middle, gains, out_grad, pack, after):
    wide = (TOKENS, WIDTH)
    shapes = [(wide, F32), (wide, BF), (wide, BF), ((TOKENS, 128), BF), (wide, BF)]
    specs = pack_specs()
    return call(
        middle_kernel,
        (8,),
        [
            pl.BlockSpec((8, TOKENS), lambda i: (i, 0)),
            pl.BlockSpec((8 * SLOTS, WIDE), lambda i: (i, 0)),
            full(wide),
            full((TOKENS, 128)),
            full(wide),
            full((8, WIDTH)),
            full(wide),
            specs[3],
            specs[1],
            ANY,
        ],
        [full(s) for s, _ in shapes],
        [out(s, d) for s, d in shapes],
        [pltpu.VMEM((TOKENS, WIDE), F32)],
    )(rank, back, shared_cot, gates, middle, gains, out_grad, pack, pack, after)


def attention_back_kernel(
    q_ref,
    k_ref,
    v_ref,
    probs_ref,
    cot_ref,
    wq_ref,
    wk_ref,
    wv_ref,
    hidden_ref,
    gains_ref,
    middle_cot_ref,
    dq_ref,
    dk_ref,
    dv_ref,
    grad_in_ref,
    gain_rows_ref,
    acc,
):
    step = pl.program_id(0)
    key, value = k_ref[...], v_ref[...]
    dk = jnp.zeros((TOKENS, HEAD), F32)
    dv = jnp.zeros((TOKENS, HEAD), F32)
    for g in range(GROUP):
        at = slice(g * HEAD, (g + 1) * HEAD)
        probs = probs_ref[g]
        cot = cot_ref[:, at]
        dprobs = mm_r(cot, value)
        dv += mm_l(probs.astype(BF), cot)
        centre = jnp.sum(probs * dprobs, axis=-1, keepdims=True)
        dscores = (probs * (dprobs - centre)).astype(BF)
        dq_ref[:, at] = (mm(dscores, key) * SCALING).astype(BF)
        dk += mm_l(dscores, q_ref[:, at])
    dk_ref[...] = (dk * SCALING).astype(BF)
    dv_ref[...] = dv.astype(BF)

    @pl.when(step == 0)
    def _():
        acc[...] = jnp.zeros_like(acc)

    for j in range(0, WIDTH, 512):
        at = slice(j, j + 512)
        acc[:, at] += (
            mm_r(dq_ref[...], wq_ref[at, :])
            + mm_r(dk_ref[...], wk_ref[at, :])
            + mm_r(dv_ref[...], wv_ref[at, :])
        )

    @pl.when(step == 3)
    def _():
        tokens = hidden_ref[...].astype(F32)
        scale = root_scale(tokens)
        cot = acc[...]
        gain_rows_ref[...] = (cot * tokens * scale).astype(BF)
        grad_in_ref[...] = middle_cot_ref[...] + norm_back(tokens, scale, gains_ref[0:1], cot)


def attention_back(q, kv, probs, attended_cot, pack, hidden, gains, middle_cot):
    wide = (TOKENS, WIDTH)
    col = lambda w, j: pl.BlockSpec((TOKENS, w), lambda h: (0, j + h))
    weight = lambda w, j: pl.BlockSpec((WIDTH, w), lambda h: (0, j + h))
    return call(
        attention_back_kernel,
        (4,),
        [
            col(GROUP * HEAD, 0),
            col(HEAD, 0),
            col(HEAD, 4),
            pl.BlockSpec((GROUP, TOKENS, TOKENS), lambda h: (h, 0, 0)),
            col(GROUP * HEAD, 0),
            weight(GROUP * HEAD, 0),
            weight(HEAD, 24),
            weight(HEAD, 28),
            full(wide),
            full((8, WIDTH)),
            full(wide),
        ],
        [col(GROUP * HEAD, 0), col(HEAD, 0), col(HEAD, 0), full(wide), full(wide)],
        [
            out(wide, BF),
            out((TOKENS, 512), BF),
            out((TOKENS, 512), BF),
            out(wide, F32),
            out(wide, BF),
        ],
        [pltpu.VMEM(wide, F32)],
    )(q, kv, kv, probs, attended_cot, pack, pack, pack, hidden, gains, middle_cot)


def dense_grad_kernel(
    attn_in_ref,
    attended_ref,
    ffn_in_ref,
    gain_one_ref,
    gain_two_ref,
    dq_ref,
    middle_ref,
    dk_ref,
    dv_ref,
    logit_ref,
    out_ref,
):
    for j in range(0, WIDTH, 512):
        at = slice(j, j + 512)
        out_ref[:, at] = mm_l(attn_in_ref[...], dq_ref[:, at]).astype(BF)
        out_ref[:, WIDTH + j : WIDTH + j + 512] = mm_l(
            attended_ref[...], middle_ref[:, at]
        ).astype(BF)
    out_ref[:, 2 * WIDTH : 2 * WIDTH + 512] = mm_l(attn_in_ref[...], dk_ref[...]).astype(BF)
    out_ref[:, 2 * WIDTH + 512 : 2 * WIDTH + 1024] = mm_l(attn_in_ref[...], dv_ref[...]).astype(BF)
    lane = lax.broadcasted_iota(jnp.int32, (TOKENS, 128), 1)
    small = mm_l(ffn_in_ref[...], logit_ref[...])
    small += mm_l(gain_one_ref[...], jnp.where(lane == 64, 1.0, 0.0).astype(BF))
    small += mm_l(gain_two_ref[...], jnp.where(lane == 65, 1.0, 0.0).astype(BF))
    out_ref[:, 2 * WIDTH + 1024 :] = small.astype(BF)


def dense_grads(attn_in, attended, ffn_in, gain_one, gain_two, dq, middle_low, dk, dv, logit):
    left = pl.BlockSpec((TOKENS, 768), lambda h: (0, h))
    wide = full((TOKENS, WIDTH))
    thin = full((TOKENS, 512))
    return call(
        dense_grad_kernel,
        (2,),
        [left] * 5 + [wide, wide, thin, thin, full((TOKENS, 128))],
        pl.BlockSpec((768, PACK), lambda h: (0, h)),
        out((768, 2 * PACK), BF),
    )(attn_in, attended, ffn_in, gain_one, gain_two, dq, middle_low, dk, dv, logit)


def body(
    hidden_in,
    out_grad,
    doc_lengths,
    expert_ids,
    gain_attn,
    w_query,
    w_key,
    w_value,
    w_out,
    gain_ffn,
    w_router,
    w_shared_gate,
    w_shared_up,
    w_shared_down,
    expert_gate,
    expert_up,
    expert_down,
):
    parts = [w_query, w_out, w_key, w_value, w_router, gain_attn[:, None], gain_ffn[:, None]]
    parts += [jnp.zeros((12, 62), BF), w_shared_gate, w_shared_up, w_shared_down.reshape(12, 1024)]
    line = lax.all_gather(jnp.concatenate(parts, axis=1), ("zh", "zl"), axis=0, tiled=False)
    dense_w = line[:, :, : PACK + 2 * SHARED].reshape(2, 24, PACK + 2 * SHARED)
    down_w = fold_down(line[:, :, PACK + 2 * SHARED :].reshape(2, 16, WIDTH))
    pack = gather_plane(jnp.concatenate([dense_w, down_w], axis=2))
    gate, up, down = expert_gate[0], expert_up[0], expert_down[0]
    gate_other, up_other, down_other = swap(gate, "zl"), swap(up, "zl"), swap(down, "zl")

    lanes = jnp.arange(128, dtype=jnp.int32)
    hits = jnp.any(expert_ids[:, :, None] == lanes, axis=1)
    hits_low = hits.astype(BF)
    place = jnp.arange(TOKENS, dtype=jnp.int32)
    earlier = (place[:, None] > place[None, :]).astype(BF)
    rank = jnp.where(hits, mm(earlier, hits_low), -1.0).T[:EXPERTS]
    own = (lanes == lax.axis_index(DP)).astype(F32)[None]

    marked = jnp.concatenate([out_grad, hits_low], axis=1)
    cot_rows = to_experts(
        tie(dispatch(rank, marked), pack, gate_other, up_other, down_other)
    )

    attn_in, q, kv, probs, attended, middle, ffn_in, gates, gains = forward(
        hidden_in, doc_lengths, hits_low, pack
    )
    send_rows = dispatch(rank, ffn_in)
    rows = to_experts(send_rows)
    pair_w = pack[:, PACK : PACK + 2 * SHARED]
    down_w = unfold_down(pack[:, PACK + 2 * SHARED :].reshape(64, 24, 1024)).reshape(SHARED, WIDTH)

    pair = mm(ffn_in, pair_w)
    shared_gate, shared_upper = pair[:, :SHARED], pair[:, SHARED:]
    sig = jax.nn.sigmoid(shared_gate)
    silu = shared_gate * sig
    shared_low = (silu * shared_upper).astype(BF)
    shared_sum = middle + mm(shared_low, down_w)
    shared_cot = mm_r(out_grad, down_w)
    slope = sig * (1.0 + shared_gate * (1.0 - sig))
    pair_low = jnp.concatenate(
        [(shared_cot * shared_upper * slope).astype(BF), (shared_cot * silu).astype(BF)], axis=1
    )
    shared_cot = mm_r(pair_low, pair_w)

    act_cot = act_cots(cot_rows, down, down_other)
    back, act, gate_cot, up_cot = expert_phase(
        rows, cot_rows, act_cot, own, pack, gate, gate_other, up, up_other, shared_cot
    )
    shared_grad = shared_grads(ffn_in, pair_low, shared_low, out_grad, act)
    kept = expert_grads(0, F32, rows, cot_rows, act, gate_cot, up_cot, shared_grad)
    shared_grad = scatter_plane(shared_grad)
    result_rows = expert_outs(act, down, down_other, kept[0])
    back = to_experts(back)
    result = to_experts(result_rows)

    middle_cot, middle_low, attended_cot, logit, gain_two_rows = middle_back(
        rank, back, shared_cot, gates, middle, gains, out_grad, pack, result_rows
    )
    dq, dk, dv, grad_in, gain_one_rows = attention_back(
        q, kv, probs, attended_cot, pack, hidden_in, gains, middle_cot
    )
    dense_grad = dense_grads(
        attn_in, attended, ffn_in, gain_one_rows, gain_two_rows, dq, middle_low, dk, dv, logit
    )
    dense = sum_zh(scatter_plane(dense_grad))
    dense = sum_zl(dense[:12], dense[12:])
    shared_grad = sum_zh(shared_grad)
    pair_grad = shared_grad[:, : 2 * SHARED]
    down_grad = unfold_down(shared_grad[None, :, 2 * SHARED :])[0]
    pair_grad = sum_zl(pair_grad[:12], pair_grad[12:])
    down_grad = sum_zl(down_grad[:8], down_grad[8:])
    block_out = add_results(rank, result, shared_sum)
    sent = expert_grads(1, BF, rows, cot_rows, act, gate_cot, up_cot, dense_grad)
    expert = [(k + swap(s, "zl").astype(F32))[None] for k, s in zip(kept, sent)]
    at = 2 * WIDTH
    return (
        block_out,
        grad_in,
        dense[:, at + 1088],
        dense[:, :WIDTH],
        dense[:, at : at + 512],
        dense[:, at + 512 : at + 1024],
        dense[:, WIDTH:at],
        dense[:, at + 1089],
        dense[:, at + 1024 : at + 1088],
        pair_grad[:, :SHARED],
        pair_grad[:, SHARED:],
        down_grad,
        expert[0],
        expert[1],
        expert[2],
    )


def solution(mesh):
    fine = Mesh(mesh.devices.reshape(2, 4, 4, 2, 2), AXES)
    rows, vector = P(AXES, None), P(AXES)
    banks = (P(DP, None, "zl"), P(DP, None, "zl"), P(DP, "zl", None))
    return jax.shard_map(
        body,
        mesh=fine,
        in_specs=(rows, rows, rows, rows, vector, rows, rows, rows, rows, vector)
        + (rows, rows, rows, rows)
        + banks,
        out_specs=(rows, rows, vector, rows, rows, rows, rows, vector)
        + (rows, rows, rows, rows)
        + banks,
        check_vma=False,
    )
```

```python
import jax
import jax.numpy as jnp
from jax import lax
from jax.experimental import pallas as pl
from jax.experimental.pallas import tpu as pltpu
from jax.sharding import Mesh, PartitionSpec as P

GROUP = 3
HEAD = 128
EXPERTS = 64
SLOTS = 32
TOKENS = 256
WIDTH = 1536
SHARED = 1024
HALF = 256
ROWS = EXPERTS * SLOTS
WIDE = WIDTH + 128
PACK = 2 * WIDTH + 1024 + 128

EPSILON = 1e-06
NEGATIVE = -1e30
SCALING = HEAD ** (-0.5)
BF = jnp.bfloat16
F32 = jnp.float32

AXES = ("zh", "x", "y", "c", "zl")
DP = ("zh", "x", "y", "c")
PLANE = ("x", "y", "c")
ANY = pl.BlockSpec(memory_space=pl.ANY)


def mm(a, b):
    return jnp.dot(a, b, preferred_element_type=F32)


def mm_l(a, b):
    return lax.dot_general(a, b, (((0,), (0,)), ((), ())), preferred_element_type=F32)


def mm_r(a, b):
    return lax.dot_general(a, b, (((1,), (1,)), ((), ())), preferred_element_type=F32)


def swap(x, axis):
    return lax.ppermute(x, axis, [(0, 1), (1, 0)])


def out(shape, dtype):
    return jax.ShapeDtypeStruct(shape, dtype)


def full(shape):
    return pl.BlockSpec(shape, lambda *i: (0,) * len(shape))


def call(kernel, grid, in_specs, out_specs, out_shape, scratch=(), flops=0, aliases=None):
    return pl.pallas_call(
        kernel,
        grid=grid,
        in_specs=in_specs,
        out_specs=out_specs,
        out_shape=out_shape,
        scratch_shapes=list(scratch),
        input_output_aliases=aliases or {},
        compiler_params=pltpu.CompilerParams(vmem_limit_bytes=56 * 1024 * 1024),
        cost_estimate=pl.CostEstimate(flops=flops, bytes_accessed=0, transcendentals=0),
    )


def fetch(source, target, sem):
    copy = pltpu.make_async_copy(source, target, sem)
    copy.start()
    return copy


def tie_kernel(*refs):
    pass


def tie(x, *after):
    return pl.pallas_call(
        tie_kernel,
        in_specs=[ANY] * (1 + len(after)),
        out_specs=ANY,
        out_shape=out(x.shape, x.dtype),
        input_output_aliases={0: 0},
    )(x, *after)


def gather_plane(pairs):
    _, rows, width = pairs.shape
    return lax.all_gather(pairs, PLANE, axis=1, tiled=True).reshape(64 * rows, width)


def scatter_plane(grads):
    return lax.psum_scatter(grads, PLANE, scatter_dimension=0, tiled=True)


def sum_zh(plane):
    width = plane.shape[1] // 2
    zh = lax.axis_index("zh")
    low, high = plane[:, :width], plane[:, width:]
    keep = jnp.where(zh == 0, low, high)
    give = jnp.where(zh == 0, high, low)
    return keep.astype(F32) + swap(give, "zh").astype(F32)


def sum_zl(mine, other):
    zl = lax.axis_index("zl")
    keep = jnp.where(zl == 0, mine, other)
    give = jnp.where(zl == 0, other, mine).astype(BF)
    return keep + swap(give, "zl").astype(F32)


def fold_down(rows):
    tail = [rows[:, :8, 1024:], rows[:, 8:, 1024:]]
    return jnp.concatenate([rows[:, :, :1024], jnp.concatenate(tail, axis=2)], axis=1)


def unfold_down(rows):
    tail = jnp.concatenate([rows[:, 16:, :512], rows[:, 16:, 512:]], axis=1)
    return jnp.concatenate([rows[:, :16], tail], axis=2)


def deal_kernel(rank_ref, cot_ref, hits_ref, deal_ref, turned_ref, out_ref):
    rank = rank_ref[...]
    slot = lax.broadcasted_iota(jnp.int32, (8, SLOTS, TOKENS), 1).astype(F32)
    hit = jnp.where(rank[:, None, :] == slot, 1.0, 0.0).reshape(8 * SLOTS, TOKENS)
    deal = hit.astype(BF)
    deal_ref[...] = deal
    turned_ref[...] = jnp.transpose(hit).astype(BF)
    out_ref[:, :WIDTH] = mm(deal, cot_ref[...]).astype(BF)
    out_ref[:, WIDTH:] = mm(deal, hits_ref[...]).astype(BF)


def deal_out(rank, out_grad, hits):
    return call(
        deal_kernel,
        (8,),
        [
            pl.BlockSpec((8, TOKENS), lambda i: (i, 0)),
            full((TOKENS, WIDTH)),
            full((TOKENS, 128)),
        ],
        [
            pl.BlockSpec((256, TOKENS), lambda i: (i, 0)),
            pl.BlockSpec((TOKENS, 256), lambda i: (0, i)),
            pl.BlockSpec((256, WIDE), lambda i: (i, 0)),
        ],
        [out((ROWS, TOKENS), BF), out((TOKENS, ROWS), BF), out((ROWS, WIDE), BF)],
    )(rank, out_grad, hits)


def dispatch_kernel(deal_ref, rows_ref, out_ref):
    out_ref[...] = mm(deal_ref[...], rows_ref[...]).astype(BF)


def dispatch(deal, rows):
    return call(
        dispatch_kernel,
        (6,),
        [full((ROWS, TOKENS)), pl.BlockSpec((TOKENS, 256), lambda j: (0, j))],
        pl.BlockSpec((ROWS, 256), lambda j: (0, j)),
        out((ROWS, WIDTH), BF),
    )(deal, rows)


def to_experts(rows):
    return lax.all_to_all(
        rows.reshape(EXPERTS, SLOTS, -1), DP, split_axis=0, concat_axis=0, tiled=True
    ).reshape(ROWS, -1)


def result_kernel(turned_ref, rows_ref, base_ref, out_ref, acc):
    step = pl.program_id(0)

    @pl.when(step == 0)
    def _():
        acc[...] = base_ref[...]

    acc[...] += mm(turned_ref[...], rows_ref[...])

    @pl.when(step == 3)
    def _():
        out_ref[...] = acc[...].astype(BF)


def add_results(turned, rows, base):
    return call(
        result_kernel,
        (4,),
        [
            pl.BlockSpec((TOKENS, 512), lambda i: (0, i)),
            pl.BlockSpec((512, WIDTH), lambda i: (i, 0)),
            full((TOKENS, WIDTH)),
        ],
        full((TOKENS, WIDTH)),
        out((TOKENS, WIDTH), BF),
        [pltpu.VMEM((TOKENS, WIDTH), F32)],
        flops=10**13,
    )(turned, rows, base)


def root_scale(values):
    return lax.rsqrt(jnp.mean(values * values, axis=-1, keepdims=True) + EPSILON)


def forward_kernel(
    hidden_ref,
    docs_ref,
    hits_ref,
    pack_ref,
    attn_in_ref,
    q_ref,
    kv_ref,
    probs_ref,
    attended_ref,
    middle_ref,
    ffn_in_ref,
    gates_ref,
    gains_ref,
    small_ref,
    wq_ref,
    wkv_ref,
    wo_ref,
    sems,
):
    copies = [
        fetch(pack_ref.at[:, at : at + ref.shape[1]], ref, sems.at[i])
        for i, (at, ref) in enumerate(
            [(2 * WIDTH + 1024, small_ref), (0, wq_ref), (2 * WIDTH, wkv_ref), (WIDTH, wo_ref)]
        )
    ]
    copies[0].wait()
    gains = jnp.transpose(small_ref[...].astype(F32))
    gains_ref[...] = gains[64:72]
    gain_one, gain_two = gains[64:65], gains[65:66]
    tokens = hidden_ref[...].astype(F32)
    attn_in_ref[...] = (tokens * root_scale(tokens) * gain_one).astype(BF)
    copies[1].wait()
    for j in range(0, WIDTH, 512):
        q_ref[:, j : j + 512] = mm(attn_in_ref[...], wq_ref[:, j : j + 512]).astype(BF)
    copies[2].wait()
    for j in range(0, 1024, 512):
        kv_ref[:, j : j + 512] = mm(attn_in_ref[...], wkv_ref[:, j : j + 512]).astype(BF)
    first = docs_ref[0, 0]
    second = first + docs_ref[0, 1]
    third = second + docs_ref[0, 2]
    row = lax.broadcasted_iota(jnp.int32, (TOKENS, TOKENS), 0)
    col = lax.broadcasted_iota(jnp.int32, (TOKENS, TOKENS), 1)

    def segment(place):
        return (
            (place >= first).astype(jnp.int32)
            + (place >= second).astype(jnp.int32)
            + (place >= third).astype(jnp.int32)
        )

    visible = (segment(row) == segment(col)) & (row >= col)
    for kv_head in range(4):
        key = kv_ref[:, kv_head * HEAD : (kv_head + 1) * HEAD]
        value = kv_ref[:, 512 + kv_head * HEAD : 512 + (kv_head + 1) * HEAD]
        for head in range(kv_head * GROUP, (kv_head + 1) * GROUP):
            at = slice(head * HEAD, (head + 1) * HEAD)
            scores = jnp.where(visible, mm_r(q_ref[:, at], key) * SCALING, NEGATIVE)
            exponent = jnp.exp(scores - jnp.max(scores, axis=-1, keepdims=True))
            probs = exponent / jnp.sum(exponent, axis=-1, keepdims=True)
            probs_ref[head] = probs
            attended_ref[:, at] = mm(probs.astype(BF), value).astype(BF)
    copies[3].wait()
    for j in range(0, WIDTH, 512):
        at = slice(j, j + 512)
        middle_ref[:, at] = hidden_ref[:, at].astype(F32) + mm(
            attended_ref[...], wo_ref[:, at]
        )
    middle = middle_ref[...]
    ffn_in_ref[...] = (middle * root_scale(middle) * gain_two).astype(BF)
    logits = mm(ffn_in_ref[...], small_ref[...])
    hits = hits_ref[...] > 0
    top = jnp.max(jnp.where(hits, logits, NEGATIVE), axis=-1, keepdims=True)
    weight = jnp.where(hits, jnp.exp(jnp.where(hits, logits - top, 0.0)), 0.0)
    gates_ref[...] = weight / jnp.sum(weight, axis=-1, keepdims=True)


def forward(hidden, docs, hits, pack):
    wide = (TOKENS, WIDTH)
    shapes = [
        (wide, BF),
        (wide, BF),
        ((TOKENS, 1024), BF),
        ((12, TOKENS, TOKENS), F32),
        (wide, BF),
        (wide, F32),
        (wide, BF),
        ((TOKENS, 128), F32),
        ((8, WIDTH), F32),
    ]
    return call(
        forward_kernel,
        (1,),
        [full(wide), pl.BlockSpec(memory_space=pltpu.SMEM), full((TOKENS, 128)), ANY],
        [full(s) for s, _ in shapes],
        [out(s, d) for s, d in shapes],
        [pltpu.VMEM((WIDTH, w), BF) for w in (128, WIDTH, 1024, WIDTH)]
        + [pltpu.SemaphoreType.DMA((4,))],
    )(hidden, docs, hits, pack)


def act_cot_kernel(cot_ref, down_ref, other_ref, _after_ref, out_ref):
    out_ref[:, :HALF] = mm_r(cot_ref[...], down_ref[...])
    out_ref[:, HALF:] = mm_r(cot_ref[...], other_ref[...])


def act_cots(cot_rows, down, other, after):
    return call(
        act_cot_kernel,
        (8,),
        [
            pl.BlockSpec((256, WIDTH), lambda i: (i, 0)),
            full((HALF, WIDTH)),
            full((HALF, WIDTH)),
            ANY,
        ],
        pl.BlockSpec((256, 2 * HALF), lambda i: (i, 0)),
        out((ROWS, 2 * HALF), F32),
    )(cot_rows, down, other, after)


def expert_kernel(
    rows_ref,
    marks_ref,
    act_cot_ref,
    own_ref,
    small_ref,
    gate_ref,
    gate_other_ref,
    up_ref,
    up_other_ref,
    _after_ref,
    back_ref,
    act_ref,
    gate_cot_ref,
    up_cot_ref,
):
    rows = rows_ref[...]
    marks = marks_ref[...] > 0
    logits = mm(rows, small_ref[...])
    top = jnp.max(jnp.where(marks, logits, NEGATIVE), axis=-1, keepdims=True)
    weight = jnp.where(marks, jnp.exp(jnp.where(marks, logits - top, 0.0)), 0.0)
    own = own_ref[...]
    total = jnp.sum(weight, axis=-1, keepdims=True)
    mine = jnp.sum(weight * own, axis=-1, keepdims=True)
    route_gate = mine / jnp.where(total > 0, total, 1.0)
    share = jnp.zeros((256, 1), F32)
    for half, gate_w, up_w in ((0, gate_ref, up_ref), (1, gate_other_ref, up_other_ref)):
        at = slice(half * HALF, (half + 1) * HALF)
        gate = mm(rows, gate_w[...])
        upper = mm(rows, up_w[...])
        sig = 1.0 / (1.0 + jnp.exp(-gate))
        silu = gate * sig
        act_cot = act_cot_ref[:, at]
        act = route_gate * silu * upper
        act_ref[:, at] = act.astype(BF)
        share += jnp.sum(act_cot * act, axis=-1, keepdims=True)
        scaled = route_gate * act_cot
        gate_cot_ref[:, at] = (scaled * upper * (sig * (1.0 + gate * (1.0 - sig)))).astype(BF)
        up_cot_ref[:, at] = (scaled * silu).astype(BF)
    for j in range(0, WIDTH, 512):
        at = slice(j, j + 512)
        total = mm_r(gate_cot_ref[:, :HALF], gate_ref[at, :])
        total += mm_r(gate_cot_ref[:, HALF:], gate_other_ref[at, :])
        total += mm_r(up_cot_ref[:, :HALF], up_ref[at, :])
        total += mm_r(up_cot_ref[:, HALF:], up_other_ref[at, :])
        back_ref[:, at] = total.astype(BF)
    high = share.astype(BF).astype(F32)
    lane = lax.broadcasted_iota(jnp.int32, (1, 128), 1)
    placed = jnp.where(lane < 64, high, share - high) * (own + pltpu.roll(own, 64, 1))
    back_ref[:, WIDTH:] = placed.astype(BF)


def expert_phase(rows, cot_rows, act_cot, own, pack, weights, after):
    tile = lambda w, j=0: pl.BlockSpec((256, w), lambda i: (i, j))
    small = pl.BlockSpec((WIDTH, 128), lambda i: (0, 32))
    return call(
        expert_kernel,
        (8,),
        [tile(WIDTH), tile(128, 12), tile(512), full((1, 128)), small]
        + [full(w.shape) for w in weights]
        + [ANY],
        [tile(WIDE), tile(512), tile(512), tile(512)],
        [out((ROWS, WIDE), BF)] + [out((ROWS, 512), BF)] * 3,
    )(rows, cot_rows, act_cot, own, pack, *weights, after)


def expert_out_kernel(act_ref, down_ref, other_ref, _after_ref, out_ref):
    total = mm(act_ref[:, :HALF], down_ref[...]) + mm(act_ref[:, HALF:], other_ref[...])
    out_ref[...] = total.astype(BF)


def expert_outs(act, down, other, after):
    return call(
        expert_out_kernel,
        (8,),
        [
            pl.BlockSpec((256, 512), lambda i: (i, 0)),
            full((HALF, WIDTH)),
            full((HALF, WIDTH)),
            ANY,
        ],
        pl.BlockSpec((256, WIDTH), lambda i: (i, 0)),
        out((ROWS, WIDTH), BF),
    )(act, down, other, after)


def expert_grad_kernel(
    rows_ref, cot_ref, act_ref, gate_cot_ref, up_cot_ref, _after_ref, gate_ref, up_ref, down_ref, gate, up, down
):
    step = pl.program_id(0)

    @pl.when(step == 0)
    def _():
        gate[...] = jnp.zeros_like(gate)
        up[...] = jnp.zeros_like(up)
        down[...] = jnp.zeros_like(down)

    gate[...] += mm_l(rows_ref[...], gate_cot_ref[...])
    up[...] += mm_l(rows_ref[...], up_cot_ref[...])
    down[...] += mm_l(act_ref[...], cot_ref[...])

    @pl.when(step == 7)
    def _():
        gate_ref[...] = gate[...].astype(gate_ref.dtype)
        up_ref[...] = up[...].astype(up_ref.dtype)
        down_ref[...] = down[...].astype(down_ref.dtype)


def expert_grads(half, dtype, rows, cot_rows, act, gate_cot, up_cot, after):
    tile = lambda w, j=0: pl.BlockSpec((256, w), lambda i: (i, j))
    shapes = [(WIDTH, HALF), (WIDTH, HALF), (HALF, WIDTH)]
    return call(
        expert_grad_kernel,
        (8,),
        [tile(WIDTH), tile(WIDTH), tile(HALF, half), tile(HALF, half), tile(HALF, half), ANY],
        [full(s) for s in shapes],
        [out(s, dtype) for s in shapes],
        [pltpu.VMEM(s, F32) for s in shapes],
    )(rows, cot_rows, act, gate_cot, up_cot, after)


def shared_kernel(
    ffn_in_ref,
    out_grad_ref,
    middle_ref,
    second_ref,
    _after_ref,
    act_ref,
    pair_cot_ref,
    sum_ref,
    cot_ref,
    pair_w_ref,
    fold_ref,
    down_ref,
    tail_ref,
    sems,
):
    pair_copy = fetch(second_ref.at[:, : 2 * SHARED], pair_w_ref, sems.at[0])
    fold_copy = fetch(second_ref.at[:, 2 * SHARED :], fold_ref, sems.at[1])
    fold_copy.wait()
    for j in range(2):
        at = slice(j * 512, (j + 1) * 512)
        rows = fold_ref[:, at].astype(F32).reshape(64, 24, 512)
        down_ref[:, at] = rows[:, :16].reshape(SHARED, 512).astype(BF)
        tail_ref[:, j * 8 : (j + 1) * 8] = rows[:, 16:]
    down_ref[:, 1024:] = tail_ref[...].reshape(SHARED, 512).astype(BF)
    pair_copy.wait()
    for j in range(0, SHARED, 256):
        at = slice(j, j + 256)
        up_at = slice(SHARED + j, SHARED + j + 256)
        gate = mm(ffn_in_ref[...], pair_w_ref[:, at])
        upper = mm(ffn_in_ref[...], pair_w_ref[:, up_at])
        sig = 1.0 / (1.0 + jnp.exp(-gate))
        silu = gate * sig
        act_ref[:, at] = (silu * upper).astype(BF)
        cot = mm_r(out_grad_ref[...], down_ref[at, :])
        pair_cot_ref[:, at] = (cot * upper * (sig * (1.0 + gate * (1.0 - sig)))).astype(BF)
        pair_cot_ref[:, up_at] = (cot * silu).astype(BF)
    for j in range(0, WIDTH, 512):
        at = slice(j, j + 512)
        sum_ref[:, at] = middle_ref[:, at] + mm(act_ref[...], down_ref[:, at])
        cot_ref[:, at] = mm_r(pair_cot_ref[...], pair_w_ref[at, :])


def shared_phase(ffn_in, out_grad, middle, second, after):
    wide = (TOKENS, WIDTH)
    shapes = [((TOKENS, SHARED), BF), ((TOKENS, 2 * SHARED), BF), (wide, F32), (wide, F32)]
    return call(
        shared_kernel,
        (1,),
        [full(wide), full(wide), full(wide), ANY, ANY],
        [full(s) for s, _ in shapes],
        [out(s, d) for s, d in shapes],
        [
            pltpu.VMEM((WIDTH, 2 * SHARED), BF),
            pltpu.VMEM((WIDTH, 1024), BF),
            pltpu.VMEM((SHARED, WIDTH), BF),
            pltpu.VMEM((64, 16, 512), F32),
            pltpu.SemaphoreType.DMA((2,)),
        ],
    )(ffn_in, out_grad, middle, second, after)


def shared_grad_kernel(ffn_in_ref, pair_ref, act_ref, cot_ref, _after_ref, out_ref):
    for j in range(0, 2 * SHARED, 512):
        at = slice(j, j + 512)
        out_ref[:, at] = mm_l(ffn_in_ref[...], pair_ref[:, at]).astype(BF)
    for j in range(0, 1024, 512):
        body = mm_l(act_ref[...], cot_ref[:, j : j + 512]).reshape(32, 16, 512)
        tail = mm_l(act_ref[...], cot_ref[:, 1024:]).reshape(32, 16, 512)
        tail = tail[:, :8] if j == 0 else tail[:, 8:]
        both = jnp.concatenate([body, tail], axis=1).reshape(768, 512)
        out_ref[:, 2 * SHARED + j : 2 * SHARED + j + 512] = both.astype(BF)


def shared_grads(ffn_in, pair_low, shared_low, out_grad, after):
    return call(
        shared_grad_kernel,
        (2,),
        [
            pl.BlockSpec((TOKENS, 768), lambda h: (0, h)),
            full((TOKENS, 2 * SHARED)),
            pl.BlockSpec((TOKENS, 512), lambda h: (0, h)),
            full((TOKENS, WIDTH)),
            ANY,
        ],
        pl.BlockSpec((768, 2 * SHARED + 1024), lambda h: (0, h)),
        out((768, 4 * SHARED + 2048), BF),
    )(ffn_in, pair_low, shared_low, out_grad, after)


def norm_back(values, scale, gain, cot):
    weighted = cot * gain
    centre = jnp.mean(weighted * values, axis=-1, keepdims=True)
    return scale * weighted - values * (scale * scale * scale * centre)


def backward_kernel(*refs):
    n_in, n_out = 13, 8
    sources, outs, scratch = refs[:n_in], refs[n_in : n_in + n_out], refs[n_in + n_out :]
    back_hbm, pack_hbm = sources[:2]
    middle_low_ref, dq_ref, dkv_ref, grad_in_ref, logit_ref, one_ref, two_ref, cot_ref = outs
    back_ref, wo_ref, wq_ref, wkv_ref, small_ref, acc, sems = scratch[:7]
    held = scratch[7:]
    loads = [(back_hbm.at[:1024], back_ref.at[:1024]), (back_hbm.at[1024:], back_ref.at[1024:])]
    loads += [(a, b) for a, b in zip(sources[2:7], held[:5])]
    loads += [
        (pack_hbm.at[:, 2 * WIDTH + 1024 : PACK], small_ref),
        (pack_hbm.at[:, WIDTH : 2 * WIDTH], wo_ref),
    ]
    loads += [(a, b) for a, b in zip(sources[7:12], held[5:])]
    loads += [
        (pack_hbm.at[:, :WIDTH], wq_ref),
        (pack_hbm.at[:, 2 * WIDTH : 2 * WIDTH + 1024], wkv_ref),
    ]
    turned_ref, shared_ref, gates_ref, middle_ref, gains_ref = held[:5]
    out_grad_ref, q_ref, kv_ref, probs_ref, hidden_ref = held[5:]
    loads = [loads[2], loads[0], loads[1]] + loads[3:]
    copies = [fetch(a, b, sems.at[i]) for i, (a, b) in enumerate(loads)]
    for i in (0, 1):
        copies[i].wait()
    acc[...] = mm(turned_ref[:, :1024], back_ref[:1024])
    copies[2].wait()
    acc[...] += mm(turned_ref[:, 1024:], back_ref[1024:])
    for i in range(3, 10):
        copies[i].wait()
    extra = acc[:, WIDTH:]
    lane = lax.broadcasted_iota(jnp.int32, (1, 128), 1)
    shares = jnp.where(lane < 64, extra + pltpu.roll(extra, 64, 1), 0.0)
    logit = shares - gates_ref[...] * jnp.sum(shares, axis=-1, keepdims=True)
    logit_ref[...] = logit.astype(BF)
    cot = acc[:, :WIDTH] + shared_ref[...] + mm_r(logit_ref[...], small_ref[...])
    middle = middle_ref[...]
    scale = root_scale(middle)
    two_ref[...] = (cot * middle * scale).astype(BF)
    total = out_grad_ref[...].astype(F32) + norm_back(middle, scale, gains_ref[1:2], cot)
    grad_in_ref[...] = total
    middle_low_ref[...] = total.astype(BF)
    for j in range(0, WIDTH, 512):
        at = slice(j, j + 512)
        cot_ref[:, at] = mm_r(middle_low_ref[...], wo_ref[at, :]).astype(BF)
    for i in range(10, 14):
        copies[i].wait()
    for kv_head in range(4):
        key_at = slice(kv_head * HEAD, (kv_head + 1) * HEAD)
        value_at = slice(512 + kv_head * HEAD, 512 + (kv_head + 1) * HEAD)
        key, value = kv_ref[:, key_at], kv_ref[:, value_at]
        dk = jnp.zeros((TOKENS, HEAD), F32)
        dv = jnp.zeros((TOKENS, HEAD), F32)
        for head in range(kv_head * GROUP, (kv_head + 1) * GROUP):
            at = slice(head * HEAD, (head + 1) * HEAD)
            probs = probs_ref[head]
            head_cot = cot_ref[:, at]
            dprobs = mm_r(head_cot, value)
            dv += mm_l(probs.astype(BF), head_cot)
            centre = jnp.sum(probs * dprobs, axis=-1, keepdims=True)
            dscores = (probs * (dprobs - centre)).astype(BF)
            dq_ref[:, at] = (mm(dscores, key) * SCALING).astype(BF)
            dk += mm_l(dscores, q_ref[:, at])
        dkv_ref[:, key_at] = (dk * SCALING).astype(BF)
        dkv_ref[:, value_at] = dv.astype(BF)
    for i in range(14, 16):
        copies[i].wait()
    for j in range(0, WIDTH, 512):
        at = slice(j, j + 512)
        acc[:, at] = mm_r(dq_ref[...], wq_ref[at, :]) + mm_r(dkv_ref[...], wkv_ref[at, :])
    tokens = hidden_ref[...].astype(F32)
    scale = root_scale(tokens)
    cot = acc[:, :WIDTH]
    one_ref[...] = (cot * tokens * scale).astype(BF)
    grad_in_ref[...] += norm_back(tokens, scale, gains_ref[0:1], cot)


def backward(back, pack, turned, shared_cot, gates, middle, gains, out_grad, q, kv, probs, hidden, after):
    wide = (TOKENS, WIDTH)
    shapes = [
        (wide, BF),
        (wide, BF),
        ((TOKENS, 1024), BF),
        (wide, F32),
        ((TOKENS, 128), BF),
        (wide, BF),
        (wide, BF),
        (wide, BF),
    ]
    held = [turned, shared_cot, gates, middle, gains, out_grad, q, kv, probs, hidden]
    scratch = [
        pltpu.VMEM((ROWS, WIDE), BF),
        pltpu.VMEM((WIDTH, WIDTH), BF),
        pltpu.VMEM((WIDTH, WIDTH), BF),
        pltpu.VMEM((WIDTH, 1024), BF),
        pltpu.VMEM((WIDTH, 128), BF),
        pltpu.VMEM((TOKENS, WIDE), F32),
        pltpu.SemaphoreType.DMA((16,)),
    ] + [pltpu.VMEM(a.shape, a.dtype) for a in held]
    return call(
        backward_kernel,
        (1,),
        [ANY] * 13,
        [full(s) for s, _ in shapes],
        [out(s, d) for s, d in shapes],
        scratch,
    )(back, pack, *held, after)


def dense_grad_kernel(
    attn_in_ref,
    attended_ref,
    ffn_in_ref,
    gain_one_ref,
    gain_two_ref,
    dq_ref,
    middle_ref,
    dkv_ref,
    logit_ref,
    out_ref,
    held,
    sems,
):
    copies = []

    def send(at, width):
        where = slice(at, at + width)
        copies.append(fetch(held.at[:, where], out_ref.at[:, where], sems.at[len(copies)]))

    for half in range(2):
        rows = slice(half * 768, (half + 1) * 768)
        base = half * PACK
        attended = attended_ref[:, rows]
        for j in range(0, WIDTH, 512):
            at = base + WIDTH + j
            held[:, at : at + 512] = mm_l(attended, middle_ref[:, j : j + 512]).astype(BF)
        send(base + WIDTH, WIDTH)
        attn_in = attn_in_ref[:, rows]
        for j in range(0, WIDTH, 512):
            at = base + j
            held[:, at : at + 512] = mm_l(attn_in, dq_ref[:, j : j + 512]).astype(BF)
        send(base, WIDTH)
        for j in range(0, 1024, 512):
            at = base + 2 * WIDTH + j
            held[:, at : at + 512] = mm_l(attn_in, dkv_ref[:, j : j + 512]).astype(BF)
        lane = lax.broadcasted_iota(jnp.int32, (TOKENS, 128), 1)
        small = mm_l(ffn_in_ref[:, rows], logit_ref[...])
        small += mm_l(gain_one_ref[:, rows], jnp.where(lane == 64, 1.0, 0.0).astype(BF))
        small += mm_l(gain_two_ref[:, rows], jnp.where(lane == 65, 1.0, 0.0).astype(BF))
        held[:, base + 2 * WIDTH + 1024 : base + PACK] = small.astype(BF)
        send(base + 2 * WIDTH, 1024 + 128)
    for copy in copies:
        copy.wait()


def dense_grads(attn_in, attended, ffn_in, gain_one, gain_two, dq, middle_low, dkv, logit):
    ins = [attn_in, attended, ffn_in, gain_one, gain_two, dq, middle_low, dkv, logit]
    return call(
        dense_grad_kernel,
        (1,),
        [full(a.shape) for a in ins],
        ANY,
        out((768, 2 * PACK), BF),
        [pltpu.VMEM((768, 2 * PACK), BF), pltpu.SemaphoreType.DMA((6,))],
        flops=10**13,
    )(*ins)


def body(
    hidden_in,
    out_grad,
    doc_lengths,
    expert_ids,
    gain_attn,
    w_query,
    w_key,
    w_value,
    w_out,
    gain_ffn,
    w_router,
    w_shared_gate,
    w_shared_up,
    w_shared_down,
    expert_gate,
    expert_up,
    expert_down,
):
    parts = [w_query, w_out, w_key, w_value, w_router, gain_attn[:, None], gain_ffn[:, None]]
    parts += [jnp.zeros((12, 62), BF), w_shared_gate, w_shared_up, w_shared_down.reshape(12, 1024)]
    line = lax.all_gather(jnp.concatenate(parts, axis=1), ("zh", "zl"), axis=0, tiled=False)
    pack = gather_plane(line[:, :, :PACK].reshape(2, 24, PACK))
    pair_w = line[:, :, PACK : PACK + 2 * SHARED].reshape(2, 24, 2 * SHARED)
    down_w = fold_down(line[:, :, PACK + 2 * SHARED :].reshape(2, 16, WIDTH))
    second = gather_plane(jnp.concatenate([pair_w, down_w], axis=2))
    gate, up, down = expert_gate[0], expert_up[0], expert_down[0]
    gate_other, up_other, down_other = swap(gate, "zl"), swap(up, "zl"), swap(down, "zl")

    lanes = jnp.arange(128, dtype=jnp.int32)
    hits = jnp.any(expert_ids[:, :, None] == lanes, axis=1)
    hits_low = hits.astype(BF)
    place = jnp.arange(TOKENS, dtype=jnp.int32)
    earlier = (place[:, None] > place[None, :]).astype(BF)
    rank = jnp.where(hits, mm(earlier, hits_low), -1.0).T[:EXPERTS]
    own = (lanes == lax.axis_index(DP)).astype(F32)[None]

    deal, turned, send_cot = deal_out(rank, out_grad, hits_low)
    cot_rows = to_experts(tie(send_cot, line, gate_other, up_other))

    attn_in, q, kv, probs, attended, middle, ffn_in, gates, gains = forward(
        hidden_in, doc_lengths, hits_low, pack
    )
    send_rows = tie(dispatch(deal, ffn_in), down_other)
    rows = to_experts(send_rows)

    act_cot = act_cots(cot_rows, down, down_other, send_rows)
    weights = (gate, gate_other, up, up_other)
    back, act, gate_cot, up_cot = expert_phase(
        rows, cot_rows, act_cot, own, pack, weights, send_rows
    )
    shared_low, pair_low, shared_sum, shared_cot = shared_phase(
        ffn_in, out_grad, middle, second, act
    )
    shared_grad = shared_grads(ffn_in, pair_low, shared_low, out_grad, shared_cot)

    kept = expert_grads(0, F32, rows, cot_rows, act, gate_cot, up_cot, shared_grad)
    shared_grad = scatter_plane(shared_grad)
    sent = expert_grads(1, BF, rows, cot_rows, act, gate_cot, up_cot, kept[0])
    result = expert_outs(act, down, down_other, sent[0])
    back = to_experts(back)

    middle_low, dq, dkv, grad_in, logit, one_rows, two_rows, _ = backward(
        back, pack, turned, shared_cot, gates, middle, gains, out_grad, q, kv, probs, hidden_in, result
    )
    result = to_experts(result)
    dense_grad = dense_grads(
        attn_in, attended, ffn_in, one_rows, two_rows, dq, middle_low, dkv, logit
    )
    dense = sum_zh(scatter_plane(dense_grad))
    dense = sum_zl(dense[:12], dense[12:])
    shared_grad = sum_zh(shared_grad)
    pair_grad = shared_grad[:, : 2 * SHARED]
    down_grad = unfold_down(shared_grad[None, :, 2 * SHARED :])[0]
    pair_grad = sum_zl(pair_grad[:12], pair_grad[12:])
    down_grad = sum_zl(down_grad[:8], down_grad[8:])
    block_out = add_results(turned, result, shared_sum)
    sent = [tie(x, dense_grad) for x in sent]
    expert = [(k + swap(s, "zl").astype(F32))[None] for k, s in zip(kept, sent)]
    at = 2 * WIDTH
    return (
        block_out,
        grad_in,
        dense[:, at + 1088],
        dense[:, :WIDTH],
        dense[:, at : at + 512],
        dense[:, at + 512 : at + 1024],
        dense[:, WIDTH:at],
        dense[:, at + 1089],
        dense[:, at + 1024 : at + 1088],
        pair_grad[:, :SHARED],
        pair_grad[:, SHARED:],
        down_grad,
        expert[0],
        expert[1],
        expert[2],
    )


def solution(mesh):
    fine = Mesh(mesh.devices.reshape(2, 4, 4, 2, 2), AXES)
    rows, vector = P(AXES, None), P(AXES)
    banks = (P(DP, None, "zl"), P(DP, None, "zl"), P(DP, "zl", None))
    return jax.shard_map(
        body,
        mesh=fine,
        in_specs=(rows, rows, rows, rows, vector, rows, rows, rows, rows, vector)
        + (rows, rows, rows, rows)
        + banks,
        out_specs=(rows, rows, vector, rows, rows, rows, rows, vector)
        + (rows, rows, rows, rows)
        + banks,
        check_vma=False,
    )
```

```python
import jax
import jax.numpy as jnp
from jax import lax
from jax.experimental import pallas as pl
from jax.experimental.pallas import tpu as pltpu
from jax.sharding import Mesh, PartitionSpec as P

GROUP = 3
HEAD = 128
EXPERTS = 64
SLOTS = 32
TOKENS = 256
WIDTH = 1536
SHARED = 1024
HALF = 256
ROWS = EXPERTS * SLOTS
PAIRS = ROWS // 2
WIDE = 2 * WIDTH + 128
PACK = 2 * WIDTH + 1024 + 128

EPSILON = 1e-06
NEGATIVE = -1e30
SCALING = HEAD ** (-0.5)
BF = jnp.bfloat16
F32 = jnp.float32

AXES = ("zh", "x", "y", "c", "zl")
DP = ("zh", "x", "y", "c")
PLANE = ("x", "y", "c")
ANY = pl.BlockSpec(memory_space=pl.ANY)


def mm(a, b):
    return jnp.dot(a, b, preferred_element_type=F32)


def mm_l(a, b):
    return lax.dot_general(a, b, (((0,), (0,)), ((), ())), preferred_element_type=F32)


def mm_r(a, b):
    return lax.dot_general(a, b, (((1,), (1,)), ((), ())), preferred_element_type=F32)


def swap(x, axis):
    return lax.ppermute(x, axis, [(0, 1), (1, 0)])


def out(shape, dtype):
    return jax.ShapeDtypeStruct(shape, dtype)


def full(shape):
    return pl.BlockSpec(shape, lambda *i: (0,) * len(shape))


def call(kernel, grid, in_specs, out_specs, out_shape, scratch=(), flops=0, aliases=None):
    return pl.pallas_call(
        kernel,
        grid=grid,
        in_specs=in_specs,
        out_specs=out_specs,
        out_shape=out_shape,
        scratch_shapes=list(scratch),
        input_output_aliases=aliases or {},
        compiler_params=pltpu.CompilerParams(vmem_limit_bytes=56 * 1024 * 1024),
        cost_estimate=pl.CostEstimate(flops=flops, bytes_accessed=0, transcendentals=0),
    )


def fetch(source, target, sem):
    copy = pltpu.make_async_copy(source, target, sem)
    copy.start()
    return copy


def tie_kernel(*refs):
    pass


def tie(x, *after):
    return pl.pallas_call(
        tie_kernel,
        in_specs=[ANY] * (1 + len(after)),
        out_specs=ANY,
        out_shape=out(x.shape, x.dtype),
        input_output_aliases={0: 0},
    )(x, *after)


def gather_plane(pairs):
    _, rows, width = pairs.shape
    return lax.all_gather(pairs, PLANE, axis=1, tiled=True).reshape(64 * rows, width)


def scatter_plane(grads):
    return lax.psum_scatter(grads, PLANE, scatter_dimension=0, tiled=True)


def sum_line(plane, cut):
    width = plane.shape[1] // 2
    zh = lax.axis_index("zh")
    zl = lax.axis_index("zl")
    low, high = plane[:, :width], plane[:, width:]
    near, far = jnp.where(zh == 0, low, high), jnp.where(zh == 0, high, low)
    ours, theirs = cut(near)
    total = jnp.where(zl == 0, ours, theirs).astype(F32)
    total += swap(jnp.where(zl == 0, theirs, ours), "zl").astype(F32)
    ours, theirs = cut(far)
    total += swap(jnp.where(zl == 0, ours, theirs), "zh").astype(F32)
    across = [(i, 3 - i) for i in range(4)]
    give = jnp.where(zl == 0, theirs, ours)
    return total + lax.ppermute(give, ("zh", "zl"), across).astype(F32)


def fold_down(rows):
    tail = [rows[:, :8, 1024:], rows[:, 8:, 1024:]]
    return jnp.concatenate([rows[:, :, :1024], jnp.concatenate(tail, axis=2)], axis=1)


def unfold_down(rows):
    tail = jnp.concatenate([rows[:, 16:, :512], rows[:, 16:, 512:]], axis=1)
    return jnp.concatenate([rows[:, :16], tail], axis=2)


def deal_kernel(rank_ref, cot_ref, hits_ref, deal_ref, turned_ref, out_ref):
    rank = rank_ref[...]
    slot = lax.broadcasted_iota(jnp.int32, (8, SLOTS, TOKENS), 1).astype(F32)
    hit = jnp.where(rank[:, None, :] == slot, 1.0, 0.0)
    lane = lax.broadcasted_iota(jnp.int32, (128, 128), 1)
    marks = jnp.zeros((128, 128), F32)
    for j in range(2):
        side = hit[:, j * 16 : (j + 1) * 16].reshape(128, TOKENS)
        deal = side.astype(BF)
        deal_ref[j] = deal
        turned_ref[j] = jnp.transpose(side).astype(BF)
        out_ref[:, j * WIDTH : (j + 1) * WIDTH] = mm(deal, cot_ref[...]).astype(BF)
        mark = mm(deal, hits_ref[...])
        marks += mark if j == 0 else pltpu.roll(mark, 64, 1)
    out_ref[:, 2 * WIDTH :] = marks.astype(BF)


def deal_out(rank, out_grad, hits):
    return call(
        deal_kernel,
        (8,),
        [
            pl.BlockSpec((8, TOKENS), lambda i: (i, 0)),
            full((TOKENS, WIDTH)),
            full((TOKENS, 128)),
        ],
        [
            pl.BlockSpec((2, 128, TOKENS), lambda i: (0, i, 0)),
            pl.BlockSpec((2, TOKENS, 128), lambda i: (0, 0, i)),
            pl.BlockSpec((128, WIDE), lambda i: (i, 0)),
        ],
        [out((2, PAIRS, TOKENS), BF), out((2, TOKENS, PAIRS), BF), out((PAIRS, WIDE), BF)],
    )(rank, out_grad, hits)


def dispatch_kernel(deal_ref, rows_ref, out_ref):
    out_ref[...] = mm(deal_ref[0], rows_ref[...]).astype(BF)


def dispatch(deal, rows):
    return call(
        dispatch_kernel,
        (4,),
        [
            pl.BlockSpec((1, PAIRS, TOKENS), lambda j: (j // 2, 0, 0)),
            pl.BlockSpec((TOKENS, 768), lambda j: (0, j % 2)),
        ],
        pl.BlockSpec((PAIRS, 768), lambda j: (0, j)),
        out((PAIRS, 2 * WIDTH), BF),
    )(deal, rows)


def to_experts(rows):
    return lax.all_to_all(
        rows.reshape(EXPERTS, SLOTS // 2, -1), DP, split_axis=0, concat_axis=0, tiled=True
    ).reshape(PAIRS, -1)


def result_kernel(turned_ref, rows_ref, base_ref, out_ref, acc):
    step = pl.program_id(0)

    @pl.when(step == 0)
    def _():
        acc[...] = base_ref[...]

    acc[...] += mm(turned_ref[0], rows_ref[...])

    @pl.when(step == 3)
    def _():
        out_ref[...] = acc[...].astype(BF)


def add_results(turned, rows, base):
    return call(
        result_kernel,
        (4,),
        [
            pl.BlockSpec((1, TOKENS, 512), lambda i: (i // 2, 0, i % 2)),
            pl.BlockSpec((512, WIDTH), lambda i: (i % 2, i // 2)),
            full((TOKENS, WIDTH)),
        ],
        full((TOKENS, WIDTH)),
        out((TOKENS, WIDTH), BF),
        [pltpu.VMEM((TOKENS, WIDTH), F32)],
        flops=10**13,
    )(turned, rows, base)


def root_scale(values):
    return lax.rsqrt(jnp.mean(values * values, axis=-1, keepdims=True) + EPSILON)


def forward_kernel(
    hidden_ref,
    docs_ref,
    hits_ref,
    pack_ref,
    attn_in_ref,
    q_ref,
    kv_ref,
    probs_ref,
    attended_ref,
    middle_ref,
    ffn_in_ref,
    gates_ref,
    gains_ref,
    small_ref,
    wq_ref,
    wkv_ref,
    wo_ref,
    sems,
):
    copies = [
        fetch(pack_ref.at[:, at : at + ref.shape[1]], ref, sems.at[i])
        for i, (at, ref) in enumerate(
            [(2 * WIDTH + 1024, small_ref), (0, wq_ref), (2 * WIDTH, wkv_ref), (WIDTH, wo_ref)]
        )
    ]
    copies[0].wait()
    gains = jnp.transpose(small_ref[...].astype(F32))
    gains_ref[...] = gains[64:72]
    gain_one, gain_two = gains[64:65], gains[65:66]
    tokens = hidden_ref[...].astype(F32)
    attn_in_ref[...] = (tokens * root_scale(tokens) * gain_one).astype(BF)
    copies[1].wait()
    for j in range(0, WIDTH, 512):
        q_ref[:, j : j + 512] = mm(attn_in_ref[...], wq_ref[:, j : j + 512]).astype(BF)
    copies[2].wait()
    for j in range(0, 1024, 512):
        kv_ref[:, j : j + 512] = mm(attn_in_ref[...], wkv_ref[:, j : j + 512]).astype(BF)
    first = docs_ref[0, 0]
    second = first + docs_ref[0, 1]
    third = second + docs_ref[0, 2]
    row = lax.broadcasted_iota(jnp.int32, (TOKENS, TOKENS), 0)
    col = lax.broadcasted_iota(jnp.int32, (TOKENS, TOKENS), 1)

    def segment(place):
        return (
            (place >= first).astype(jnp.int32)
            + (place >= second).astype(jnp.int32)
            + (place >= third).astype(jnp.int32)
        )

    visible = (segment(row) == segment(col)) & (row >= col)
    for kv_head in range(4):
        key = kv_ref[:, kv_head * HEAD : (kv_head + 1) * HEAD]
        value = kv_ref[:, 512 + kv_head * HEAD : 512 + (kv_head + 1) * HEAD]
        for head in range(kv_head * GROUP, (kv_head + 1) * GROUP):
            at = slice(head * HEAD, (head + 1) * HEAD)
            scores = jnp.where(visible, mm_r(q_ref[:, at], key) * SCALING, NEGATIVE)
            exponent = jnp.exp(scores - jnp.max(scores, axis=-1, keepdims=True))
            probs = exponent / jnp.sum(exponent, axis=-1, keepdims=True)
            probs_ref[head] = probs
            attended_ref[:, at] = mm(probs.astype(BF), value).astype(BF)
    copies[3].wait()
    for j in range(0, WIDTH, 512):
        at = slice(j, j + 512)
        middle_ref[:, at] = hidden_ref[:, at].astype(F32) + mm(
            attended_ref[...], wo_ref[:, at]
        )
    middle = middle_ref[...]
    ffn_in_ref[...] = (middle * root_scale(middle) * gain_two).astype(BF)
    logits = mm(ffn_in_ref[...], small_ref[...])
    hits = hits_ref[...] > 0
    top = jnp.max(jnp.where(hits, logits, NEGATIVE), axis=-1, keepdims=True)
    weight = jnp.where(hits, jnp.exp(jnp.where(hits, logits - top, 0.0)), 0.0)
    gates_ref[...] = weight / jnp.sum(weight, axis=-1, keepdims=True)


def forward(hidden, docs, hits, pack):
    wide = (TOKENS, WIDTH)
    shapes = [
        (wide, BF),
        (wide, BF),
        ((TOKENS, 1024), BF),
        ((12, TOKENS, TOKENS), F32),
        (wide, BF),
        (wide, F32),
        (wide, BF),
        ((TOKENS, 128), F32),
        ((8, WIDTH), F32),
    ]
    return call(
        forward_kernel,
        (1,),
        [full(wide), pl.BlockSpec(memory_space=pltpu.SMEM), full((TOKENS, 128)), ANY],
        [full(s) for s, _ in shapes],
        [out(s, d) for s, d in shapes],
        [pltpu.VMEM((WIDTH, w), BF) for w in (128, WIDTH, 1024, WIDTH)]
        + [pltpu.SemaphoreType.DMA((4,))],
    )(hidden, docs, hits, pack)


def unpaired(ref):
    return jnp.concatenate([ref[:, :WIDTH], ref[:, WIDTH : 2 * WIDTH]], axis=0)


def act_cot_kernel(cot_ref, down_ref, other_ref, _after_ref, out_ref):
    cot = unpaired(cot_ref)
    out_ref[:, :HALF] = mm_r(cot, down_ref[...])
    out_ref[:, HALF:] = mm_r(cot, other_ref[...])


def act_cots(cot_rows, down, other, after):
    return call(
        act_cot_kernel,
        (8,),
        [
            pl.BlockSpec((128, 2 * WIDTH), lambda i: (i, 0)),
            full((HALF, WIDTH)),
            full((HALF, WIDTH)),
            ANY,
        ],
        pl.BlockSpec((256, 2 * HALF), lambda i: (i, 0)),
        out((ROWS, 2 * HALF), F32),
    )(cot_rows, down, other, after)


def expert_kernel(
    rows_ref,
    marks_ref,
    act_cot_ref,
    own_ref,
    small_ref,
    gate_ref,
    gate_other_ref,
    up_ref,
    up_other_ref,
    _after_ref,
    back_ref,
    act_ref,
    gate_cot_ref,
    up_cot_ref,
):
    rows = unpaired(rows_ref)
    lane = lax.broadcasted_iota(jnp.int32, (1, 128), 1)
    marks = marks_ref[...].astype(F32)
    marks = jnp.concatenate([marks, pltpu.roll(marks, 64, 1)], axis=0)
    marks = (marks > 0) & (lane < 64)
    logits = mm(rows, small_ref[...])
    top = jnp.max(jnp.where(marks, logits, NEGATIVE), axis=-1, keepdims=True)
    weight = jnp.where(marks, jnp.exp(jnp.where(marks, logits - top, 0.0)), 0.0)
    own = own_ref[...]
    total = jnp.sum(weight, axis=-1, keepdims=True)
    mine = jnp.sum(weight * own, axis=-1, keepdims=True)
    route_gate = mine / jnp.where(total > 0, total, 1.0)
    share = jnp.zeros((256, 1), F32)
    for half, gate_w, up_w in ((0, gate_ref, up_ref), (1, gate_other_ref, up_other_ref)):
        at = slice(half * HALF, (half + 1) * HALF)
        gate = mm(rows, gate_w[...])
        upper = mm(rows, up_w[...])
        sig = 1.0 / (1.0 + jnp.exp(-gate))
        silu = gate * sig
        act_cot = act_cot_ref[:, at]
        act = route_gate * silu * upper
        act_ref[:, at] = act.astype(BF)
        share += jnp.sum(act_cot * act, axis=-1, keepdims=True)
        scaled = route_gate * act_cot
        gate_cot_ref[:, at] = (scaled * upper * (sig * (1.0 + gate * (1.0 - sig)))).astype(BF)
        up_cot_ref[:, at] = (scaled * silu).astype(BF)
    for j in range(0, WIDTH, 512):
        at = slice(j, j + 512)
        total = mm_r(gate_cot_ref[:, :HALF], gate_ref[at, :])
        total += mm_r(gate_cot_ref[:, HALF:], gate_other_ref[at, :])
        total += mm_r(up_cot_ref[:, :HALF], up_ref[at, :])
        total += mm_r(up_cot_ref[:, HALF:], up_other_ref[at, :])
        back_ref[:, at] = total[:128].astype(BF)
        back_ref[:, WIDTH + j : WIDTH + j + 512] = total[128:].astype(BF)
    high = share.astype(BF).astype(F32)
    extra = jnp.zeros((128, 128), F32)
    for j, value in enumerate((high[:128], high[128:], (share - high)[:128], (share - high)[128:])):
        extra += jnp.where(lane == j, value, 0.0)
    back_ref[:, 2 * WIDTH :] = extra.astype(BF)


def expert_phase(rows, cot_rows, act_cot, own, pack, weights, after):
    tile = lambda w: pl.BlockSpec((256, w), lambda i: (i, 0))
    pair = lambda w, j=0: pl.BlockSpec((128, w), lambda i: (i, j))
    small = pl.BlockSpec((WIDTH, 128), lambda i: (0, 32))
    return call(
        expert_kernel,
        (8,),
        [pair(2 * WIDTH), pair(128, 24), tile(512), full((1, 128)), small]
        + [full(w.shape) for w in weights]
        + [ANY],
        [pair(WIDE), tile(512), tile(512), tile(512)],
        [out((PAIRS, WIDE), BF)] + [out((ROWS, 512), BF)] * 3,
    )(rows, cot_rows, act_cot, own, pack, *weights, after)


def expert_out_kernel(act_ref, down_ref, other_ref, _after_ref, out_ref):
    total = mm(act_ref[:, :HALF], down_ref[...]) + mm(act_ref[:, HALF:], other_ref[...])
    out_ref[:, :WIDTH] = total[:128].astype(BF)
    out_ref[:, WIDTH:] = total[128:].astype(BF)


def expert_outs(act, down, other, after):
    return call(
        expert_out_kernel,
        (8,),
        [
            pl.BlockSpec((256, 512), lambda i: (i, 0)),
            full((HALF, WIDTH)),
            full((HALF, WIDTH)),
            ANY,
        ],
        pl.BlockSpec((128, 2 * WIDTH), lambda i: (i, 0)),
        out((PAIRS, 2 * WIDTH), BF),
    )(act, down, other, after)


def expert_grad_kernel(
    rows_ref, cot_ref, act_ref, gate_cot_ref, up_cot_ref, _after_ref, gate_ref, up_ref, down_ref, gate, up, down
):
    step = pl.program_id(0)

    @pl.when(step == 0)
    def _():
        gate[...] = jnp.zeros_like(gate)
        up[...] = jnp.zeros_like(up)
        down[...] = jnp.zeros_like(down)

    rows = unpaired(rows_ref)
    gate[...] += mm_l(rows, gate_cot_ref[...])
    up[...] += mm_l(rows, up_cot_ref[...])
    down[...] += mm_l(act_ref[...], unpaired(cot_ref))

    @pl.when(step == 7)
    def _():
        gate_ref[...] = gate[...].astype(gate_ref.dtype)
        up_ref[...] = up[...].astype(up_ref.dtype)
        down_ref[...] = down[...].astype(down_ref.dtype)


def expert_grads(half, dtype, rows, cot_rows, act, gate_cot, up_cot, after):
    tile = lambda w, j=0: pl.BlockSpec((256, w), lambda i: (i, j))
    pair = pl.BlockSpec((128, 2 * WIDTH), lambda i: (i, 0))
    shapes = [(WIDTH, HALF), (WIDTH, HALF), (HALF, WIDTH)]
    return call(
        expert_grad_kernel,
        (8,),
        [pair, pair, tile(HALF, half), tile(HALF, half), tile(HALF, half), ANY],
        [full(s) for s in shapes],
        [out(s, dtype) for s in shapes],
        [pltpu.VMEM(s, F32) for s in shapes],
    )(rows, cot_rows, act, gate_cot, up_cot, after)


def shared_kernel(
    ffn_in_ref,
    out_grad_ref,
    middle_ref,
    second_ref,
    _after_ref,
    act_ref,
    pair_cot_ref,
    sum_ref,
    cot_ref,
    pair_w_ref,
    fold_ref,
    down_ref,
    tail_ref,
    sems,
):
    pair_copy = fetch(second_ref.at[:, : 2 * SHARED], pair_w_ref, sems.at[0])
    fold_copy = fetch(second_ref.at[:, 2 * SHARED :], fold_ref, sems.at[1])
    fold_copy.wait()
    for j in range(2):
        at = slice(j * 512, (j + 1) * 512)
        rows = fold_ref[:, at].astype(F32).reshape(64, 24, 512)
        down_ref[:, at] = rows[:, :16].reshape(SHARED, 512).astype(BF)
        tail_ref[:, j * 8 : (j + 1) * 8] = rows[:, 16:]
    down_ref[:, 1024:] = tail_ref[...].reshape(SHARED, 512).astype(BF)
    pair_copy.wait()
    for j in range(0, SHARED, 256):
        at = slice(j, j + 256)
        up_at = slice(SHARED + j, SHARED + j + 256)
        gate = mm(ffn_in_ref[...], pair_w_ref[:, at])
        upper = mm(ffn_in_ref[...], pair_w_ref[:, up_at])
        sig = 1.0 / (1.0 + jnp.exp(-gate))
        silu = gate * sig
        act_ref[:, at] = (silu * upper).astype(BF)
        cot = mm_r(out_grad_ref[...], down_ref[at, :])
        pair_cot_ref[:, at] = (cot * upper * (sig * (1.0 + gate * (1.0 - sig)))).astype(BF)
        pair_cot_ref[:, up_at] = (cot * silu).astype(BF)
    for j in range(0, WIDTH, 512):
        at = slice(j, j + 512)
        sum_ref[:, at] = middle_ref[:, at] + mm(act_ref[...], down_ref[:, at])
        cot_ref[:, at] = mm_r(pair_cot_ref[...], pair_w_ref[at, :])


def shared_phase(ffn_in, out_grad, middle, second, after):
    wide = (TOKENS, WIDTH)
    shapes = [((TOKENS, SHARED), BF), ((TOKENS, 2 * SHARED), BF), (wide, F32), (wide, F32)]
    return call(
        shared_kernel,
        (1,),
        [full(wide), full(wide), full(wide), ANY, ANY],
        [full(s) for s, _ in shapes],
        [out(s, d) for s, d in shapes],
        [
            pltpu.VMEM((WIDTH, 2 * SHARED), BF),
            pltpu.VMEM((WIDTH, 1024), BF),
            pltpu.VMEM((SHARED, WIDTH), BF),
            pltpu.VMEM((64, 16, 512), F32),
            pltpu.SemaphoreType.DMA((2,)),
        ],
    )(ffn_in, out_grad, middle, second, after)


def shared_grad_kernel(ffn_in_ref, pair_ref, act_ref, cot_ref, _after_ref, out_ref):
    for j in range(0, 2 * SHARED, 512):
        at = slice(j, j + 512)
        out_ref[:, at] = mm_l(ffn_in_ref[...], pair_ref[:, at]).astype(BF)
    for j in range(0, 1024, 512):
        body = mm_l(act_ref[...], cot_ref[:, j : j + 512]).reshape(32, 16, 512)
        tail = mm_l(act_ref[...], cot_ref[:, 1024:]).reshape(32, 16, 512)
        tail = tail[:, :8] if j == 0 else tail[:, 8:]
        both = jnp.concatenate([body, tail], axis=1).reshape(768, 512)
        out_ref[:, 2 * SHARED + j : 2 * SHARED + j + 512] = both.astype(BF)


def shared_grads(ffn_in, pair_low, shared_low, out_grad, after):
    return call(
        shared_grad_kernel,
        (2,),
        [
            pl.BlockSpec((TOKENS, 768), lambda h: (0, h)),
            full((TOKENS, 2 * SHARED)),
            pl.BlockSpec((TOKENS, 512), lambda h: (0, h)),
            full((TOKENS, WIDTH)),
            ANY,
        ],
        pl.BlockSpec((768, 2 * SHARED + 1024), lambda h: (0, h)),
        out((768, 4 * SHARED + 2048), BF),
    )(ffn_in, pair_low, shared_low, out_grad, after)


def norm_back(values, scale, gain, cot):
    weighted = cot * gain
    centre = jnp.mean(weighted * values, axis=-1, keepdims=True)
    return scale * weighted - values * (scale * scale * scale * centre)


def backward_kernel(*refs):
    n_in, n_out = 13, 8
    sources, outs, scratch = refs[:n_in], refs[n_in : n_in + n_out], refs[n_in + n_out :]
    back_hbm, pack_hbm = sources[:2]
    middle_low_ref, dq_ref, dkv_ref, grad_in_ref, logit_ref, one_ref, two_ref, cot_ref = outs
    back_ref, wo_ref, wq_ref, wkv_ref, small_ref, acc, sems = scratch[:7]
    held = scratch[7:]
    loads = [(back_hbm.at[:512], back_ref.at[:512]), (back_hbm.at[512:], back_ref.at[512:])]
    loads += [(a, b) for a, b in zip(sources[2:7], held[:5])]
    loads += [
        (pack_hbm.at[:, 2 * WIDTH + 1024 : PACK], small_ref),
        (pack_hbm.at[:, WIDTH : 2 * WIDTH], wo_ref),
    ]
    loads += [(a, b) for a, b in zip(sources[7:12], held[5:])]
    loads += [
        (pack_hbm.at[:, :WIDTH], wq_ref),
        (pack_hbm.at[:, 2 * WIDTH : 2 * WIDTH + 1024], wkv_ref),
    ]
    turned_ref, shared_ref, gates_ref, middle_ref, gains_ref = held[:5]
    out_grad_ref, q_ref, kv_ref, probs_ref, hidden_ref = held[5:]
    loads = [loads[2], loads[0], loads[1]] + loads[3:]
    copies = [fetch(a, b, sems.at[i]) for i, (a, b) in enumerate(loads)]
    for i in (0, 1):
        copies[i].wait()
    lane = lax.broadcasted_iota(jnp.int32, (512, 128), 1)
    row = lax.broadcasted_iota(jnp.int32, (512, 128), 0)
    shares = jnp.zeros((TOKENS, 128), F32)
    for half in range(2):
        at = slice(half * 512, (half + 1) * 512)
        if half:
            copies[2].wait()
        total = mm(turned_ref[0, :, at], back_ref[at, :WIDTH])
        total += mm(turned_ref[1, :, at], back_ref[at, WIDTH : 2 * WIDTH])
        if half:
            acc[...] += total
        else:
            acc[...] = total
        extra = back_ref[at, 2 * WIDTH :].astype(F32)
        mine = lane == row // 16 + half * 32
        for j in range(2):
            for value in (extra[:, j : j + 1], extra[:, 2 + j : 3 + j]):
                shares += mm(turned_ref[j, :, at], jnp.where(mine, value, 0.0).astype(BF))
    for i in range(3, 10):
        copies[i].wait()
    logit = shares - gates_ref[...] * jnp.sum(shares, axis=-1, keepdims=True)
    logit_ref[...] = logit.astype(BF)
    cot = acc[...] + shared_ref[...] + mm_r(logit_ref[...], small_ref[...])
    middle = middle_ref[...]
    scale = root_scale(middle)
    two_ref[...] = (cot * middle * scale).astype(BF)
    total = out_grad_ref[...].astype(F32) + norm_back(middle, scale, gains_ref[1:2], cot)
    grad_in_ref[...] = total
    middle_low_ref[...] = total.astype(BF)
    for j in range(0, WIDTH, 512):
        at = slice(j, j + 512)
        cot_ref[:, at] = mm_r(middle_low_ref[...], wo_ref[at, :]).astype(BF)
    for i in range(10, 14):
        copies[i].wait()
    for kv_head in range(4):
        key_at = slice(kv_head * HEAD, (kv_head + 1) * HEAD)
        value_at = slice(512 + kv_head * HEAD, 512 + (kv_head + 1) * HEAD)
        key, value = kv_ref[:, key_at], kv_ref[:, value_at]
        dk = jnp.zeros((TOKENS, HEAD), F32)
        dv = jnp.zeros((TOKENS, HEAD), F32)
        for head in range(kv_head * GROUP, (kv_head + 1) * GROUP):
            at = slice(head * HEAD, (head + 1) * HEAD)
            probs = probs_ref[head]
            head_cot = cot_ref[:, at]
            dprobs = mm_r(head_cot, value)
            dv += mm_l(probs.astype(BF), head_cot)
            centre = jnp.sum(probs * dprobs, axis=-1, keepdims=True)
            dscores = (probs * (dprobs - centre)).astype(BF)
            dq_ref[:, at] = (mm(dscores, key) * SCALING).astype(BF)
            dk += mm_l(dscores, q_ref[:, at])
        dkv_ref[:, key_at] = (dk * SCALING).astype(BF)
        dkv_ref[:, value_at] = dv.astype(BF)
    for i in range(14, 16):
        copies[i].wait()
    for j in range(0, WIDTH, 512):
        at = slice(j, j + 512)
        acc[:, at] = mm_r(dq_ref[...], wq_ref[at, :]) + mm_r(dkv_ref[...], wkv_ref[at, :])
    tokens = hidden_ref[...].astype(F32)
    scale = root_scale(tokens)
    cot = acc[...]
    one_ref[...] = (cot * tokens * scale).astype(BF)
    grad_in_ref[...] += norm_back(tokens, scale, gains_ref[0:1], cot)


def backward(back, pack, turned, shared_cot, gates, middle, gains, out_grad, q, kv, probs, hidden, after):
    wide = (TOKENS, WIDTH)
    shapes = [
        (wide, BF),
        (wide, BF),
        ((TOKENS, 1024), BF),
        (wide, F32),
        ((TOKENS, 128), BF),
        (wide, BF),
        (wide, BF),
        (wide, BF),
    ]
    held = [turned, shared_cot, gates, middle, gains, out_grad, q, kv, probs, hidden]
    scratch = [
        pltpu.VMEM((PAIRS, WIDE), BF),
        pltpu.VMEM((WIDTH, WIDTH), BF),
        pltpu.VMEM((WIDTH, WIDTH), BF),
        pltpu.VMEM((WIDTH, 1024), BF),
        pltpu.VMEM((WIDTH, 128), BF),
        pltpu.VMEM((TOKENS, WIDTH), F32),
        pltpu.SemaphoreType.DMA((16,)),
    ] + [pltpu.VMEM(a.shape, a.dtype) for a in held]
    return call(
        backward_kernel,
        (1,),
        [ANY] * 13,
        [full(s) for s, _ in shapes],
        [out(s, d) for s, d in shapes],
        scratch,
    )(back, pack, *held, after)


def dense_grad_kernel(
    attn_in_ref,
    attended_ref,
    ffn_in_ref,
    gain_one_ref,
    gain_two_ref,
    dq_ref,
    middle_ref,
    dkv_ref,
    logit_ref,
    out_ref,
    held,
    sems,
):
    copies = []

    def send(at, width):
        where = slice(at, at + width)
        copies.append(fetch(held.at[:, where], out_ref.at[:, where], sems.at[len(copies)]))

    for half in range(2):
        rows = slice(half * 768, (half + 1) * 768)
        base = half * PACK
        attended = attended_ref[:, rows]
        for j in range(0, WIDTH, 512):
            at = base + WIDTH + j
            held[:, at : at + 512] = mm_l(attended, middle_ref[:, j : j + 512]).astype(BF)
        send(base + WIDTH, WIDTH)
        attn_in = attn_in_ref[:, rows]
        for j in range(0, WIDTH, 512):
            at = base + j
            held[:, at : at + 512] = mm_l(attn_in, dq_ref[:, j : j + 512]).astype(BF)
        send(base, WIDTH)
        for j in range(0, 1024, 512):
            at = base + 2 * WIDTH + j
            held[:, at : at + 512] = mm_l(attn_in, dkv_ref[:, j : j + 512]).astype(BF)
        lane = lax.broadcasted_iota(jnp.int32, (TOKENS, 128), 1)
        small = mm_l(ffn_in_ref[:, rows], logit_ref[...])
        small += mm_l(gain_one_ref[:, rows], jnp.where(lane == 64, 1.0, 0.0).astype(BF))
        small += mm_l(gain_two_ref[:, rows], jnp.where(lane == 65, 1.0, 0.0).astype(BF))
        held[:, base + 2 * WIDTH + 1024 : base + PACK] = small.astype(BF)
        send(base + 2 * WIDTH, 1024 + 128)
    for copy in copies:
        copy.wait()


def dense_grads(attn_in, attended, ffn_in, gain_one, gain_two, dq, middle_low, dkv, logit):
    ins = [attn_in, attended, ffn_in, gain_one, gain_two, dq, middle_low, dkv, logit]
    return call(
        dense_grad_kernel,
        (1,),
        [full(a.shape) for a in ins],
        ANY,
        out((768, 2 * PACK), BF),
        [pltpu.VMEM((768, 2 * PACK), BF), pltpu.SemaphoreType.DMA((6,))],
        flops=10**13,
    )(*ins)


def body(
    hidden_in,
    out_grad,
    doc_lengths,
    expert_ids,
    gain_attn,
    w_query,
    w_key,
    w_value,
    w_out,
    gain_ffn,
    w_router,
    w_shared_gate,
    w_shared_up,
    w_shared_down,
    expert_gate,
    expert_up,
    expert_down,
):
    parts = [w_query, w_out, w_key, w_value, w_router, gain_attn[:, None], gain_ffn[:, None]]
    parts += [jnp.zeros((12, 62), BF), w_shared_gate, w_shared_up, w_shared_down.reshape(12, 1024)]
    line = lax.all_gather(jnp.concatenate(parts, axis=1), ("zh", "zl"), axis=0, tiled=False)
    pack = gather_plane(line[:, :, :PACK].reshape(2, 24, PACK))
    pair_w = line[:, :, PACK : PACK + 2 * SHARED].reshape(2, 24, 2 * SHARED)
    down_w = fold_down(line[:, :, PACK + 2 * SHARED :].reshape(2, 16, WIDTH))
    second = gather_plane(jnp.concatenate([pair_w, down_w], axis=2))
    gate, up, down = expert_gate[0], expert_up[0], expert_down[0]
    gate_other, up_other, down_other = swap(gate, "zl"), swap(up, "zl"), swap(down, "zl")

    lanes = jnp.arange(128, dtype=jnp.int32)
    hits = jnp.any(expert_ids[:, :, None] == lanes, axis=1)
    hits_low = hits.astype(BF)
    place = jnp.arange(TOKENS, dtype=jnp.int32)
    earlier = (place[:, None] > place[None, :]).astype(BF)
    rank = jnp.where(hits, mm(earlier, hits_low), -1.0).T[:EXPERTS]
    own = (lanes == lax.axis_index(DP)).astype(F32)[None]

    deal, turned, send_cot = deal_out(rank, out_grad, hits_low)
    cot_rows = to_experts(tie(send_cot, line))

    attn_in, q, kv, probs, attended, middle, ffn_in, gates, gains = forward(
        hidden_in, doc_lengths, hits_low, pack
    )
    send_rows = tie(dispatch(deal, ffn_in), gate_other, up_other, down_other)
    rows = to_experts(send_rows)

    act_cot = act_cots(cot_rows, down, down_other, send_rows)
    weights = (gate, gate_other, up, up_other)
    back, act, gate_cot, up_cot = expert_phase(
        rows, cot_rows, act_cot, own, pack, weights, send_rows
    )
    shared_low, pair_low, shared_sum, shared_cot = shared_phase(
        ffn_in, out_grad, middle, second, act
    )
    shared_grad = shared_grads(ffn_in, pair_low, shared_low, out_grad, shared_cot)

    kept = expert_grads(0, F32, rows, cot_rows, act, gate_cot, up_cot, shared_grad)
    shared_grad = scatter_plane(shared_grad)
    sent = expert_grads(1, BF, rows, cot_rows, act, gate_cot, up_cot, kept[0])
    result = expert_outs(act, down, down_other, sent[0])
    back = to_experts(back)

    middle_low, dq, dkv, grad_in, logit, one_rows, two_rows, _ = backward(
        back, pack, turned, shared_cot, gates, middle, gains, out_grad, q, kv, probs, hidden_in, result
    )
    result = to_experts(result)
    dense_grad = dense_grads(
        attn_in, attended, ffn_in, one_rows, two_rows, dq, middle_low, dkv, logit
    )
    dense = sum_line(scatter_plane(dense_grad), lambda x: (x[:12], x[12:]))

    def cut_shared(x):
        down = unfold_down(x[None, :, 2 * SHARED :])[0]
        return [
            jnp.concatenate([x[12 * i : 12 * i + 12, : 2 * SHARED], down[8 * i : 8 * i + 8].reshape(12, 1024)], axis=1)
            for i in range(2)
        ]

    shared_grad = sum_line(shared_grad, cut_shared)
    pair_grad = shared_grad[:, : 2 * SHARED]
    down_grad = shared_grad[:, 2 * SHARED :].reshape(8, WIDTH)
    block_out = add_results(turned, result, shared_sum)
    sent = [tie(x, dense_grad) for x in sent]
    expert = [(k + swap(s, "zl").astype(F32))[None] for k, s in zip(kept, sent)]
    at = 2 * WIDTH
    return (
        block_out,
        grad_in,
        dense[:, at + 1088],
        dense[:, :WIDTH],
        dense[:, at : at + 512],
        dense[:, at + 512 : at + 1024],
        dense[:, WIDTH:at],
        dense[:, at + 1089],
        dense[:, at + 1024 : at + 1088],
        pair_grad[:, :SHARED],
        pair_grad[:, SHARED:],
        down_grad,
        expert[0],
        expert[1],
        expert[2],
    )


def solution(mesh):
    fine = Mesh(mesh.devices.reshape(2, 4, 4, 2, 2), AXES)
    rows, vector = P(AXES, None), P(AXES)
    banks = (P(DP, None, "zl"), P(DP, None, "zl"), P(DP, "zl", None))
    return jax.shard_map(
        body,
        mesh=fine,
        in_specs=(rows, rows, rows, rows, vector, rows, rows, rows, rows, vector)
        + (rows, rows, rows, rows)
        + banks,
        out_specs=(rows, rows, vector, rows, rows, rows, rows, vector)
        + (rows, rows, rows, rows)
        + banks,
        check_vma=False,
    )
```

```python
import jax
import jax.numpy as jnp
from jax import lax
from jax.experimental import pallas as pl
from jax.experimental.pallas import tpu as pltpu
from jax.sharding import Mesh, PartitionSpec as P

GROUP = 3
HEAD = 128
EXPERTS = 64
SLOTS = 32
TOKENS = 256
WIDTH = 1536
SHARED = 1024
HALF = 256
ROWS = EXPERTS * SLOTS
PAIRS = ROWS // 2
WIDE = 2 * WIDTH + 128
PACK = 2 * WIDTH + 1024 + 128

EPSILON = 1e-06
NEGATIVE = -1e30
SCALING = HEAD ** (-0.5)
BF = jnp.bfloat16
F32 = jnp.float32

AXES = ("zh", "x", "y", "c", "zl")
DP = ("zh", "x", "y", "c")
PLANE = ("x", "y", "c")
ANY = pl.BlockSpec(memory_space=pl.ANY)


def mm(a, b):
    return jnp.dot(a, b, preferred_element_type=F32)


def mm_l(a, b):
    return lax.dot_general(a, b, (((0,), (0,)), ((), ())), preferred_element_type=F32)


def mm_r(a, b):
    return lax.dot_general(a, b, (((1,), (1,)), ((), ())), preferred_element_type=F32)


def swap(x, axis):
    return lax.ppermute(x, axis, [(0, 1), (1, 0)])


def out(shape, dtype):
    return jax.ShapeDtypeStruct(shape, dtype)


def full(shape):
    return pl.BlockSpec(shape, lambda *i: (0,) * len(shape))


def call(kernel, grid, in_specs, out_specs, out_shape, scratch=(), flops=0, aliases=None):
    return pl.pallas_call(
        kernel,
        grid=grid,
        in_specs=in_specs,
        out_specs=out_specs,
        out_shape=out_shape,
        scratch_shapes=list(scratch),
        input_output_aliases=aliases or {},
        compiler_params=pltpu.CompilerParams(vmem_limit_bytes=56 * 1024 * 1024),
        cost_estimate=pl.CostEstimate(flops=flops, bytes_accessed=0, transcendentals=0),
    )


def fetch(source, target, sem):
    copy = pltpu.make_async_copy(source, target, sem)
    copy.start()
    return copy


def tie_kernel(*refs):
    pass


def tie(x, *after):
    return pl.pallas_call(
        tie_kernel,
        in_specs=[ANY] * (1 + len(after)),
        out_specs=ANY,
        out_shape=out(x.shape, x.dtype),
        input_output_aliases={0: 0},
    )(x, *after)


def gather_plane(pairs):
    _, rows, width = pairs.shape
    return lax.all_gather(pairs, PLANE, axis=1, tiled=True).reshape(64 * rows, width)


def scatter_plane(grads):
    return lax.psum_scatter(grads, PLANE, scatter_dimension=0, tiled=True)


def sum_line(plane, cut):
    width = plane.shape[1] // 2
    zh = lax.axis_index("zh")
    zl = lax.axis_index("zl")
    low, high = plane[:, :width], plane[:, width:]
    near, far = jnp.where(zh == 0, low, high), jnp.where(zh == 0, high, low)
    ours, theirs = cut(near)
    total = jnp.where(zl == 0, ours, theirs).astype(F32)
    total += swap(jnp.where(zl == 0, theirs, ours), "zl").astype(F32)
    ours, theirs = cut(far)
    total += swap(jnp.where(zl == 0, ours, theirs), "zh").astype(F32)
    across = [(i, 3 - i) for i in range(4)]
    give = jnp.where(zl == 0, theirs, ours)
    return total + lax.ppermute(give, ("zh", "zl"), across).astype(F32)


def fold_down(rows):
    tail = [rows[:, :8, 1024:], rows[:, 8:, 1024:]]
    return jnp.concatenate([rows[:, :, :1024], jnp.concatenate(tail, axis=2)], axis=1)


def unfold_down(rows):
    tail = jnp.concatenate([rows[:, 16:, :512], rows[:, 16:, 512:]], axis=1)
    return jnp.concatenate([rows[:, :16], tail], axis=2)


def deal_kernel(rank_ref, cot_ref, hits_ref, deal_ref, turned_ref, out_ref):
    rank = rank_ref[...]
    slot = lax.broadcasted_iota(jnp.int32, (8, SLOTS, TOKENS), 1).astype(F32)
    hit = jnp.where(rank[:, None, :] == slot, 1.0, 0.0)
    lane = lax.broadcasted_iota(jnp.int32, (128, 128), 1)
    marks = jnp.zeros((128, 128), F32)
    for j in range(2):
        side = hit[:, j * 16 : (j + 1) * 16].reshape(128, TOKENS)
        deal = side.astype(BF)
        deal_ref[j] = deal
        turned_ref[j] = jnp.transpose(side).astype(BF)
        out_ref[:, j * WIDTH : (j + 1) * WIDTH] = mm(deal, cot_ref[...]).astype(BF)
        mark = mm(deal, hits_ref[...])
        marks += mark if j == 0 else pltpu.roll(mark, 64, 1)
    out_ref[:, 2 * WIDTH :] = marks.astype(BF)


def deal_out(rank, out_grad, hits):
    return call(
        deal_kernel,
        (8,),
        [
            pl.BlockSpec((8, TOKENS), lambda i: (i, 0)),
            full((TOKENS, WIDTH)),
            full((TOKENS, 128)),
        ],
        [
            pl.BlockSpec((2, 128, TOKENS), lambda i: (0, i, 0)),
            pl.BlockSpec((2, TOKENS, 128), lambda i: (0, 0, i)),
            pl.BlockSpec((128, WIDE), lambda i: (i, 0)),
        ],
        [out((2, PAIRS, TOKENS), BF), out((2, TOKENS, PAIRS), BF), out((PAIRS, WIDE), BF)],
    )(rank, out_grad, hits)


def dispatch_kernel(deal_ref, rows_ref, out_ref):
    out_ref[...] = mm(deal_ref[0], rows_ref[...]).astype(BF)


def dispatch(deal, rows):
    return call(
        dispatch_kernel,
        (4,),
        [
            pl.BlockSpec((1, PAIRS, TOKENS), lambda j: (j // 2, 0, 0)),
            pl.BlockSpec((TOKENS, 768), lambda j: (0, j % 2)),
        ],
        pl.BlockSpec((PAIRS, 768), lambda j: (0, j)),
        out((PAIRS, 2 * WIDTH), BF),
    )(deal, rows)


def to_experts(rows):
    return lax.all_to_all(
        rows.reshape(EXPERTS, SLOTS // 2, -1), DP, split_axis=0, concat_axis=0, tiled=True
    ).reshape(PAIRS, -1)


def result_kernel(turned_ref, rows_ref, base_ref, out_ref, acc):
    step = pl.program_id(0)

    @pl.when(step == 0)
    def _():
        acc[...] = base_ref[...]

    acc[...] += mm(turned_ref[0], rows_ref[...])

    @pl.when(step == 3)
    def _():
        out_ref[...] = acc[...].astype(BF)


def add_results(turned, rows, base):
    return call(
        result_kernel,
        (4,),
        [
            pl.BlockSpec((1, TOKENS, 512), lambda i: (i // 2, 0, i % 2)),
            pl.BlockSpec((512, WIDTH), lambda i: (i % 2, i // 2)),
            full((TOKENS, WIDTH)),
        ],
        full((TOKENS, WIDTH)),
        out((TOKENS, WIDTH), BF),
        [pltpu.VMEM((TOKENS, WIDTH), F32)],
        flops=10**13,
    )(turned, rows, base)


def root_scale(values):
    return lax.rsqrt(jnp.mean(values * values, axis=-1, keepdims=True) + EPSILON)


def forward_kernel(
    hidden_ref,
    docs_ref,
    hits_ref,
    pack_ref,
    attn_in_ref,
    q_ref,
    kv_ref,
    probs_ref,
    attended_ref,
    middle_ref,
    ffn_in_ref,
    gates_ref,
    gains_ref,
    small_ref,
    wq_ref,
    wkv_ref,
    wo_ref,
    sems,
):
    copies = [
        fetch(pack_ref.at[:, at : at + ref.shape[1]], ref, sems.at[i])
        for i, (at, ref) in enumerate(
            [(2 * WIDTH + 1024, small_ref), (0, wq_ref), (2 * WIDTH, wkv_ref), (WIDTH, wo_ref)]
        )
    ]
    copies[0].wait()
    gains = jnp.transpose(small_ref[...].astype(F32))
    gains_ref[...] = gains[64:72]
    gain_one, gain_two = gains[64:65], gains[65:66]
    tokens = hidden_ref[...].astype(F32)
    attn_in_ref[...] = (tokens * root_scale(tokens) * gain_one).astype(BF)
    copies[1].wait()
    for j in range(0, WIDTH, 512):
        q_ref[:, j : j + 512] = mm(attn_in_ref[...], wq_ref[:, j : j + 512]).astype(BF)
    copies[2].wait()
    for j in range(0, 1024, 512):
        kv_ref[:, j : j + 512] = mm(attn_in_ref[...], wkv_ref[:, j : j + 512]).astype(BF)
    first = docs_ref[0, 0]
    second = first + docs_ref[0, 1]
    third = second + docs_ref[0, 2]
    row = lax.broadcasted_iota(jnp.int32, (TOKENS, TOKENS), 0)
    col = lax.broadcasted_iota(jnp.int32, (TOKENS, TOKENS), 1)

    def segment(place):
        return (
            (place >= first).astype(jnp.int32)
            + (place >= second).astype(jnp.int32)
            + (place >= third).astype(jnp.int32)
        )

    visible = (segment(row) == segment(col)) & (row >= col)
    for kv_head in range(4):
        key = kv_ref[:, kv_head * HEAD : (kv_head + 1) * HEAD]
        value = kv_ref[:, 512 + kv_head * HEAD : 512 + (kv_head + 1) * HEAD]
        for head in range(kv_head * GROUP, (kv_head + 1) * GROUP):
            at = slice(head * HEAD, (head + 1) * HEAD)
            scores = jnp.where(visible, mm_r(q_ref[:, at], key) * SCALING, NEGATIVE)
            exponent = jnp.exp(scores - jnp.max(scores, axis=-1, keepdims=True))
            probs = exponent / jnp.sum(exponent, axis=-1, keepdims=True)
            probs_ref[head] = probs
            attended_ref[:, at] = mm(probs.astype(BF), value).astype(BF)
    copies[3].wait()
    for j in range(0, WIDTH, 512):
        at = slice(j, j + 512)
        middle_ref[:, at] = hidden_ref[:, at].astype(F32) + mm(
            attended_ref[...], wo_ref[:, at]
        )
    middle = middle_ref[...]
    ffn_in_ref[...] = (middle * root_scale(middle) * gain_two).astype(BF)
    logits = mm(ffn_in_ref[...], small_ref[...])
    hits = hits_ref[...] > 0
    top = jnp.max(jnp.where(hits, logits, NEGATIVE), axis=-1, keepdims=True)
    weight = jnp.where(hits, jnp.exp(jnp.where(hits, logits - top, 0.0)), 0.0)
    gates_ref[...] = weight / jnp.sum(weight, axis=-1, keepdims=True)


def forward(hidden, docs, hits, pack):
    wide = (TOKENS, WIDTH)
    shapes = [
        (wide, BF),
        (wide, BF),
        ((TOKENS, 1024), BF),
        ((12, TOKENS, TOKENS), F32),
        (wide, BF),
        (wide, F32),
        (wide, BF),
        ((TOKENS, 128), F32),
        ((8, WIDTH), F32),
    ]
    return call(
        forward_kernel,
        (1,),
        [full(wide), pl.BlockSpec(memory_space=pltpu.SMEM), full((TOKENS, 128)), ANY],
        [full(s) for s, _ in shapes],
        [out(s, d) for s, d in shapes],
        [pltpu.VMEM((WIDTH, w), BF) for w in (128, WIDTH, 1024, WIDTH)]
        + [pltpu.SemaphoreType.DMA((4,))],
    )(hidden, docs, hits, pack)


def unpaired(ref):
    return jnp.concatenate([ref[:, :WIDTH], ref[:, WIDTH : 2 * WIDTH]], axis=0)


def act_cot_kernel(cot_ref, down_ref, other_ref, _after_ref, out_ref):
    cot = unpaired(cot_ref)
    out_ref[:, :HALF] = mm_r(cot, down_ref[...])
    out_ref[:, HALF:] = mm_r(cot, other_ref[...])


def act_cots(cot_rows, down, other, after):
    return call(
        act_cot_kernel,
        (8,),
        [
            pl.BlockSpec((128, 2 * WIDTH), lambda i: (i, 0)),
            full((HALF, WIDTH)),
            full((HALF, WIDTH)),
            ANY,
        ],
        pl.BlockSpec((256, 2 * HALF), lambda i: (i, 0)),
        out((ROWS, 2 * HALF), F32),
    )(cot_rows, down, other, after)


def expert_kernel(
    rows_ref,
    marks_ref,
    act_cot_ref,
    own_ref,
    small_ref,
    gate_ref,
    gate_other_ref,
    up_ref,
    up_other_ref,
    _after_ref,
    back_ref,
    act_ref,
    gate_cot_ref,
    up_cot_ref,
):
    rows = unpaired(rows_ref)
    lane = lax.broadcasted_iota(jnp.int32, (1, 128), 1)
    marks = marks_ref[...].astype(F32)
    marks = jnp.concatenate([marks, pltpu.roll(marks, 64, 1)], axis=0)
    marks = (marks > 0) & (lane < 64)
    logits = mm(rows, small_ref[...])
    top = jnp.max(jnp.where(marks, logits, NEGATIVE), axis=-1, keepdims=True)
    weight = jnp.where(marks, jnp.exp(jnp.where(marks, logits - top, 0.0)), 0.0)
    own = own_ref[...]
    total = jnp.sum(weight, axis=-1, keepdims=True)
    mine = jnp.sum(weight * own, axis=-1, keepdims=True)
    route_gate = mine / jnp.where(total > 0, total, 1.0)
    share = jnp.zeros((256, 1), F32)
    for half, gate_w, up_w in ((0, gate_ref, up_ref), (1, gate_other_ref, up_other_ref)):
        at = slice(half * HALF, (half + 1) * HALF)
        gate = mm(rows, gate_w[...])
        upper = mm(rows, up_w[...])
        sig = 1.0 / (1.0 + jnp.exp(-gate))
        silu = gate * sig
        act_cot = act_cot_ref[:, at]
        act = route_gate * silu * upper
        act_ref[:, at] = act.astype(BF)
        share += jnp.sum(act_cot * act, axis=-1, keepdims=True)
        scaled = route_gate * act_cot
        gate_cot_ref[:, at] = (scaled * upper * (sig * (1.0 + gate * (1.0 - sig)))).astype(BF)
        up_cot_ref[:, at] = (scaled * silu).astype(BF)
    for j in range(0, WIDTH, 512):
        at = slice(j, j + 512)
        total = mm_r(gate_cot_ref[:, :HALF], gate_ref[at, :])
        total += mm_r(gate_cot_ref[:, HALF:], gate_other_ref[at, :])
        total += mm_r(up_cot_ref[:, :HALF], up_ref[at, :])
        total += mm_r(up_cot_ref[:, HALF:], up_other_ref[at, :])
        back_ref[:, at] = total[:128].astype(BF)
        back_ref[:, WIDTH + j : WIDTH + j + 512] = total[128:].astype(BF)
    high = share.astype(BF).astype(F32)
    extra = jnp.zeros((128, 128), F32)
    for j, value in enumerate((high[:128], high[128:], (share - high)[:128], (share - high)[128:])):
        extra += jnp.where(lane == j, value, 0.0)
    back_ref[:, 2 * WIDTH :] = extra.astype(BF)


def expert_phase(rows, cot_rows, act_cot, own, pack, weights, after):
    tile = lambda w: pl.BlockSpec((256, w), lambda i: (i, 0))
    pair = lambda w, j=0: pl.BlockSpec((128, w), lambda i: (i, j))
    small = pl.BlockSpec((WIDTH, 128), lambda i: (0, 32))
    return call(
        expert_kernel,
        (8,),
        [pair(2 * WIDTH), pair(128, 24), tile(512), full((1, 128)), small]
        + [full(w.shape) for w in weights]
        + [ANY],
        [pair(WIDE), tile(512), tile(512), tile(512)],
        [out((PAIRS, WIDE), BF)] + [out((ROWS, 512), BF)] * 3,
    )(rows, cot_rows, act_cot, own, pack, *weights, after)


def expert_out_kernel(act_ref, down_ref, other_ref, _after_ref, out_ref):
    total = mm(act_ref[:, :HALF], down_ref[...]) + mm(act_ref[:, HALF:], other_ref[...])
    out_ref[:, :WIDTH] = total[:128].astype(BF)
    out_ref[:, WIDTH:] = total[128:].astype(BF)


def expert_outs(act, down, other, after):
    return call(
        expert_out_kernel,
        (8,),
        [
            pl.BlockSpec((256, 512), lambda i: (i, 0)),
            full((HALF, WIDTH)),
            full((HALF, WIDTH)),
            ANY,
        ],
        pl.BlockSpec((128, 2 * WIDTH), lambda i: (i, 0)),
        out((PAIRS, 2 * WIDTH), BF),
    )(act, down, other, after)


def expert_grad_kernel(
    rows_ref, cot_ref, act_ref, gate_cot_ref, up_cot_ref, _after_ref, gate_ref, up_ref, down_ref, gate, up, down
):
    step = pl.program_id(0)

    @pl.when(step == 0)
    def _():
        gate[...] = jnp.zeros_like(gate)
        up[...] = jnp.zeros_like(up)
        down[...] = jnp.zeros_like(down)

    rows = unpaired(rows_ref)
    gate[...] += mm_l(rows, gate_cot_ref[...])
    up[...] += mm_l(rows, up_cot_ref[...])
    down[...] += mm_l(act_ref[...], unpaired(cot_ref))

    @pl.when(step == 7)
    def _():
        gate_ref[...] = gate[...].astype(gate_ref.dtype)
        up_ref[...] = up[...].astype(up_ref.dtype)
        down_ref[...] = down[...].astype(down_ref.dtype)


def expert_grads(half, dtype, rows, cot_rows, act, gate_cot, up_cot, after):
    tile = lambda w, j=0: pl.BlockSpec((256, w), lambda i: (i, j))
    pair = pl.BlockSpec((128, 2 * WIDTH), lambda i: (i, 0))
    shapes = [(WIDTH, HALF), (WIDTH, HALF), (HALF, WIDTH)]
    return call(
        expert_grad_kernel,
        (8,),
        [pair, pair, tile(HALF, half), tile(HALF, half), tile(HALF, half), ANY],
        [full(s) for s in shapes],
        [out(s, dtype) for s in shapes],
        [pltpu.VMEM(s, F32) for s in shapes],
    )(rows, cot_rows, act, gate_cot, up_cot, after)


def shared_kernel(
    ffn_in_ref,
    out_grad_ref,
    middle_ref,
    second_ref,
    _after_ref,
    act_ref,
    pair_cot_ref,
    sum_ref,
    cot_ref,
    pair_w_ref,
    fold_ref,
    down_ref,
    tail_ref,
    sems,
):
    pair_copy = fetch(second_ref.at[:, : 2 * SHARED], pair_w_ref, sems.at[0])
    fold_copy = fetch(second_ref.at[:, 2 * SHARED :], fold_ref, sems.at[1])
    fold_copy.wait()
    for j in range(2):
        at = slice(j * 512, (j + 1) * 512)
        rows = fold_ref[:, at].astype(F32).reshape(64, 24, 512)
        down_ref[:, at] = rows[:, :16].reshape(SHARED, 512).astype(BF)
        tail_ref[:, j * 8 : (j + 1) * 8] = rows[:, 16:]
    down_ref[:, 1024:] = tail_ref[...].reshape(SHARED, 512).astype(BF)
    pair_copy.wait()
    for j in range(0, SHARED, 256):
        at = slice(j, j + 256)
        up_at = slice(SHARED + j, SHARED + j + 256)
        gate = mm(ffn_in_ref[...], pair_w_ref[:, at])
        upper = mm(ffn_in_ref[...], pair_w_ref[:, up_at])
        sig = 1.0 / (1.0 + jnp.exp(-gate))
        silu = gate * sig
        act_ref[:, at] = (silu * upper).astype(BF)
        cot = mm_r(out_grad_ref[...], down_ref[at, :])
        pair_cot_ref[:, at] = (cot * upper * (sig * (1.0 + gate * (1.0 - sig)))).astype(BF)
        pair_cot_ref[:, up_at] = (cot * silu).astype(BF)
    for j in range(0, WIDTH, 512):
        at = slice(j, j + 512)
        sum_ref[:, at] = middle_ref[:, at] + mm(act_ref[...], down_ref[:, at])
        cot_ref[:, at] = mm_r(pair_cot_ref[...], pair_w_ref[at, :])


def shared_phase(ffn_in, out_grad, middle, second, after):
    wide = (TOKENS, WIDTH)
    shapes = [((TOKENS, SHARED), BF), ((TOKENS, 2 * SHARED), BF), (wide, F32), (wide, F32)]
    return call(
        shared_kernel,
        (1,),
        [full(wide), full(wide), full(wide), ANY, ANY],
        [full(s) for s, _ in shapes],
        [out(s, d) for s, d in shapes],
        [
            pltpu.VMEM((WIDTH, 2 * SHARED), BF),
            pltpu.VMEM((WIDTH, 1024), BF),
            pltpu.VMEM((SHARED, WIDTH), BF),
            pltpu.VMEM((64, 16, 512), F32),
            pltpu.SemaphoreType.DMA((2,)),
        ],
    )(ffn_in, out_grad, middle, second, after)


def shared_grad_kernel(ffn_in_ref, pair_ref, act_ref, cot_ref, _after_ref, out_ref):
    for j in range(0, 2 * SHARED, 512):
        at = slice(j, j + 512)
        out_ref[:, at] = mm_l(ffn_in_ref[...], pair_ref[:, at]).astype(BF)
    for j in range(0, 1024, 512):
        body = mm_l(act_ref[...], cot_ref[:, j : j + 512]).reshape(32, 16, 512)
        tail = mm_l(act_ref[...], cot_ref[:, 1024:]).reshape(32, 16, 512)
        tail = tail[:, :8] if j == 0 else tail[:, 8:]
        both = jnp.concatenate([body, tail], axis=1).reshape(768, 512)
        out_ref[:, 2 * SHARED + j : 2 * SHARED + j + 512] = both.astype(BF)


def shared_grads(ffn_in, pair_low, shared_low, out_grad, after):
    return call(
        shared_grad_kernel,
        (2,),
        [
            pl.BlockSpec((TOKENS, 768), lambda h: (0, h)),
            full((TOKENS, 2 * SHARED)),
            pl.BlockSpec((TOKENS, 512), lambda h: (0, h)),
            full((TOKENS, WIDTH)),
            ANY,
        ],
        pl.BlockSpec((768, 2 * SHARED + 1024), lambda h: (0, h)),
        out((768, 4 * SHARED + 2048), BF),
    )(ffn_in, pair_low, shared_low, out_grad, after)


def norm_back(values, scale, gain, cot):
    weighted = cot * gain
    centre = jnp.mean(weighted * values, axis=-1, keepdims=True)
    return scale * weighted - values * (scale * scale * scale * centre)


def backward_kernel(*refs):
    n_in, n_out = 13, 8
    sources, outs, scratch = refs[:n_in], refs[n_in : n_in + n_out], refs[n_in + n_out :]
    back_hbm, pack_hbm = sources[:2]
    middle_low_ref, dq_ref, dkv_ref, grad_in_ref, logit_ref, one_ref, two_ref, cot_ref = outs
    back_ref, wo_ref, wq_ref, wkv_ref, small_ref, acc, sems = scratch[:7]
    held = scratch[7:]
    loads = [(back_hbm.at[:512], back_ref.at[:512]), (back_hbm.at[512:], back_ref.at[512:])]
    loads += [(a, b) for a, b in zip(sources[2:7], held[:5])]
    loads += [
        (pack_hbm.at[:, 2 * WIDTH + 1024 : PACK], small_ref),
        (pack_hbm.at[:, WIDTH : 2 * WIDTH], wo_ref),
    ]
    loads += [(a, b) for a, b in zip(sources[7:12], held[5:])]
    loads += [
        (pack_hbm.at[:, :WIDTH], wq_ref),
        (pack_hbm.at[:, 2 * WIDTH : 2 * WIDTH + 1024], wkv_ref),
    ]
    turned_ref, shared_ref, gates_ref, middle_ref, gains_ref = held[:5]
    out_grad_ref, q_ref, kv_ref, probs_ref, hidden_ref = held[5:]
    loads = [loads[2], loads[0], loads[1]] + loads[3:]
    copies = [fetch(a, b, sems.at[i]) for i, (a, b) in enumerate(loads)]
    for i in (0, 1):
        copies[i].wait()
    lane = lax.broadcasted_iota(jnp.int32, (512, 128), 1)
    row = lax.broadcasted_iota(jnp.int32, (512, 128), 0)
    shares = jnp.zeros((TOKENS, 128), F32)
    for half in range(2):
        at = slice(half * 512, (half + 1) * 512)
        if half:
            copies[2].wait()
        total = mm(turned_ref[0, :, at], back_ref[at, :WIDTH])
        total += mm(turned_ref[1, :, at], back_ref[at, WIDTH : 2 * WIDTH])
        if half:
            acc[...] += total
        else:
            acc[...] = total
        extra = back_ref[at, 2 * WIDTH :].astype(F32)
        mine = lane == row // 16 + half * 32
        for j in range(2):
            for value in (extra[:, j : j + 1], extra[:, 2 + j : 3 + j]):
                shares += mm(turned_ref[j, :, at], jnp.where(mine, value, 0.0).astype(BF))
    for i in range(3, 10):
        copies[i].wait()
    logit = shares - gates_ref[...] * jnp.sum(shares, axis=-1, keepdims=True)
    logit_ref[...] = logit.astype(BF)
    cot = acc[...] + shared_ref[...] + mm_r(logit_ref[...], small_ref[...])
    middle = middle_ref[...]
    scale = root_scale(middle)
    two_ref[...] = (cot * middle * scale).astype(BF)
    total = out_grad_ref[...].astype(F32) + norm_back(middle, scale, gains_ref[1:2], cot)
    grad_in_ref[...] = total
    middle_low_ref[...] = total.astype(BF)
    for j in range(0, WIDTH, 512):
        at = slice(j, j + 512)
        cot_ref[:, at] = mm_r(middle_low_ref[...], wo_ref[at, :]).astype(BF)
    for i in range(10, 14):
        copies[i].wait()
    for kv_head in range(4):
        key_at = slice(kv_head * HEAD, (kv_head + 1) * HEAD)
        value_at = slice(512 + kv_head * HEAD, 512 + (kv_head + 1) * HEAD)
        key, value = kv_ref[:, key_at], kv_ref[:, value_at]
        dk = jnp.zeros((TOKENS, HEAD), F32)
        dv = jnp.zeros((TOKENS, HEAD), F32)
        for head in range(kv_head * GROUP, (kv_head + 1) * GROUP):
            at = slice(head * HEAD, (head + 1) * HEAD)
            probs = probs_ref[head]
            head_cot = cot_ref[:, at]
            dprobs = mm_r(head_cot, value)
            dv += mm_l(probs.astype(BF), head_cot)
            centre = jnp.sum(probs * dprobs, axis=-1, keepdims=True)
            dscores = (probs * (dprobs - centre)).astype(BF)
            dq_ref[:, at] = (mm(dscores, key) * SCALING).astype(BF)
            dk += mm_l(dscores, q_ref[:, at])
        dkv_ref[:, key_at] = (dk * SCALING).astype(BF)
        dkv_ref[:, value_at] = dv.astype(BF)
    for i in range(14, 16):
        copies[i].wait()
    for j in range(0, WIDTH, 512):
        at = slice(j, j + 512)
        acc[:, at] = mm_r(dq_ref[...], wq_ref[at, :]) + mm_r(dkv_ref[...], wkv_ref[at, :])
    tokens = hidden_ref[...].astype(F32)
    scale = root_scale(tokens)
    cot = acc[...]
    one_ref[...] = (cot * tokens * scale).astype(BF)
    grad_in_ref[...] += norm_back(tokens, scale, gains_ref[0:1], cot)


def backward(back, pack, turned, shared_cot, gates, middle, gains, out_grad, q, kv, probs, hidden, after):
    wide = (TOKENS, WIDTH)
    shapes = [
        (wide, BF),
        (wide, BF),
        ((TOKENS, 1024), BF),
        (wide, F32),
        ((TOKENS, 128), BF),
        (wide, BF),
        (wide, BF),
        (wide, BF),
    ]
    held = [turned, shared_cot, gates, middle, gains, out_grad, q, kv, probs, hidden]
    scratch = [
        pltpu.VMEM((PAIRS, WIDE), BF),
        pltpu.VMEM((WIDTH, WIDTH), BF),
        pltpu.VMEM((WIDTH, WIDTH), BF),
        pltpu.VMEM((WIDTH, 1024), BF),
        pltpu.VMEM((WIDTH, 128), BF),
        pltpu.VMEM((TOKENS, WIDTH), F32),
        pltpu.SemaphoreType.DMA((16,)),
    ] + [pltpu.VMEM(a.shape, a.dtype) for a in held]
    return call(
        backward_kernel,
        (1,),
        [ANY] * 13,
        [full(s) for s, _ in shapes],
        [out(s, d) for s, d in shapes],
        scratch,
    )(back, pack, *held, after)


def dense_grad_kernel(
    attn_in_ref,
    attended_ref,
    ffn_in_ref,
    gain_one_ref,
    gain_two_ref,
    dq_ref,
    middle_ref,
    dkv_ref,
    logit_ref,
    out_ref,
    held,
    sems,
):
    copies = []

    def send(at, width):
        where = slice(at, at + width)
        copies.append(fetch(held.at[:, where], out_ref.at[:, where], sems.at[len(copies)]))

    for half in range(2):
        rows = slice(half * 768, (half + 1) * 768)
        base = half * PACK
        attended = attended_ref[:, rows]
        for j in range(0, WIDTH, 512):
            at = base + WIDTH + j
            held[:, at : at + 512] = mm_l(attended, middle_ref[:, j : j + 512]).astype(BF)
        send(base + WIDTH, WIDTH)
        attn_in = attn_in_ref[:, rows]
        for j in range(0, WIDTH, 512):
            at = base + j
            held[:, at : at + 512] = mm_l(attn_in, dq_ref[:, j : j + 512]).astype(BF)
        send(base, WIDTH)
        for j in range(0, 1024, 512):
            at = base + 2 * WIDTH + j
            held[:, at : at + 512] = mm_l(attn_in, dkv_ref[:, j : j + 512]).astype(BF)
        lane = lax.broadcasted_iota(jnp.int32, (TOKENS, 128), 1)
        small = mm_l(ffn_in_ref[:, rows], logit_ref[...])
        small += mm_l(gain_one_ref[:, rows], jnp.where(lane == 64, 1.0, 0.0).astype(BF))
        small += mm_l(gain_two_ref[:, rows], jnp.where(lane == 65, 1.0, 0.0).astype(BF))
        held[:, base + 2 * WIDTH + 1024 : base + PACK] = small.astype(BF)
        send(base + 2 * WIDTH, 1024 + 128)
    for copy in copies:
        copy.wait()


def dense_grads(attn_in, attended, ffn_in, gain_one, gain_two, dq, middle_low, dkv, logit):
    ins = [attn_in, attended, ffn_in, gain_one, gain_two, dq, middle_low, dkv, logit]
    return call(
        dense_grad_kernel,
        (1,),
        [full(a.shape) for a in ins],
        ANY,
        out((768, 2 * PACK), BF),
        [pltpu.VMEM((768, 2 * PACK), BF), pltpu.SemaphoreType.DMA((6,))],
        flops=10**13,
    )(*ins)


def body(
    hidden_in,
    out_grad,
    doc_lengths,
    expert_ids,
    gain_attn,
    w_query,
    w_key,
    w_value,
    w_out,
    gain_ffn,
    w_router,
    w_shared_gate,
    w_shared_up,
    w_shared_down,
    expert_gate,
    expert_up,
    expert_down,
):
    parts = [w_query, w_out, w_key, w_value, w_router, gain_attn[:, None], gain_ffn[:, None]]
    parts += [jnp.zeros((12, 62), BF), w_shared_gate, w_shared_up, w_shared_down.reshape(12, 1024)]
    line = lax.all_gather(jnp.concatenate(parts, axis=1), ("zh", "zl"), axis=0, tiled=False)
    pack = gather_plane(line[:, :, :PACK].reshape(2, 24, PACK))
    pair_w = line[:, :, PACK : PACK + 2 * SHARED].reshape(2, 24, 2 * SHARED)
    down_w = fold_down(line[:, :, PACK + 2 * SHARED :].reshape(2, 16, WIDTH))
    second = gather_plane(jnp.concatenate([pair_w, down_w], axis=2))
    gate, up, down = expert_gate[0], expert_up[0], expert_down[0]
    gate_other, up_other, down_other = swap(gate, "zl"), swap(up, "zl"), swap(down, "zl")

    lanes = jnp.arange(128, dtype=jnp.int32)
    hits = jnp.any(expert_ids[:, :, None] == lanes, axis=1)
    hits_low = hits.astype(BF)
    place = jnp.arange(TOKENS, dtype=jnp.int32)
    earlier = (place[:, None] > place[None, :]).astype(BF)
    rank = jnp.where(hits, mm(earlier, hits_low), -1.0).T[:EXPERTS]
    own = (lanes == lax.axis_index(DP)).astype(F32)[None]

    deal, turned, send_cot = deal_out(rank, out_grad, hits_low)
    cot_rows = to_experts(tie(send_cot, line))

    attn_in, q, kv, probs, attended, middle, ffn_in, gates, gains = forward(
        hidden_in, doc_lengths, hits_low, pack
    )
    send_rows = tie(dispatch(deal, ffn_in), gate_other, up_other, down_other)
    rows = to_experts(send_rows)

    act_cot = act_cots(cot_rows, down, down_other, send_rows)
    shared_low, pair_low, shared_sum, shared_cot = shared_phase(
        ffn_in, out_grad, middle, second, act_cot
    )

    weights = (gate, gate_other, up, up_other)
    back, act, gate_cot, up_cot = expert_phase(
        rows, cot_rows, act_cot, own, pack, weights, shared_cot
    )
    shared_grad = shared_grads(ffn_in, pair_low, shared_low, out_grad, act)
    kept = expert_grads(0, F32, rows, cot_rows, act, gate_cot, up_cot, shared_grad)
    shared_grad = scatter_plane(shared_grad)
    sent = expert_grads(1, BF, rows, cot_rows, act, gate_cot, up_cot, kept[0])
    result = expert_outs(act, down, down_other, sent[0])
    back = to_experts(back)

    middle_low, dq, dkv, grad_in, logit, one_rows, two_rows, _ = backward(
        back, pack, turned, shared_cot, gates, middle, gains, out_grad, q, kv, probs, hidden_in, result
    )
    result = to_experts(result)
    dense_grad = dense_grads(
        attn_in, attended, ffn_in, one_rows, two_rows, dq, middle_low, dkv, logit
    )
    dense = sum_line(scatter_plane(dense_grad), lambda x: (x[:12], x[12:]))

    def cut_shared(x):
        down = unfold_down(x[None, :, 2 * SHARED :])[0]
        return [
            jnp.concatenate([x[12 * i : 12 * i + 12, : 2 * SHARED], down[8 * i : 8 * i + 8].reshape(12, 1024)], axis=1)
            for i in range(2)
        ]

    shared_grad = sum_line(shared_grad, cut_shared)
    pair_grad = shared_grad[:, : 2 * SHARED]
    down_grad = shared_grad[:, 2 * SHARED :].reshape(8, WIDTH)
    block_out = add_results(turned, result, shared_sum)
    sent = [tie(x, dense_grad) for x in sent]
    expert = [(k + swap(s, "zl").astype(F32))[None] for k, s in zip(kept, sent)]
    at = 2 * WIDTH
    return (
        block_out,
        grad_in,
        dense[:, at + 1088],
        dense[:, :WIDTH],
        dense[:, at : at + 512],
        dense[:, at + 512 : at + 1024],
        dense[:, WIDTH:at],
        dense[:, at + 1089],
        dense[:, at + 1024 : at + 1088],
        pair_grad[:, :SHARED],
        pair_grad[:, SHARED:],
        down_grad,
        expert[0],
        expert[1],
        expert[2],
    )


def solution(mesh):
    fine = Mesh(mesh.devices.reshape(2, 4, 4, 2, 2), AXES)
    rows, vector = P(AXES, None), P(AXES)
    banks = (P(DP, None, "zl"), P(DP, None, "zl"), P(DP, "zl", None))
    return jax.shard_map(
        body,
        mesh=fine,
        in_specs=(rows, rows, rows, rows, vector, rows, rows, rows, rows, vector)
        + (rows, rows, rows, rows)
        + banks,
        out_specs=(rows, rows, vector, rows, rows, rows, rows, vector)
        + (rows, rows, rows, rows)
        + banks,
        check_vma=False,
    )
```

```python
import jax
import jax.numpy as jnp
from jax import lax
from jax.experimental import pallas as pl
from jax.experimental.pallas import tpu as pltpu
from jax.sharding import Mesh, PartitionSpec as P

GROUP = 3
HEAD = 128
EXPERTS = 64
SLOTS = 32
TOKENS = 256
WIDTH = 1536
SHARED = 1024
HALF = 256
ROWS = EXPERTS * SLOTS
PAIRS = ROWS // 2
WIDE = 2 * WIDTH + 128
PACK = 2 * WIDTH + 1024 + 128

EPSILON = 1e-06
NEGATIVE = -1e30
SCALING = HEAD ** (-0.5)
BF = jnp.bfloat16
F32 = jnp.float32

AXES = ("zh", "x", "y", "c", "zl")
DP = ("zh", "x", "y", "c")
PLANE = ("x", "y", "c")
ANY = pl.BlockSpec(memory_space=pl.ANY)


def mm(a, b):
    return jnp.dot(a, b, preferred_element_type=F32)


def mm_l(a, b):
    return lax.dot_general(a, b, (((0,), (0,)), ((), ())), preferred_element_type=F32)


def mm_r(a, b):
    return lax.dot_general(a, b, (((1,), (1,)), ((), ())), preferred_element_type=F32)


def swap(x, axis):
    return lax.ppermute(x, axis, [(0, 1), (1, 0)])


def out(shape, dtype):
    return jax.ShapeDtypeStruct(shape, dtype)


def full(shape):
    return pl.BlockSpec(shape, lambda *i: (0,) * len(shape))


def call(kernel, grid, in_specs, out_specs, out_shape, scratch=(), flops=0, aliases=None):
    return pl.pallas_call(
        kernel,
        grid=grid,
        in_specs=in_specs,
        out_specs=out_specs,
        out_shape=out_shape,
        scratch_shapes=list(scratch),
        input_output_aliases=aliases or {},
        compiler_params=pltpu.CompilerParams(vmem_limit_bytes=56 * 1024 * 1024),
        cost_estimate=pl.CostEstimate(flops=flops, bytes_accessed=0, transcendentals=0),
    )


def fetch(source, target, sem):
    copy = pltpu.make_async_copy(source, target, sem)
    copy.start()
    return copy


def tie_kernel(*refs):
    pass


def tie(x, *after):
    return pl.pallas_call(
        tie_kernel,
        in_specs=[ANY] * (1 + len(after)),
        out_specs=ANY,
        out_shape=out(x.shape, x.dtype),
        input_output_aliases={0: 0},
    )(x, *after)


def gather_plane(pairs):
    _, rows, width = pairs.shape
    return lax.all_gather(pairs, PLANE, axis=1, tiled=True).reshape(64 * rows, width)


def scatter_plane(grads):
    return lax.psum_scatter(grads, PLANE, scatter_dimension=0, tiled=True)


def sum_line(plane, cut):
    width = plane.shape[1] // 2
    zh = lax.axis_index("zh")
    zl = lax.axis_index("zl")
    low, high = plane[:, :width], plane[:, width:]
    near, far = jnp.where(zh == 0, low, high), jnp.where(zh == 0, high, low)
    ours, theirs = cut(near)
    total = jnp.where(zl == 0, ours, theirs).astype(F32)
    total += swap(jnp.where(zl == 0, theirs, ours), "zl").astype(F32)
    ours, theirs = cut(far)
    total += swap(jnp.where(zl == 0, ours, theirs), "zh").astype(F32)
    across = [(i, 3 - i) for i in range(4)]
    give = jnp.where(zl == 0, theirs, ours)
    return total + lax.ppermute(give, ("zh", "zl"), across).astype(F32)


def fold_down(rows):
    tail = [rows[:, :8, 1024:], rows[:, 8:, 1024:]]
    return jnp.concatenate([rows[:, :, :1024], jnp.concatenate(tail, axis=2)], axis=1)


def unfold_down(rows):
    tail = jnp.concatenate([rows[:, 16:, :512], rows[:, 16:, 512:]], axis=1)
    return jnp.concatenate([rows[:, :16], tail], axis=2)


def deal_kernel(rank_ref, cot_ref, hits_ref, deal_ref, turned_ref, out_ref):
    rank = rank_ref[...]
    slot = lax.broadcasted_iota(jnp.int32, (8, SLOTS, TOKENS), 1).astype(F32)
    hit = jnp.where(rank[:, None, :] == slot, 1.0, 0.0)
    lane = lax.broadcasted_iota(jnp.int32, (128, 128), 1)
    marks = jnp.zeros((128, 128), F32)
    for j in range(2):
        side = hit[:, j * 16 : (j + 1) * 16].reshape(128, TOKENS)
        deal = side.astype(BF)
        deal_ref[j] = deal
        turned_ref[j] = jnp.transpose(side).astype(BF)
        out_ref[:, j * WIDTH : (j + 1) * WIDTH] = mm(deal, cot_ref[...]).astype(BF)
        mark = mm(deal, hits_ref[...])
        marks += mark if j == 0 else pltpu.roll(mark, 64, 1)
    out_ref[:, 2 * WIDTH :] = marks.astype(BF)


def deal_out(rank, out_grad, hits):
    return call(
        deal_kernel,
        (8,),
        [
            pl.BlockSpec((8, TOKENS), lambda i: (i, 0)),
            full((TOKENS, WIDTH)),
            full((TOKENS, 128)),
        ],
        [
            pl.BlockSpec((2, 128, TOKENS), lambda i: (0, i, 0)),
            pl.BlockSpec((2, TOKENS, 128), lambda i: (0, 0, i)),
            pl.BlockSpec((128, WIDE), lambda i: (i, 0)),
        ],
        [out((2, PAIRS, TOKENS), BF), out((2, TOKENS, PAIRS), BF), out((PAIRS, WIDE), BF)],
    )(rank, out_grad, hits)


def to_experts(rows):
    return lax.all_to_all(
        rows.reshape(EXPERTS, SLOTS // 2, -1), DP, split_axis=0, concat_axis=0, tiled=True
    ).reshape(PAIRS, -1)


def result_kernel(turned_ref, rows_ref, base_ref, out_ref, acc):
    step = pl.program_id(0)

    @pl.when(step == 0)
    def _():
        acc[...] = base_ref[...]

    acc[...] += mm(turned_ref[0], rows_ref[...])

    @pl.when(step == 3)
    def _():
        out_ref[...] = acc[...].astype(BF)


def add_results(turned, rows, base):
    return call(
        result_kernel,
        (4,),
        [
            pl.BlockSpec((1, TOKENS, 512), lambda i: (i // 2, 0, i % 2)),
            pl.BlockSpec((512, WIDTH), lambda i: (i % 2, i // 2)),
            full((TOKENS, WIDTH)),
        ],
        full((TOKENS, WIDTH)),
        out((TOKENS, WIDTH), BF),
        [pltpu.VMEM((TOKENS, WIDTH), F32)],
        flops=10**13,
    )(turned, rows, base)


def root_scale(values):
    return lax.rsqrt(jnp.mean(values * values, axis=-1, keepdims=True) + EPSILON)


def forward_kernel(hidden_ref, docs_ref, hits_ref, pack_ref, deal_hbm, *refs):
    outs, (small_ref, wq_ref, wkv_ref, wo_ref, deal_ref), held = refs[:10], refs[10:15], refs[15:25]
    sems = refs[25]
    (
        attn_in_ref,
        q_ref,
        kv_ref,
        probs_ref,
        attended_ref,
        middle_ref,
        ffn_in_ref,
        gates_ref,
        gains_ref,
        send_ref,
    ) = held
    copies = [
        fetch(pack_ref.at[:, at : at + ref.shape[1]], ref, sems.at[i])
        for i, (at, ref) in enumerate(
            [(2 * WIDTH + 1024, small_ref), (0, wq_ref), (2 * WIDTH, wkv_ref), (WIDTH, wo_ref)]
        )
    ]
    copies.append(fetch(deal_hbm, deal_ref, sems.at[4]))
    sent = []

    def send(i):
        sent.append(fetch(held[i], outs[i], sems.at[5 + i]))

    copies[0].wait()
    gains = jnp.transpose(small_ref[...].astype(F32))
    gains_ref[...] = gains[64:72]
    gain_one, gain_two = gains[64:65], gains[65:66]
    tokens = hidden_ref[...].astype(F32)
    attn_in_ref[...] = (tokens * root_scale(tokens) * gain_one).astype(BF)
    send(8)
    send(0)
    copies[1].wait()
    for j in range(0, WIDTH, 512):
        q_ref[:, j : j + 512] = mm(attn_in_ref[...], wq_ref[:, j : j + 512]).astype(BF)
    send(1)
    copies[2].wait()
    for j in range(0, 1024, 512):
        kv_ref[:, j : j + 512] = mm(attn_in_ref[...], wkv_ref[:, j : j + 512]).astype(BF)
    send(2)
    first = docs_ref[0, 0]
    second = first + docs_ref[0, 1]
    third = second + docs_ref[0, 2]
    row = lax.broadcasted_iota(jnp.int32, (TOKENS, TOKENS), 0)
    col = lax.broadcasted_iota(jnp.int32, (TOKENS, TOKENS), 1)

    def segment(place):
        return (
            (place >= first).astype(jnp.int32)
            + (place >= second).astype(jnp.int32)
            + (place >= third).astype(jnp.int32)
        )

    visible = (segment(row) == segment(col)) & (row >= col)
    for kv_head in range(4):
        key = kv_ref[:, kv_head * HEAD : (kv_head + 1) * HEAD]
        value = kv_ref[:, 512 + kv_head * HEAD : 512 + (kv_head + 1) * HEAD]
        for head in range(kv_head * GROUP, (kv_head + 1) * GROUP):
            at = slice(head * HEAD, (head + 1) * HEAD)
            scores = jnp.where(visible, mm_r(q_ref[:, at], key) * SCALING, NEGATIVE)
            exponent = jnp.exp(scores - jnp.max(scores, axis=-1, keepdims=True))
            probs = exponent / jnp.sum(exponent, axis=-1, keepdims=True)
            probs_ref[head] = probs
            attended_ref[:, at] = mm(probs.astype(BF), value).astype(BF)
    send(3)
    send(4)
    copies[3].wait()
    for j in range(0, WIDTH, 512):
        at = slice(j, j + 512)
        middle_ref[:, at] = hidden_ref[:, at].astype(F32) + mm(
            attended_ref[...], wo_ref[:, at]
        )
    middle = middle_ref[...]
    send(5)
    ffn_in_ref[...] = (middle * root_scale(middle) * gain_two).astype(BF)
    send(6)
    copies[4].wait()
    for j in range(4):
        at = slice(j * 768, (j + 1) * 768)
        from_at = slice(j % 2 * 768, (j % 2 + 1) * 768)
        send_ref[:, at] = mm(deal_ref[j // 2], ffn_in_ref[:, from_at]).astype(BF)
        sent.append(fetch(send_ref.at[:, at], outs[9].at[:, at], sems.at[14 + j]))
    logits = mm(ffn_in_ref[...], small_ref[...])
    hits = hits_ref[...] > 0
    top = jnp.max(jnp.where(hits, logits, NEGATIVE), axis=-1, keepdims=True)
    weight = jnp.where(hits, jnp.exp(jnp.where(hits, logits - top, 0.0)), 0.0)
    gates_ref[...] = weight / jnp.sum(weight, axis=-1, keepdims=True)
    send(7)
    for copy in sent:
        copy.wait()


def forward(hidden, docs, hits, pack, deal):
    wide = (TOKENS, WIDTH)
    shapes = [
        (wide, BF),
        (wide, BF),
        ((TOKENS, 1024), BF),
        ((12, TOKENS, TOKENS), F32),
        (wide, BF),
        (wide, F32),
        (wide, BF),
        ((TOKENS, 128), F32),
        ((8, WIDTH), F32),
        ((PAIRS, 2 * WIDTH), BF),
    ]
    return call(
        forward_kernel,
        (1,),
        [full(wide), pl.BlockSpec(memory_space=pltpu.SMEM), full((TOKENS, 128)), ANY, ANY],
        [ANY] * 10,
        [out(s, d) for s, d in shapes],
        [pltpu.VMEM((WIDTH, w), BF) for w in (128, WIDTH, 1024, WIDTH)]
        + [pltpu.VMEM(deal.shape, BF)]
        + [pltpu.VMEM(s, d) for s, d in shapes]
        + [pltpu.SemaphoreType.DMA((18,))],
    )(hidden, docs, hits, pack, deal)


def unpaired(ref):
    return jnp.concatenate([ref[:, :WIDTH], ref[:, WIDTH : 2 * WIDTH]], axis=0)


def act_cot_kernel(cot_ref, down_ref, other_ref, _after_ref, out_ref):
    cot = unpaired(cot_ref)
    out_ref[:, :HALF] = mm_r(cot, down_ref[...])
    out_ref[:, HALF:] = mm_r(cot, other_ref[...])


def act_cots(cot_rows, down, other, after):
    return call(
        act_cot_kernel,
        (8,),
        [
            pl.BlockSpec((128, 2 * WIDTH), lambda i: (i, 0)),
            full((HALF, WIDTH)),
            full((HALF, WIDTH)),
            ANY,
        ],
        pl.BlockSpec((256, 2 * HALF), lambda i: (i, 0)),
        out((ROWS, 2 * HALF), F32),
    )(cot_rows, down, other, after)


def expert_kernel(
    rows_ref,
    marks_ref,
    act_cot_ref,
    own_ref,
    small_ref,
    gate_ref,
    gate_other_ref,
    up_ref,
    up_other_ref,
    _after_ref,
    back_ref,
    act_ref,
    gate_cot_ref,
    up_cot_ref,
):
    rows = unpaired(rows_ref)
    lane = lax.broadcasted_iota(jnp.int32, (1, 128), 1)
    marks = marks_ref[...].astype(F32)
    marks = jnp.concatenate([marks, pltpu.roll(marks, 64, 1)], axis=0)
    marks = (marks > 0) & (lane < 64)
    logits = mm(rows, small_ref[...])
    top = jnp.max(jnp.where(marks, logits, NEGATIVE), axis=-1, keepdims=True)
    weight = jnp.where(marks, jnp.exp(jnp.where(marks, logits - top, 0.0)), 0.0)
    own = own_ref[...]
    total = jnp.sum(weight, axis=-1, keepdims=True)
    mine = jnp.sum(weight * own, axis=-1, keepdims=True)
    route_gate = mine / jnp.where(total > 0, total, 1.0)
    share = jnp.zeros((256, 1), F32)
    for half, gate_w, up_w in ((0, gate_ref, up_ref), (1, gate_other_ref, up_other_ref)):
        at = slice(half * HALF, (half + 1) * HALF)
        gate = mm(rows, gate_w[...])
        upper = mm(rows, up_w[...])
        sig = 1.0 / (1.0 + jnp.exp(-gate))
        silu = gate * sig
        act_cot = act_cot_ref[:, at]
        act = route_gate * silu * upper
        act_ref[:, at] = act.astype(BF)
        share += jnp.sum(act_cot * act, axis=-1, keepdims=True)
        scaled = route_gate * act_cot
        gate_cot_ref[:, at] = (scaled * upper * (sig * (1.0 + gate * (1.0 - sig)))).astype(BF)
        up_cot_ref[:, at] = (scaled * silu).astype(BF)
    for j in range(0, WIDTH, 512):
        at = slice(j, j + 512)
        total = mm_r(gate_cot_ref[:, :HALF], gate_ref[at, :])
        total += mm_r(gate_cot_ref[:, HALF:], gate_other_ref[at, :])
        total += mm_r(up_cot_ref[:, :HALF], up_ref[at, :])
        total += mm_r(up_cot_ref[:, HALF:], up_other_ref[at, :])
        back_ref[:, at] = total[:128].astype(BF)
        back_ref[:, WIDTH + j : WIDTH + j + 512] = total[128:].astype(BF)
    high = share.astype(BF).astype(F32)
    extra = jnp.zeros((128, 128), F32)
    for j, value in enumerate((high[:128], high[128:], (share - high)[:128], (share - high)[128:])):
        extra += jnp.where(lane == j, value, 0.0)
    back_ref[:, 2 * WIDTH :] = extra.astype(BF)


def expert_phase(rows, cot_rows, act_cot, own, pack, weights, after):
    tile = lambda w: pl.BlockSpec((256, w), lambda i: (i, 0))
    pair = lambda w, j=0: pl.BlockSpec((128, w), lambda i: (i, j))
    small = pl.BlockSpec((WIDTH, 128), lambda i: (0, 32))
    return call(
        expert_kernel,
        (8,),
        [pair(2 * WIDTH), pair(128, 24), tile(512), full((1, 128)), small]
        + [full(w.shape) for w in weights]
        + [ANY],
        [pair(WIDE), tile(512), tile(512), tile(512)],
        [out((PAIRS, WIDE), BF)] + [out((ROWS, 512), BF)] * 3,
    )(rows, cot_rows, act_cot, own, pack, *weights, after)


def expert_out_kernel(act_ref, down_ref, other_ref, _after_ref, out_ref):
    total = mm(act_ref[:, :HALF], down_ref[...]) + mm(act_ref[:, HALF:], other_ref[...])
    out_ref[:, :WIDTH] = total[:128].astype(BF)
    out_ref[:, WIDTH:] = total[128:].astype(BF)


def expert_outs(act, down, other, after):
    return call(
        expert_out_kernel,
        (8,),
        [
            pl.BlockSpec((256, 512), lambda i: (i, 0)),
            full((HALF, WIDTH)),
            full((HALF, WIDTH)),
            ANY,
        ],
        pl.BlockSpec((128, 2 * WIDTH), lambda i: (i, 0)),
        out((PAIRS, 2 * WIDTH), BF),
    )(act, down, other, after)


def expert_grad_kernel(
    rows_ref, cot_ref, act_ref, gate_cot_ref, up_cot_ref, _after_ref, gate_ref, up_ref, down_ref, gate, up, down
):
    step = pl.program_id(0)

    @pl.when(step == 0)
    def _():
        gate[...] = jnp.zeros_like(gate)
        up[...] = jnp.zeros_like(up)
        down[...] = jnp.zeros_like(down)

    rows = unpaired(rows_ref)
    gate[...] += mm_l(rows, gate_cot_ref[...])
    up[...] += mm_l(rows, up_cot_ref[...])
    down[...] += mm_l(act_ref[...], unpaired(cot_ref))

    @pl.when(step == 7)
    def _():
        gate_ref[...] = gate[...].astype(gate_ref.dtype)
        up_ref[...] = up[...].astype(up_ref.dtype)
        down_ref[...] = down[...].astype(down_ref.dtype)


def expert_grads(half, dtype, rows, cot_rows, act, gate_cot, up_cot, after):
    tile = lambda w, j=0: pl.BlockSpec((256, w), lambda i: (i, j))
    pair = pl.BlockSpec((128, 2 * WIDTH), lambda i: (i, 0))
    shapes = [(WIDTH, HALF), (WIDTH, HALF), (HALF, WIDTH)]
    return call(
        expert_grad_kernel,
        (8,),
        [pair, pair, tile(HALF, half), tile(HALF, half), tile(HALF, half), ANY],
        [full(s) for s in shapes],
        [out(s, dtype) for s in shapes],
        [pltpu.VMEM(s, F32) for s in shapes],
    )(rows, cot_rows, act, gate_cot, up_cot, after)


def unfold_into(down_ref, fold_ref, tail_ref):
    for j in range(2):
        at = slice(j * 512, (j + 1) * 512)
        rows = fold_ref[:, at].astype(F32).reshape(64, 24, 512)
        down_ref[:, at] = rows[:, :16].reshape(SHARED, 512).astype(BF)
        tail_ref[:, j * 8 : (j + 1) * 8] = rows[:, 16:]
    down_ref[:, 1024:] = tail_ref[...].reshape(SHARED, 512).astype(BF)


def shared_kernel(
    ffn_in_ref,
    out_grad_ref,
    second_ref,
    _after_ref,
    act_ref,
    pair_cot_ref,
    pair_w_ref,
    fold_ref,
    down_ref,
    tail_ref,
    sems,
):
    fold_copy = fetch(second_ref.at[:, 2 * SHARED :], fold_ref, sems.at[0])
    pair_copy = fetch(second_ref.at[:, : 2 * SHARED], pair_w_ref, sems.at[1])
    fold_copy.wait()
    unfold_into(down_ref, fold_ref, tail_ref)
    pair_copy.wait()
    for j in range(0, SHARED, 256):
        at = slice(j, j + 256)
        up_at = slice(SHARED + j, SHARED + j + 256)
        gate = mm(ffn_in_ref[...], pair_w_ref[:, at])
        upper = mm(ffn_in_ref[...], pair_w_ref[:, up_at])
        sig = 1.0 / (1.0 + jnp.exp(-gate))
        silu = gate * sig
        act_ref[:, at] = (silu * upper).astype(BF)
        cot = mm_r(out_grad_ref[...], down_ref[at, :])
        pair_cot_ref[:, at] = (cot * upper * (sig * (1.0 + gate * (1.0 - sig)))).astype(BF)
        pair_cot_ref[:, up_at] = (cot * silu).astype(BF)


def shared_scratch():
    return [
        pltpu.VMEM((WIDTH, 2 * SHARED), BF),
        pltpu.VMEM((WIDTH, 1024), BF),
        pltpu.VMEM((SHARED, WIDTH), BF),
        pltpu.VMEM((64, 16, 512), F32),
        pltpu.SemaphoreType.DMA((2,)),
    ]


def shared_phase(ffn_in, out_grad, second, after):
    wide = (TOKENS, WIDTH)
    shapes = [(TOKENS, SHARED), (TOKENS, 2 * SHARED)]
    return call(
        shared_kernel,
        (1,),
        [full(wide), full(wide), ANY, ANY],
        [full(s) for s in shapes],
        [out(s, BF) for s in shapes],
        shared_scratch(),
    )(ffn_in, out_grad, second, after)


def shared_end_kernel(
    act_ref,
    pair_cot_ref,
    middle_ref,
    second_ref,
    _after_ref,
    sum_ref,
    cot_ref,
    pair_w_ref,
    fold_ref,
    down_ref,
    tail_ref,
    sems,
):
    fold_copy = fetch(second_ref.at[:, 2 * SHARED :], fold_ref, sems.at[0])
    pair_copy = fetch(second_ref.at[:, : 2 * SHARED], pair_w_ref, sems.at[1])
    fold_copy.wait()
    unfold_into(down_ref, fold_ref, tail_ref)
    pair_copy.wait()
    for j in range(0, WIDTH, 512):
        at = slice(j, j + 512)
        sum_ref[:, at] = middle_ref[:, at] + mm(act_ref[...], down_ref[:, at])
        cot_ref[:, at] = mm_r(pair_cot_ref[...], pair_w_ref[at, :])


def shared_end(act, pair_cot, middle, second, after):
    wide = (TOKENS, WIDTH)
    return call(
        shared_end_kernel,
        (1,),
        [full(act.shape), full(pair_cot.shape), full(wide), ANY, ANY],
        [full(wide)] * 2,
        [out(wide, F32)] * 2,
        shared_scratch(),
    )(act, pair_cot, middle, second, after)


def shared_grad_kernel(ffn_in_ref, pair_ref, act_ref, cot_ref, _after_ref, out_ref):
    for j in range(0, 2 * SHARED, 512):
        at = slice(j, j + 512)
        out_ref[:, at] = mm_l(ffn_in_ref[...], pair_ref[:, at]).astype(BF)
    for j in range(0, 1024, 512):
        body = mm_l(act_ref[...], cot_ref[:, j : j + 512]).reshape(32, 16, 512)
        tail = mm_l(act_ref[...], cot_ref[:, 1024:]).reshape(32, 16, 512)
        tail = tail[:, :8] if j == 0 else tail[:, 8:]
        both = jnp.concatenate([body, tail], axis=1).reshape(768, 512)
        out_ref[:, 2 * SHARED + j : 2 * SHARED + j + 512] = both.astype(BF)


def shared_grads(ffn_in, pair_low, shared_low, out_grad, after):
    return call(
        shared_grad_kernel,
        (2,),
        [
            pl.BlockSpec((TOKENS, 768), lambda h: (0, h)),
            full((TOKENS, 2 * SHARED)),
            pl.BlockSpec((TOKENS, 512), lambda h: (0, h)),
            full((TOKENS, WIDTH)),
            ANY,
        ],
        pl.BlockSpec((768, 2 * SHARED + 1024), lambda h: (0, h)),
        out((768, 4 * SHARED + 2048), BF),
    )(ffn_in, pair_low, shared_low, out_grad, after)


def norm_back(values, scale, gain, cot):
    weighted = cot * gain
    centre = jnp.mean(weighted * values, axis=-1, keepdims=True)
    return scale * weighted - values * (scale * scale * scale * centre)


def backward_kernel(*refs):
    n_in, n_out = 13, 8
    sources, outs, scratch = refs[:n_in], refs[n_in : n_in + n_out], refs[n_in + n_out :]
    back_hbm, pack_hbm = sources[:2]
    middle_low_ref, dq_ref, dkv_ref, grad_in_ref, logit_ref, one_ref, two_ref, cot_ref = outs
    back_ref, wo_ref, wq_ref, wkv_ref, small_ref, acc, sems = scratch[:7]
    held = scratch[7:]
    loads = [(back_hbm.at[:512], back_ref.at[:512]), (back_hbm.at[512:], back_ref.at[512:])]
    loads += [(a, b) for a, b in zip(sources[2:7], held[:5])]
    loads += [
        (pack_hbm.at[:, 2 * WIDTH + 1024 : PACK], small_ref),
        (pack_hbm.at[:, WIDTH : 2 * WIDTH], wo_ref),
    ]
    loads += [(a, b) for a, b in zip(sources[7:12], held[5:])]
    loads += [
        (pack_hbm.at[:, :WIDTH], wq_ref),
        (pack_hbm.at[:, 2 * WIDTH : 2 * WIDTH + 1024], wkv_ref),
    ]
    turned_ref, shared_ref, gates_ref, middle_ref, gains_ref = held[:5]
    out_grad_ref, q_ref, kv_ref, probs_ref, hidden_ref = held[5:]
    loads = [loads[2], loads[0], loads[1]] + loads[3:]
    copies = [fetch(a, b, sems.at[i]) for i, (a, b) in enumerate(loads)]
    for i in (0, 1):
        copies[i].wait()
    lane = lax.broadcasted_iota(jnp.int32, (512, 128), 1)
    row = lax.broadcasted_iota(jnp.int32, (512, 128), 0)
    shares = jnp.zeros((TOKENS, 128), F32)
    for half in range(2):
        at = slice(half * 512, (half + 1) * 512)
        if half:
            copies[2].wait()
        total = mm(turned_ref[0, :, at], back_ref[at, :WIDTH])
        total += mm(turned_ref[1, :, at], back_ref[at, WIDTH : 2 * WIDTH])
        if half:
            acc[...] += total
        else:
            acc[...] = total
        extra = back_ref[at, 2 * WIDTH :].astype(F32)
        mine = lane == row // 16 + half * 32
        for j in range(2):
            for value in (extra[:, j : j + 1], extra[:, 2 + j : 3 + j]):
                shares += mm(turned_ref[j, :, at], jnp.where(mine, value, 0.0).astype(BF))
    for i in range(3, 10):
        copies[i].wait()
    logit = shares - gates_ref[...] * jnp.sum(shares, axis=-1, keepdims=True)
    logit_ref[...] = logit.astype(BF)
    cot = acc[...] + shared_ref[...] + mm_r(logit_ref[...], small_ref[...])
    middle = middle_ref[...]
    scale = root_scale(middle)
    two_ref[...] = (cot * middle * scale).astype(BF)
    total = out_grad_ref[...].astype(F32) + norm_back(middle, scale, gains_ref[1:2], cot)
    grad_in_ref[...] = total
    middle_low_ref[...] = total.astype(BF)
    for j in range(0, WIDTH, 512):
        at = slice(j, j + 512)
        cot_ref[:, at] = mm_r(middle_low_ref[...], wo_ref[at, :]).astype(BF)
    for i in range(10, 14):
        copies[i].wait()
    for kv_head in range(4):
        key_at = slice(kv_head * HEAD, (kv_head + 1) * HEAD)
        value_at = slice(512 + kv_head * HEAD, 512 + (kv_head + 1) * HEAD)
        key, value = kv_ref[:, key_at], kv_ref[:, value_at]
        dk = jnp.zeros((TOKENS, HEAD), F32)
        dv = jnp.zeros((TOKENS, HEAD), F32)
        for head in range(kv_head * GROUP, (kv_head + 1) * GROUP):
            at = slice(head * HEAD, (head + 1) * HEAD)
            probs = probs_ref[head]
            head_cot = cot_ref[:, at]
            dprobs = mm_r(head_cot, value)
            dv += mm_l(probs.astype(BF), head_cot)
            centre = jnp.sum(probs * dprobs, axis=-1, keepdims=True)
            dscores = (probs * (dprobs - centre)).astype(BF)
            dq_ref[:, at] = (mm(dscores, key) * SCALING).astype(BF)
            dk += mm_l(dscores, q_ref[:, at])
        dkv_ref[:, key_at] = (dk * SCALING).astype(BF)
        dkv_ref[:, value_at] = dv.astype(BF)
    for i in range(14, 16):
        copies[i].wait()
    for j in range(0, WIDTH, 512):
        at = slice(j, j + 512)
        acc[:, at] = mm_r(dq_ref[...], wq_ref[at, :]) + mm_r(dkv_ref[...], wkv_ref[at, :])
    tokens = hidden_ref[...].astype(F32)
    scale = root_scale(tokens)
    cot = acc[...]
    one_ref[...] = (cot * tokens * scale).astype(BF)
    grad_in_ref[...] += norm_back(tokens, scale, gains_ref[0:1], cot)


def backward(back, pack, turned, shared_cot, gates, middle, gains, out_grad, q, kv, probs, hidden, after):
    wide = (TOKENS, WIDTH)
    shapes = [
        (wide, BF),
        (wide, BF),
        ((TOKENS, 1024), BF),
        (wide, F32),
        ((TOKENS, 128), BF),
        (wide, BF),
        (wide, BF),
        (wide, BF),
    ]
    held = [turned, shared_cot, gates, middle, gains, out_grad, q, kv, probs, hidden]
    scratch = [
        pltpu.VMEM((PAIRS, WIDE), BF),
        pltpu.VMEM((WIDTH, WIDTH), BF),
        pltpu.VMEM((WIDTH, WIDTH), BF),
        pltpu.VMEM((WIDTH, 1024), BF),
        pltpu.VMEM((WIDTH, 128), BF),
        pltpu.VMEM((TOKENS, WIDTH), F32),
        pltpu.SemaphoreType.DMA((16,)),
    ] + [pltpu.VMEM(a.shape, a.dtype) for a in held]
    return call(
        backward_kernel,
        (1,),
        [ANY] * 13,
        [full(s) for s, _ in shapes],
        [out(s, d) for s, d in shapes],
        scratch,
    )(back, pack, *held, after)


def dense_grad_kernel(
    attn_in_ref,
    attended_ref,
    ffn_in_ref,
    gain_one_ref,
    gain_two_ref,
    dq_ref,
    middle_ref,
    dkv_ref,
    logit_ref,
    out_ref,
    held,
    sems,
):
    copies = []

    def send(at, width):
        where = slice(at, at + width)
        copies.append(fetch(held.at[:, where], out_ref.at[:, where], sems.at[len(copies)]))

    for half in range(2):
        rows = slice(half * 768, (half + 1) * 768)
        base = half * PACK
        attended = attended_ref[:, rows]
        for j in range(0, WIDTH, 512):
            at = base + WIDTH + j
            held[:, at : at + 512] = mm_l(attended, middle_ref[:, j : j + 512]).astype(BF)
        send(base + WIDTH, WIDTH)
        attn_in = attn_in_ref[:, rows]
        for j in range(0, WIDTH, 512):
            at = base + j
            held[:, at : at + 512] = mm_l(attn_in, dq_ref[:, j : j + 512]).astype(BF)
        send(base, WIDTH)
        for j in range(0, 1024, 512):
            at = base + 2 * WIDTH + j
            held[:, at : at + 512] = mm_l(attn_in, dkv_ref[:, j : j + 512]).astype(BF)
        lane = lax.broadcasted_iota(jnp.int32, (TOKENS, 128), 1)
        small = mm_l(ffn_in_ref[:, rows], logit_ref[...])
        small += mm_l(gain_one_ref[:, rows], jnp.where(lane == 64, 1.0, 0.0).astype(BF))
        small += mm_l(gain_two_ref[:, rows], jnp.where(lane == 65, 1.0, 0.0).astype(BF))
        held[:, base + 2 * WIDTH + 1024 : base + PACK] = small.astype(BF)
        send(base + 2 * WIDTH, 1024 + 128)
    for copy in copies:
        copy.wait()


def dense_grads(attn_in, attended, ffn_in, gain_one, gain_two, dq, middle_low, dkv, logit):
    ins = [attn_in, attended, ffn_in, gain_one, gain_two, dq, middle_low, dkv, logit]
    return call(
        dense_grad_kernel,
        (1,),
        [full(a.shape) for a in ins],
        ANY,
        out((768, 2 * PACK), BF),
        [pltpu.VMEM((768, 2 * PACK), BF), pltpu.SemaphoreType.DMA((6,))],
        flops=10**13,
    )(*ins)


def body(
    hidden_in,
    out_grad,
    doc_lengths,
    expert_ids,
    gain_attn,
    w_query,
    w_key,
    w_value,
    w_out,
    gain_ffn,
    w_router,
    w_shared_gate,
    w_shared_up,
    w_shared_down,
    expert_gate,
    expert_up,
    expert_down,
):
    parts = [w_query, w_out, w_key, w_value, w_router, gain_attn[:, None], gain_ffn[:, None]]
    parts += [jnp.zeros((12, 62), BF), w_shared_gate, w_shared_up, w_shared_down.reshape(12, 1024)]
    line = lax.all_gather(jnp.concatenate(parts, axis=1), ("zh", "zl"), axis=0, tiled=False)
    pack = gather_plane(line[:, :, :PACK].reshape(2, 24, PACK))
    pair_w = line[:, :, PACK : PACK + 2 * SHARED].reshape(2, 24, 2 * SHARED)
    down_w = fold_down(line[:, :, PACK + 2 * SHARED :].reshape(2, 16, WIDTH))
    second = gather_plane(jnp.concatenate([pair_w, down_w], axis=2))
    gate, up, down = expert_gate[0], expert_up[0], expert_down[0]
    gate_other, up_other, down_other = swap(gate, "zl"), swap(up, "zl"), swap(down, "zl")

    lanes = jnp.arange(128, dtype=jnp.int32)
    hits = jnp.any(expert_ids[:, :, None] == lanes, axis=1)
    hits_low = hits.astype(BF)
    place = jnp.arange(TOKENS, dtype=jnp.int32)
    earlier = (place[:, None] > place[None, :]).astype(BF)
    rank = jnp.where(hits, mm(earlier, hits_low), -1.0).T[:EXPERTS]
    own = (lanes == lax.axis_index(DP)).astype(F32)[None]

    deal, turned, send_cot = deal_out(rank, out_grad, hits_low)
    cot_rows = to_experts(tie(send_cot, line))

    attn_in, q, kv, probs, attended, middle, ffn_in, gates, gains, send_rows = forward(
        hidden_in, doc_lengths, hits_low, pack, deal
    )
    send_rows = tie(send_rows, gate_other, up_other, down_other)
    rows = to_experts(send_rows)

    act_cot = act_cots(cot_rows, down, down_other, send_rows)
    shared_low, pair_low = shared_phase(ffn_in, out_grad, second, act_cot)

    weights = (gate, gate_other, up, up_other)
    back, act, gate_cot, up_cot = expert_phase(
        rows, cot_rows, act_cot, own, pack, weights, pair_low
    )
    shared_grad = shared_grads(ffn_in, pair_low, shared_low, out_grad, act)
    shared_sum, shared_cot = shared_end(shared_low, pair_low, middle, second, shared_grad)
    kept = expert_grads(0, F32, rows, cot_rows, act, gate_cot, up_cot, shared_cot)
    shared_grad = scatter_plane(shared_grad)
    sent = expert_grads(1, BF, rows, cot_rows, act, gate_cot, up_cot, kept[0])
    result = expert_outs(act, down, down_other, sent[0])
    back = to_experts(back)

    middle_low, dq, dkv, grad_in, logit, one_rows, two_rows, _ = backward(
        back, pack, turned, shared_cot, gates, middle, gains, out_grad, q, kv, probs, hidden_in, result
    )
    result = to_experts(result)
    dense_grad = dense_grads(
        attn_in, attended, ffn_in, one_rows, two_rows, dq, middle_low, dkv, logit
    )
    dense = sum_line(scatter_plane(dense_grad), lambda x: (x[:12], x[12:]))

    def cut_shared(x):
        down = unfold_down(x[None, :, 2 * SHARED :])[0]
        return [
            jnp.concatenate([x[12 * i : 12 * i + 12, : 2 * SHARED], down[8 * i : 8 * i + 8].reshape(12, 1024)], axis=1)
            for i in range(2)
        ]

    shared_grad = sum_line(shared_grad, cut_shared)
    pair_grad = shared_grad[:, : 2 * SHARED]
    down_grad = shared_grad[:, 2 * SHARED :].reshape(8, WIDTH)
    block_out = add_results(turned, result, shared_sum)
    sent = [tie(x, dense_grad) for x in sent]
    expert = [(k + swap(s, "zl").astype(F32))[None] for k, s in zip(kept, sent)]
    at = 2 * WIDTH
    return (
        block_out,
        grad_in,
        dense[:, at + 1088],
        dense[:, :WIDTH],
        dense[:, at : at + 512],
        dense[:, at + 512 : at + 1024],
        dense[:, WIDTH:at],
        dense[:, at + 1089],
        dense[:, at + 1024 : at + 1088],
        pair_grad[:, :SHARED],
        pair_grad[:, SHARED:],
        down_grad,
        expert[0],
        expert[1],
        expert[2],
    )


def solution(mesh):
    fine = Mesh(mesh.devices.reshape(2, 4, 4, 2, 2), AXES)
    rows, vector = P(AXES, None), P(AXES)
    banks = (P(DP, None, "zl"), P(DP, None, "zl"), P(DP, "zl", None))
    return jax.shard_map(
        body,
        mesh=fine,
        in_specs=(rows, rows, rows, rows, vector, rows, rows, rows, rows, vector)
        + (rows, rows, rows, rows)
        + banks,
        out_specs=(rows, rows, vector, rows, rows, rows, rows, vector)
        + (rows, rows, rows, rows)
        + banks,
        check_vma=False,
    )
```

```python
import jax
import jax.numpy as jnp
from jax import lax
from jax.experimental import pallas as pl
from jax.experimental.pallas import tpu as pltpu
from jax.sharding import Mesh, PartitionSpec as P

GROUP = 3
HEAD = 128
EXPERTS = 64
SLOTS = 32
TOKENS = 256
WIDTH = 1536
SHARED = 1024
HALF = 256
ROWS = EXPERTS * SLOTS
PAIRS = ROWS // 2
WIDE = 2 * WIDTH + 128
PACK = 2 * WIDTH + 1024 + 128

EPSILON = 1e-06
NEGATIVE = -1e30
SCALING = HEAD ** (-0.5)
BF = jnp.bfloat16
F32 = jnp.float32

AXES = ("zh", "x", "y", "c", "zl")
DP = ("zh", "x", "y", "c")
PLANE = ("x", "y", "c")
ANY = pl.BlockSpec(memory_space=pl.ANY)


def mm(a, b):
    return jnp.dot(a, b, preferred_element_type=F32)


def mm_l(a, b):
    return lax.dot_general(a, b, (((0,), (0,)), ((), ())), preferred_element_type=F32)


def mm_r(a, b):
    return lax.dot_general(a, b, (((1,), (1,)), ((), ())), preferred_element_type=F32)


def swap(x, axis):
    return lax.ppermute(x, axis, [(0, 1), (1, 0)])


def out(shape, dtype):
    return jax.ShapeDtypeStruct(shape, dtype)


def full(shape):
    return pl.BlockSpec(shape, lambda *i: (0,) * len(shape))


def call(kernel, grid, in_specs, out_specs, out_shape, scratch=(), flops=0, aliases=None):
    return pl.pallas_call(
        kernel,
        grid=grid,
        in_specs=in_specs,
        out_specs=out_specs,
        out_shape=out_shape,
        scratch_shapes=list(scratch),
        input_output_aliases=aliases or {},
        compiler_params=pltpu.CompilerParams(vmem_limit_bytes=56 * 1024 * 1024),
        cost_estimate=pl.CostEstimate(flops=flops, bytes_accessed=0, transcendentals=0),
    )


def fetch(source, target, sem):
    copy = pltpu.make_async_copy(source, target, sem)
    copy.start()
    return copy


def tie_kernel(*refs):
    pass


def tie(x, *after):
    return pl.pallas_call(
        tie_kernel,
        in_specs=[ANY] * (1 + len(after)),
        out_specs=ANY,
        out_shape=out(x.shape, x.dtype),
        input_output_aliases={0: 0},
    )(x, *after)


def gather_plane(pairs):
    _, rows, width = pairs.shape
    return lax.all_gather(pairs, PLANE, axis=1, tiled=True).reshape(64 * rows, width)


def scatter_plane(grads):
    return lax.psum_scatter(grads, PLANE, scatter_dimension=0, tiled=True)


def sum_line(plane, cut):
    width = plane.shape[1] // 2
    zh = lax.axis_index("zh")
    zl = lax.axis_index("zl")
    low, high = plane[:, :width], plane[:, width:]
    near, far = jnp.where(zh == 0, low, high), jnp.where(zh == 0, high, low)
    ours, theirs = cut(near)
    total = jnp.where(zl == 0, ours, theirs).astype(F32)
    total += swap(jnp.where(zl == 0, theirs, ours), "zl").astype(F32)
    ours, theirs = cut(far)
    total += swap(jnp.where(zl == 0, ours, theirs), "zh").astype(F32)
    across = [(i, 3 - i) for i in range(4)]
    give = jnp.where(zl == 0, theirs, ours)
    return total + lax.ppermute(give, ("zh", "zl"), across).astype(F32)


def fold_down(rows):
    tail = [rows[:, :8, 1024:], rows[:, 8:, 1024:]]
    return jnp.concatenate([rows[:, :, :1024], jnp.concatenate(tail, axis=2)], axis=1)


def unfold_down(rows):
    tail = jnp.concatenate([rows[:, 16:, :512], rows[:, 16:, 512:]], axis=1)
    return jnp.concatenate([rows[:, :16], tail], axis=2)


def deal_kernel(rank_ref, cot_ref, hits_ref, deal_ref, turned_ref, out_ref):
    rank = rank_ref[...]
    slot = lax.broadcasted_iota(jnp.int32, (8, SLOTS, TOKENS), 1).astype(F32)
    hit = jnp.where(rank[:, None, :] == slot, 1.0, 0.0)
    lane = lax.broadcasted_iota(jnp.int32, (128, 128), 1)
    marks = jnp.zeros((128, 128), F32)
    for j in range(2):
        side = hit[:, j * 16 : (j + 1) * 16].reshape(128, TOKENS)
        deal = side.astype(BF)
        deal_ref[j] = deal
        turned_ref[j] = jnp.transpose(side).astype(BF)
        out_ref[:, j * WIDTH : (j + 1) * WIDTH] = mm(deal, cot_ref[...]).astype(BF)
        mark = mm(deal, hits_ref[...])
        marks += mark if j == 0 else pltpu.roll(mark, 64, 1)
    out_ref[:, 2 * WIDTH :] = marks.astype(BF)


def deal_out(rank, out_grad, hits):
    return call(
        deal_kernel,
        (8,),
        [
            pl.BlockSpec((8, TOKENS), lambda i: (i, 0)),
            full((TOKENS, WIDTH)),
            full((TOKENS, 128)),
        ],
        [
            pl.BlockSpec((2, 128, TOKENS), lambda i: (0, i, 0)),
            pl.BlockSpec((2, TOKENS, 128), lambda i: (0, 0, i)),
            pl.BlockSpec((128, WIDE), lambda i: (i, 0)),
        ],
        [out((2, PAIRS, TOKENS), BF), out((2, TOKENS, PAIRS), BF), out((PAIRS, WIDE), BF)],
    )(rank, out_grad, hits)


def to_experts(rows):
    return lax.all_to_all(
        rows.reshape(EXPERTS, SLOTS // 2, -1), DP, split_axis=0, concat_axis=0, tiled=True
    ).reshape(PAIRS, -1)


def result_kernel(turned_ref, rows_ref, base_ref, out_ref, acc):
    step = pl.program_id(0)

    @pl.when(step == 0)
    def _():
        acc[...] = base_ref[...]

    acc[...] += mm(turned_ref[0], rows_ref[...])

    @pl.when(step == 3)
    def _():
        out_ref[...] = acc[...].astype(BF)


def add_results(turned, rows, base):
    return call(
        result_kernel,
        (4,),
        [
            pl.BlockSpec((1, TOKENS, 512), lambda i: (i // 2, 0, i % 2)),
            pl.BlockSpec((512, WIDTH), lambda i: (i % 2, i // 2)),
            full((TOKENS, WIDTH)),
        ],
        full((TOKENS, WIDTH)),
        out((TOKENS, WIDTH), BF),
        [pltpu.VMEM((TOKENS, WIDTH), F32)],
        flops=10**13,
    )(turned, rows, base)


def root_scale(values):
    return lax.rsqrt(jnp.mean(values * values, axis=-1, keepdims=True) + EPSILON)


def forward_kernel(hidden_ref, docs_ref, hits_ref, pack_ref, deal_hbm, *refs):
    outs, (small_ref, wq_ref, wkv_ref, wo_ref, deal_ref), held = refs[:10], refs[10:15], refs[15:25]
    sems = refs[25]
    (
        attn_in_ref,
        q_ref,
        kv_ref,
        probs_ref,
        attended_ref,
        middle_ref,
        ffn_in_ref,
        gates_ref,
        gains_ref,
        send_ref,
    ) = held
    copies = [
        fetch(pack_ref.at[:, at : at + ref.shape[1]], ref, sems.at[i])
        for i, (at, ref) in enumerate(
            [(2 * WIDTH + 1024, small_ref), (0, wq_ref), (2 * WIDTH, wkv_ref), (WIDTH, wo_ref)]
        )
    ]
    copies.append(fetch(deal_hbm, deal_ref, sems.at[4]))
    sent = []

    def send(i):
        sent.append(fetch(held[i], outs[i], sems.at[5 + i]))

    copies[0].wait()
    gains = jnp.transpose(small_ref[...].astype(F32))
    gains_ref[...] = gains[64:72]
    gain_one, gain_two = gains[64:65], gains[65:66]
    tokens = hidden_ref[...].astype(F32)
    attn_in_ref[...] = (tokens * root_scale(tokens) * gain_one).astype(BF)
    send(8)
    send(0)
    copies[1].wait()
    for j in range(0, WIDTH, 512):
        q_ref[:, j : j + 512] = mm(attn_in_ref[...], wq_ref[:, j : j + 512]).astype(BF)
    send(1)
    copies[2].wait()
    for j in range(0, 1024, 512):
        kv_ref[:, j : j + 512] = mm(attn_in_ref[...], wkv_ref[:, j : j + 512]).astype(BF)
    send(2)
    first = docs_ref[0, 0]
    second = first + docs_ref[0, 1]
    third = second + docs_ref[0, 2]
    row = lax.broadcasted_iota(jnp.int32, (TOKENS, TOKENS), 0)
    col = lax.broadcasted_iota(jnp.int32, (TOKENS, TOKENS), 1)

    def segment(place):
        return (
            (place >= first).astype(jnp.int32)
            + (place >= second).astype(jnp.int32)
            + (place >= third).astype(jnp.int32)
        )

    visible = (segment(row) == segment(col)) & (row >= col)
    for kv_head in range(4):
        key = kv_ref[:, kv_head * HEAD : (kv_head + 1) * HEAD]
        value = kv_ref[:, 512 + kv_head * HEAD : 512 + (kv_head + 1) * HEAD]
        for head in range(kv_head * GROUP, (kv_head + 1) * GROUP):
            at = slice(head * HEAD, (head + 1) * HEAD)
            scores = jnp.where(visible, mm_r(q_ref[:, at], key) * SCALING, NEGATIVE)
            exponent = jnp.exp(scores - jnp.max(scores, axis=-1, keepdims=True))
            probs = exponent / jnp.sum(exponent, axis=-1, keepdims=True)
            probs_ref[head] = probs
            attended_ref[:, at] = mm(probs.astype(BF), value).astype(BF)
    send(3)
    send(4)
    copies[3].wait()
    for j in range(0, WIDTH, 512):
        at = slice(j, j + 512)
        middle_ref[:, at] = hidden_ref[:, at].astype(F32) + mm(
            attended_ref[...], wo_ref[:, at]
        )
    middle = middle_ref[...]
    send(5)
    ffn_in_ref[...] = (middle * root_scale(middle) * gain_two).astype(BF)
    send(6)
    copies[4].wait()
    for j in range(4):
        at = slice(j * 768, (j + 1) * 768)
        from_at = slice(j % 2 * 768, (j % 2 + 1) * 768)
        send_ref[:, at] = mm(deal_ref[j // 2], ffn_in_ref[:, from_at]).astype(BF)
        sent.append(fetch(send_ref.at[:, at], outs[9].at[:, at], sems.at[14 + j]))
    logits = mm(ffn_in_ref[...], small_ref[...])
    hits = hits_ref[...] > 0
    top = jnp.max(jnp.where(hits, logits, NEGATIVE), axis=-1, keepdims=True)
    weight = jnp.where(hits, jnp.exp(jnp.where(hits, logits - top, 0.0)), 0.0)
    gates_ref[...] = weight / jnp.sum(weight, axis=-1, keepdims=True)
    send(7)
    for copy in sent:
        copy.wait()


def forward(hidden, docs, hits, pack, deal):
    wide = (TOKENS, WIDTH)
    shapes = [
        (wide, BF),
        (wide, BF),
        ((TOKENS, 1024), BF),
        ((12, TOKENS, TOKENS), F32),
        (wide, BF),
        (wide, F32),
        (wide, BF),
        ((TOKENS, 128), F32),
        ((8, WIDTH), F32),
        ((PAIRS, 2 * WIDTH), BF),
    ]
    return call(
        forward_kernel,
        (1,),
        [full(wide), pl.BlockSpec(memory_space=pltpu.SMEM), full((TOKENS, 128)), ANY, ANY],
        [ANY] * 10,
        [out(s, d) for s, d in shapes],
        [pltpu.VMEM((WIDTH, w), BF) for w in (128, WIDTH, 1024, WIDTH)]
        + [pltpu.VMEM(deal.shape, BF)]
        + [pltpu.VMEM(s, d) for s, d in shapes]
        + [pltpu.SemaphoreType.DMA((18,))],
    )(hidden, docs, hits, pack, deal)


def unpaired(ref):
    return jnp.concatenate([ref[:, :WIDTH], ref[:, WIDTH : 2 * WIDTH]], axis=0)


def act_cot_kernel(cot_ref, down_ref, other_ref, _after_ref, out_ref):
    cot = unpaired(cot_ref)
    out_ref[:, :HALF] = mm_r(cot, down_ref[...])
    out_ref[:, HALF:] = mm_r(cot, other_ref[...])


def act_cots(cot_rows, down, other, after):
    return call(
        act_cot_kernel,
        (8,),
        [
            pl.BlockSpec((128, 2 * WIDTH), lambda i: (i, 0)),
            full((HALF, WIDTH)),
            full((HALF, WIDTH)),
            ANY,
        ],
        pl.BlockSpec((256, 2 * HALF), lambda i: (i, 0)),
        out((ROWS, 2 * HALF), F32),
    )(cot_rows, down, other, after)


def expert_kernel(
    rows_ref,
    marks_ref,
    act_cot_ref,
    own_ref,
    small_ref,
    gate_ref,
    gate_other_ref,
    up_ref,
    up_other_ref,
    _after_ref,
    back_ref,
    act_ref,
    gate_cot_ref,
    up_cot_ref,
):
    rows = unpaired(rows_ref)
    lane = lax.broadcasted_iota(jnp.int32, (1, 128), 1)
    marks = marks_ref[...].astype(F32)
    marks = jnp.concatenate([marks, pltpu.roll(marks, 64, 1)], axis=0)
    marks = (marks > 0) & (lane < 64)
    logits = mm(rows, small_ref[...])
    top = jnp.max(jnp.where(marks, logits, NEGATIVE), axis=-1, keepdims=True)
    weight = jnp.where(marks, jnp.exp(jnp.where(marks, logits - top, 0.0)), 0.0)
    own = own_ref[...]
    total = jnp.sum(weight, axis=-1, keepdims=True)
    mine = jnp.sum(weight * own, axis=-1, keepdims=True)
    route_gate = mine / jnp.where(total > 0, total, 1.0)
    share = jnp.zeros((256, 1), F32)
    for half, gate_w, up_w in ((0, gate_ref, up_ref), (1, gate_other_ref, up_other_ref)):
        at = slice(half * HALF, (half + 1) * HALF)
        gate = mm(rows, gate_w[...])
        upper = mm(rows, up_w[...])
        sig = 1.0 / (1.0 + jnp.exp(-gate))
        silu = gate * sig
        act_cot = act_cot_ref[:, at]
        act = route_gate * silu * upper
        act_ref[:, at] = act.astype(BF)
        share += jnp.sum(act_cot * act, axis=-1, keepdims=True)
        scaled = route_gate * act_cot
        gate_cot_ref[:, at] = (scaled * upper * (sig * (1.0 + gate * (1.0 - sig)))).astype(BF)
        up_cot_ref[:, at] = (scaled * silu).astype(BF)
    for j in range(0, WIDTH, 512):
        at = slice(j, j + 512)
        total = mm_r(gate_cot_ref[:, :HALF], gate_ref[at, :])
        total += mm_r(gate_cot_ref[:, HALF:], gate_other_ref[at, :])
        total += mm_r(up_cot_ref[:, :HALF], up_ref[at, :])
        total += mm_r(up_cot_ref[:, HALF:], up_other_ref[at, :])
        back_ref[:, at] = total[:128].astype(BF)
        back_ref[:, WIDTH + j : WIDTH + j + 512] = total[128:].astype(BF)
    high = share.astype(BF).astype(F32)
    extra = jnp.zeros((128, 128), F32)
    for j, value in enumerate((high[:128], high[128:], (share - high)[:128], (share - high)[128:])):
        extra += jnp.where(lane == j, value, 0.0)
    back_ref[:, 2 * WIDTH :] = extra.astype(BF)


def expert_phase(rows, cot_rows, act_cot, own, pack, weights, after):
    tile = lambda w: pl.BlockSpec((256, w), lambda i: (i, 0))
    pair = lambda w, j=0: pl.BlockSpec((128, w), lambda i: (i, j))
    small = pl.BlockSpec((WIDTH, 128), lambda i: (0, 32))
    return call(
        expert_kernel,
        (8,),
        [pair(2 * WIDTH), pair(128, 24), tile(512), full((1, 128)), small]
        + [full(w.shape) for w in weights]
        + [ANY],
        [pair(WIDE), tile(512), tile(512), tile(512)],
        [out((PAIRS, WIDE), BF)] + [out((ROWS, 512), BF)] * 3,
    )(rows, cot_rows, act_cot, own, pack, *weights, after)


def expert_out_kernel(act_ref, down_ref, other_ref, _after_ref, out_ref):
    total = mm(act_ref[:, :HALF], down_ref[...]) + mm(act_ref[:, HALF:], other_ref[...])
    out_ref[:, :WIDTH] = total[:128].astype(BF)
    out_ref[:, WIDTH:] = total[128:].astype(BF)


def expert_outs(act, down, other, after):
    return call(
        expert_out_kernel,
        (8,),
        [
            pl.BlockSpec((256, 512), lambda i: (i, 0)),
            full((HALF, WIDTH)),
            full((HALF, WIDTH)),
            ANY,
        ],
        pl.BlockSpec((128, 2 * WIDTH), lambda i: (i, 0)),
        out((PAIRS, 2 * WIDTH), BF),
    )(act, down, other, after)


def expert_grad_kernel(
    rows_ref, cot_ref, act_ref, gate_cot_ref, up_cot_ref, _after_ref, gate_ref, up_ref, down_ref, gate, up, down
):
    step = pl.program_id(0)

    @pl.when(step == 0)
    def _():
        gate[...] = jnp.zeros_like(gate)
        up[...] = jnp.zeros_like(up)
        down[...] = jnp.zeros_like(down)

    rows = unpaired(rows_ref)
    gate[...] += mm_l(rows, gate_cot_ref[...])
    up[...] += mm_l(rows, up_cot_ref[...])
    down[...] += mm_l(act_ref[...], unpaired(cot_ref))

    @pl.when(step == 7)
    def _():
        gate_ref[...] = gate[...].astype(gate_ref.dtype)
        up_ref[...] = up[...].astype(up_ref.dtype)
        down_ref[...] = down[...].astype(down_ref.dtype)


def expert_grads(half, dtype, rows, cot_rows, act, gate_cot, up_cot, after):
    tile = lambda w, j=0: pl.BlockSpec((256, w), lambda i: (i, j))
    pair = pl.BlockSpec((128, 2 * WIDTH), lambda i: (i, 0))
    shapes = [(WIDTH, HALF), (WIDTH, HALF), (HALF, WIDTH)]
    return call(
        expert_grad_kernel,
        (8,),
        [pair, pair, tile(HALF, half), tile(HALF, half), tile(HALF, half), ANY],
        [full(s) for s in shapes],
        [out(s, dtype) for s in shapes],
        [pltpu.VMEM(s, F32) for s in shapes],
    )(rows, cot_rows, act, gate_cot, up_cot, after)


def unfold_into(down_ref, fold_ref, tail_ref):
    for j in range(2):
        at = slice(j * 512, (j + 1) * 512)
        rows = fold_ref[:, at].astype(F32).reshape(64, 24, 512)
        down_ref[:, at] = rows[:, :16].reshape(SHARED, 512).astype(BF)
        tail_ref[:, j * 8 : (j + 1) * 8] = rows[:, 16:]
    down_ref[:, 1024:] = tail_ref[...].reshape(SHARED, 512).astype(BF)


def shared_kernel(
    ffn_in_ref,
    out_grad_ref,
    second_ref,
    _after_ref,
    act_ref,
    pair_cot_ref,
    pair_w_ref,
    fold_ref,
    down_ref,
    tail_ref,
    sems,
):
    fold_copy = fetch(second_ref.at[:, 2 * SHARED :], fold_ref, sems.at[0])
    pair_copy = fetch(second_ref.at[:, : 2 * SHARED], pair_w_ref, sems.at[1])
    fold_copy.wait()
    unfold_into(down_ref, fold_ref, tail_ref)
    pair_copy.wait()
    for j in range(0, SHARED, 256):
        at = slice(j, j + 256)
        up_at = slice(SHARED + j, SHARED + j + 256)
        gate = mm(ffn_in_ref[...], pair_w_ref[:, at])
        upper = mm(ffn_in_ref[...], pair_w_ref[:, up_at])
        sig = 1.0 / (1.0 + jnp.exp(-gate))
        silu = gate * sig
        act_ref[:, at] = (silu * upper).astype(BF)
        cot = mm_r(out_grad_ref[...], down_ref[at, :])
        pair_cot_ref[:, at] = (cot * upper * (sig * (1.0 + gate * (1.0 - sig)))).astype(BF)
        pair_cot_ref[:, up_at] = (cot * silu).astype(BF)


def shared_scratch():
    return [
        pltpu.VMEM((WIDTH, 2 * SHARED), BF),
        pltpu.VMEM((WIDTH, 1024), BF),
        pltpu.VMEM((SHARED, WIDTH), BF),
        pltpu.VMEM((64, 16, 512), F32),
        pltpu.SemaphoreType.DMA((2,)),
    ]


def shared_phase(ffn_in, out_grad, second, after):
    wide = (TOKENS, WIDTH)
    shapes = [(TOKENS, SHARED), (TOKENS, 2 * SHARED)]
    return call(
        shared_kernel,
        (1,),
        [full(wide), full(wide), ANY, ANY],
        [full(s) for s in shapes],
        [out(s, BF) for s in shapes],
        shared_scratch(),
    )(ffn_in, out_grad, second, after)


def shared_end_kernel(
    act_ref,
    pair_cot_ref,
    middle_ref,
    second_ref,
    _after_ref,
    sum_ref,
    cot_ref,
    pair_w_ref,
    fold_ref,
    down_ref,
    tail_ref,
    sems,
):
    fold_copy = fetch(second_ref.at[:, 2 * SHARED :], fold_ref, sems.at[0])
    pair_copy = fetch(second_ref.at[:, : 2 * SHARED], pair_w_ref, sems.at[1])
    fold_copy.wait()
    unfold_into(down_ref, fold_ref, tail_ref)
    pair_copy.wait()
    for j in range(0, WIDTH, 512):
        at = slice(j, j + 512)
        sum_ref[:, at] = middle_ref[:, at] + mm(act_ref[...], down_ref[:, at])
        cot_ref[:, at] = mm_r(pair_cot_ref[...], pair_w_ref[at, :])


def shared_end(act, pair_cot, middle, second, after):
    wide = (TOKENS, WIDTH)
    return call(
        shared_end_kernel,
        (1,),
        [full(act.shape), full(pair_cot.shape), full(wide), ANY, ANY],
        [full(wide)] * 2,
        [out(wide, F32)] * 2,
        shared_scratch(),
    )(act, pair_cot, middle, second, after)


def shared_grad_kernel(ffn_in_ref, pair_ref, act_ref, cot_ref, _after_ref, out_ref):
    for j in range(0, 2 * SHARED, 512):
        at = slice(j, j + 512)
        out_ref[:, at] = mm_l(ffn_in_ref[...], pair_ref[:, at]).astype(BF)
    for j in range(0, 1024, 512):
        body = mm_l(act_ref[...], cot_ref[:, j : j + 512]).reshape(32, 16, 512)
        tail = mm_l(act_ref[...], cot_ref[:, 1024:]).reshape(32, 16, 512)
        tail = tail[:, :8] if j == 0 else tail[:, 8:]
        both = jnp.concatenate([body, tail], axis=1).reshape(768, 512)
        out_ref[:, 2 * SHARED + j : 2 * SHARED + j + 512] = both.astype(BF)


def shared_grads(ffn_in, pair_low, shared_low, out_grad, after):
    return call(
        shared_grad_kernel,
        (2,),
        [
            pl.BlockSpec((TOKENS, 768), lambda h: (0, h)),
            full((TOKENS, 2 * SHARED)),
            pl.BlockSpec((TOKENS, 512), lambda h: (0, h)),
            full((TOKENS, WIDTH)),
            ANY,
        ],
        pl.BlockSpec((768, 2 * SHARED + 1024), lambda h: (0, h)),
        out((768, 4 * SHARED + 2048), BF),
    )(ffn_in, pair_low, shared_low, out_grad, after)


def norm_back(values, scale, gain, cot):
    weighted = cot * gain
    centre = jnp.mean(weighted * values, axis=-1, keepdims=True)
    return scale * weighted - values * (scale * scale * scale * centre)


def backward_kernel(*refs):
    n_in, n_out = 13, 7
    sources, outs, scratch = refs[:n_in], refs[n_in : n_in + n_out], refs[n_in + n_out :]
    back_hbm, pack_hbm = sources[:2]
    results, scratch = scratch[:8], scratch[8:]
    middle_low_ref, dq_ref, dkv_ref, grad_in_ref, logit_ref, one_ref, two_ref, cot_ref = results
    back_ref, wo_ref, wq_ref, wkv_ref, small_ref, acc, sems = scratch[:7]
    held = scratch[7:]
    loads = [(back_hbm.at[:512], back_ref.at[:512]), (back_hbm.at[512:], back_ref.at[512:])]
    loads += [(a, b) for a, b in zip(sources[2:7], held[:5])]
    loads += [
        (pack_hbm.at[:, 2 * WIDTH + 1024 : PACK], small_ref),
        (pack_hbm.at[:, WIDTH : 2 * WIDTH], wo_ref),
    ]
    loads += [(a, b) for a, b in zip(sources[7:12], held[5:])]
    loads += [
        (pack_hbm.at[:, :WIDTH], wq_ref),
        (pack_hbm.at[:, 2 * WIDTH : 2 * WIDTH + 1024], wkv_ref),
    ]
    turned_ref, shared_ref, gates_ref, middle_ref, gains_ref = held[:5]
    out_grad_ref, q_ref, kv_ref, probs_ref, hidden_ref = held[5:]
    loads = [loads[2], loads[0], loads[1]] + loads[3:]
    copies = [fetch(a, b, sems.at[i]) for i, (a, b) in enumerate(loads)]
    sent = []

    def send(*which):
        for i in which:
            sent.append(fetch(results[i], outs[i], sems.at[16 + i]))

    for i in (0, 1):
        copies[i].wait()
    lane = lax.broadcasted_iota(jnp.int32, (512, 128), 1)
    row = lax.broadcasted_iota(jnp.int32, (512, 128), 0)
    shares = jnp.zeros((TOKENS, 128), F32)
    for half in range(2):
        at = slice(half * 512, (half + 1) * 512)
        if half:
            copies[2].wait()
        total = mm(turned_ref[0, :, at], back_ref[at, :WIDTH])
        total += mm(turned_ref[1, :, at], back_ref[at, WIDTH : 2 * WIDTH])
        if half:
            acc[...] += total
        else:
            acc[...] = total
        extra = back_ref[at, 2 * WIDTH :].astype(F32)
        mine = lane == row // 16 + half * 32
        for j in range(2):
            for value in (extra[:, j : j + 1], extra[:, 2 + j : 3 + j]):
                shares += mm(turned_ref[j, :, at], jnp.where(mine, value, 0.0).astype(BF))
    for i in range(3, 10):
        copies[i].wait()
    logit = shares - gates_ref[...] * jnp.sum(shares, axis=-1, keepdims=True)
    logit_ref[...] = logit.astype(BF)
    cot = acc[...] + shared_ref[...] + mm_r(logit_ref[...], small_ref[...])
    middle = middle_ref[...]
    scale = root_scale(middle)
    two_ref[...] = (cot * middle * scale).astype(BF)
    total = out_grad_ref[...].astype(F32) + norm_back(middle, scale, gains_ref[1:2], cot)
    grad_in_ref[...] = total
    middle_low_ref[...] = total.astype(BF)
    send(0, 4, 6)
    for j in range(0, WIDTH, 512):
        at = slice(j, j + 512)
        cot_ref[:, at] = mm_r(middle_low_ref[...], wo_ref[at, :]).astype(BF)
    for i in range(10, 14):
        copies[i].wait()
    for kv_head in range(4):
        key_at = slice(kv_head * HEAD, (kv_head + 1) * HEAD)
        value_at = slice(512 + kv_head * HEAD, 512 + (kv_head + 1) * HEAD)
        key, value = kv_ref[:, key_at], kv_ref[:, value_at]
        dk = jnp.zeros((TOKENS, HEAD), F32)
        dv = jnp.zeros((TOKENS, HEAD), F32)
        for head in range(kv_head * GROUP, (kv_head + 1) * GROUP):
            at = slice(head * HEAD, (head + 1) * HEAD)
            probs = probs_ref[head]
            head_cot = cot_ref[:, at]
            dprobs = mm_r(head_cot, value)
            dv += mm_l(probs.astype(BF), head_cot)
            centre = jnp.sum(probs * dprobs, axis=-1, keepdims=True)
            dscores = (probs * (dprobs - centre)).astype(BF)
            dq_ref[:, at] = (mm(dscores, key) * SCALING).astype(BF)
            dk += mm_l(dscores, q_ref[:, at])
        dkv_ref[:, key_at] = (dk * SCALING).astype(BF)
        dkv_ref[:, value_at] = dv.astype(BF)
    send(1, 2)
    for i in range(14, 16):
        copies[i].wait()
    for j in range(0, WIDTH, 512):
        at = slice(j, j + 512)
        acc[:, at] = mm_r(dq_ref[...], wq_ref[at, :]) + mm_r(dkv_ref[...], wkv_ref[at, :])
    tokens = hidden_ref[...].astype(F32)
    scale = root_scale(tokens)
    cot = acc[...]
    one_ref[...] = (cot * tokens * scale).astype(BF)
    send(5)
    grad_in_ref[...] += norm_back(tokens, scale, gains_ref[0:1], cot)
    send(3)
    for copy in sent:
        copy.wait()


def backward(back, pack, turned, shared_cot, gates, middle, gains, out_grad, q, kv, probs, hidden, after):
    wide = (TOKENS, WIDTH)
    shapes = [
        (wide, BF),
        (wide, BF),
        ((TOKENS, 1024), BF),
        (wide, F32),
        ((TOKENS, 128), BF),
        (wide, BF),
        (wide, BF),
        (wide, BF),
    ]
    held = [turned, shared_cot, gates, middle, gains, out_grad, q, kv, probs, hidden]
    scratch = [
        pltpu.VMEM((PAIRS, WIDE), BF),
        pltpu.VMEM((WIDTH, WIDTH), BF),
        pltpu.VMEM((WIDTH, WIDTH), BF),
        pltpu.VMEM((WIDTH, 1024), BF),
        pltpu.VMEM((WIDTH, 128), BF),
        pltpu.VMEM((TOKENS, WIDTH), F32),
        pltpu.SemaphoreType.DMA((23,)),
    ] + [pltpu.VMEM(a.shape, a.dtype) for a in held]
    scratch = [pltpu.VMEM(s, d) for s, d in shapes] + scratch
    return call(
        backward_kernel,
        (1,),
        [ANY] * 13,
        [ANY] * 7,
        [out(s, d) for s, d in shapes[:7]],
        scratch,
    )(back, pack, *held, after)


def dense_grad_kernel(*refs):
    out_ref, held, sems = refs[9], refs[10], refs[20]
    (
        attn_in_ref,
        attended_ref,
        ffn_in_ref,
        gain_one_ref,
        gain_two_ref,
        dq_ref,
        middle_ref,
        dkv_ref,
        logit_ref,
    ) = refs[11:20]
    loads = {i: fetch(refs[i], refs[11 + i], sems.at[6 + i]) for i in (1, 6, 0, 5, 7, 2, 8, 3, 4)}

    def need(*which):
        for i in which:
            if i in loads:
                loads.pop(i).wait()

    copies = []

    def send(at, width):
        where = slice(at, at + width)
        copies.append(fetch(held.at[:, where], out_ref.at[:, where], sems.at[len(copies)]))

    for half in range(2):
        rows = slice(half * 768, (half + 1) * 768)
        base = half * PACK
        need(1, 6)
        attended = attended_ref[:, rows]
        for j in range(0, WIDTH, 512):
            at = base + WIDTH + j
            held[:, at : at + 512] = mm_l(attended, middle_ref[:, j : j + 512]).astype(BF)
        send(base + WIDTH, WIDTH)
        need(0, 5)
        attn_in = attn_in_ref[:, rows]
        for j in range(0, WIDTH, 512):
            at = base + j
            held[:, at : at + 512] = mm_l(attn_in, dq_ref[:, j : j + 512]).astype(BF)
        send(base, WIDTH)
        need(7)
        for j in range(0, 1024, 512):
            at = base + 2 * WIDTH + j
            held[:, at : at + 512] = mm_l(attn_in, dkv_ref[:, j : j + 512]).astype(BF)
        lane = lax.broadcasted_iota(jnp.int32, (TOKENS, 128), 1)
        need(2, 8, 3, 4)
        small = mm_l(ffn_in_ref[:, rows], logit_ref[...])
        small += mm_l(gain_one_ref[:, rows], jnp.where(lane == 64, 1.0, 0.0).astype(BF))
        small += mm_l(gain_two_ref[:, rows], jnp.where(lane == 65, 1.0, 0.0).astype(BF))
        held[:, base + 2 * WIDTH + 1024 : base + PACK] = small.astype(BF)
        send(base + 2 * WIDTH, 1024 + 128)
    for copy in copies:
        copy.wait()


def dense_grads(attn_in, attended, ffn_in, gain_one, gain_two, dq, middle_low, dkv, logit):
    ins = [attn_in, attended, ffn_in, gain_one, gain_two, dq, middle_low, dkv, logit]
    return call(
        dense_grad_kernel,
        (1,),
        [ANY] * 9,
        ANY,
        out((768, 2 * PACK), BF),
        [pltpu.VMEM((768, 2 * PACK), BF)]
        + [pltpu.VMEM(a.shape, a.dtype) for a in ins]
        + [pltpu.SemaphoreType.DMA((15,))],
        flops=10**13,
    )(*ins)


def body(
    hidden_in,
    out_grad,
    doc_lengths,
    expert_ids,
    gain_attn,
    w_query,
    w_key,
    w_value,
    w_out,
    gain_ffn,
    w_router,
    w_shared_gate,
    w_shared_up,
    w_shared_down,
    expert_gate,
    expert_up,
    expert_down,
):
    parts = [w_query, w_out, w_key, w_value, w_router, gain_attn[:, None], gain_ffn[:, None]]
    parts += [jnp.zeros((12, 62), BF), w_shared_gate, w_shared_up, w_shared_down.reshape(12, 1024)]
    line = lax.all_gather(jnp.concatenate(parts, axis=1), ("zh", "zl"), axis=0, tiled=False)
    pack = gather_plane(line[:, :, :PACK].reshape(2, 24, PACK))
    pair_w = line[:, :, PACK : PACK + 2 * SHARED].reshape(2, 24, 2 * SHARED)
    down_w = fold_down(line[:, :, PACK + 2 * SHARED :].reshape(2, 16, WIDTH))
    second = gather_plane(jnp.concatenate([pair_w, down_w], axis=2))
    gate, up, down = expert_gate[0], expert_up[0], expert_down[0]
    gate_other, up_other, down_other = swap(gate, "zl"), swap(up, "zl"), swap(down, "zl")

    lanes = jnp.arange(128, dtype=jnp.int32)
    hits = jnp.any(expert_ids[:, :, None] == lanes, axis=1)
    hits_low = hits.astype(BF)
    place = jnp.arange(TOKENS, dtype=jnp.int32)
    earlier = (place[:, None] > place[None, :]).astype(BF)
    rank = jnp.where(hits, mm(earlier, hits_low), -1.0).T[:EXPERTS]
    own = (lanes == lax.axis_index(DP)).astype(F32)[None]

    deal, turned, send_cot = deal_out(rank, out_grad, hits_low)
    cot_rows = to_experts(tie(send_cot, line))

    attn_in, q, kv, probs, attended, middle, ffn_in, gates, gains, send_rows = forward(
        hidden_in, doc_lengths, hits_low, pack, deal
    )
    send_rows = tie(send_rows, gate_other, up_other, down_other)
    rows = to_experts(send_rows)

    act_cot = act_cots(cot_rows, down, down_other, send_rows)
    shared_low, pair_low = shared_phase(ffn_in, out_grad, second, act_cot)

    weights = (gate, gate_other, up, up_other)
    back, act, gate_cot, up_cot = expert_phase(
        rows, cot_rows, act_cot, own, pack, weights, pair_low
    )
    shared_grad = shared_grads(ffn_in, pair_low, shared_low, out_grad, act)
    shared_sum, shared_cot = shared_end(shared_low, pair_low, middle, second, shared_grad)
    kept = expert_grads(0, F32, rows, cot_rows, act, gate_cot, up_cot, shared_cot)
    shared_grad = scatter_plane(shared_grad)
    sent = expert_grads(1, BF, rows, cot_rows, act, gate_cot, up_cot, kept[0])
    result = expert_outs(act, down, down_other, sent[0])
    back = to_experts(back)

    middle_low, dq, dkv, grad_in, logit, one_rows, two_rows = backward(
        back, pack, turned, shared_cot, gates, middle, gains, out_grad, q, kv, probs, hidden_in, result
    )
    result = to_experts(result)
    dense_grad = dense_grads(
        attn_in, attended, ffn_in, one_rows, two_rows, dq, middle_low, dkv, logit
    )
    dense = sum_line(scatter_plane(dense_grad), lambda x: (x[:12], x[12:]))

    def cut_shared(x):
        down = unfold_down(x[None, :, 2 * SHARED :])[0]
        return [
            jnp.concatenate([x[12 * i : 12 * i + 12, : 2 * SHARED], down[8 * i : 8 * i + 8].reshape(12, 1024)], axis=1)
            for i in range(2)
        ]

    shared_grad = sum_line(shared_grad, cut_shared)
    pair_grad = shared_grad[:, : 2 * SHARED]
    down_grad = shared_grad[:, 2 * SHARED :].reshape(8, WIDTH)
    block_out = add_results(turned, result, shared_sum)
    sent = [tie(x, dense_grad) for x in sent]
    expert = [(k + swap(s, "zl").astype(F32))[None] for k, s in zip(kept, sent)]
    at = 2 * WIDTH
    return (
        block_out,
        grad_in,
        dense[:, at + 1088],
        dense[:, :WIDTH],
        dense[:, at : at + 512],
        dense[:, at + 512 : at + 1024],
        dense[:, WIDTH:at],
        dense[:, at + 1089],
        dense[:, at + 1024 : at + 1088],
        pair_grad[:, :SHARED],
        pair_grad[:, SHARED:],
        down_grad,
        expert[0],
        expert[1],
        expert[2],
    )


def solution(mesh):
    fine = Mesh(mesh.devices.reshape(2, 4, 4, 2, 2), AXES)
    rows, vector = P(AXES, None), P(AXES)
    banks = (P(DP, None, "zl"), P(DP, None, "zl"), P(DP, "zl", None))
    return jax.shard_map(
        body,
        mesh=fine,
        in_specs=(rows, rows, rows, rows, vector, rows, rows, rows, rows, vector)
        + (rows, rows, rows, rows)
        + banks,
        out_specs=(rows, rows, vector, rows, rows, rows, rows, vector)
        + (rows, rows, rows, rows)
        + banks,
        check_vma=False,
    )
```
